128 devices in a mesh: view: 4 (over y_hi, core), row: 32 (over x, z, y_lo).
Axes of the slice: x: 4, y: 4 (y_hi: 2, y_lo: 2; y = y_hi * 2 + y_lo), z: 4, core: 2. Of those that a mesh axis runs over, the one named last changes fastest.
Arguments:
- tokens: bfloat16 [32, 4, 128, 1024], P('row', 'view'), may hold values from -6 to 6
- patches: bfloat16 [32, 4, 256, 768], P('row', 'view'), may hold values from -6 to 6
- patch_counts: int32 [8, 4], replicated, may hold values from 256 to 1024, as said below
- camera_ids: int32 [8], replicated, may hold values from 0 to 15
- modulation: float32 [16, 6144], replicated, may hold values from -1.5 to 1.5
- query_weight: bfloat16 [1024, 1024], replicated, may hold values from -0.1875 to 0.1875
- key_weight: bfloat16 [1024, 1024], replicated, may hold values from -0.1875 to 0.1875
- value_weight: bfloat16 [1024, 1024], replicated, may hold values from -0.1875 to 0.1875
- output_weight: bfloat16 [1024, 1024], replicated, may hold values from -0.75 to 0.75
- cross_query: bfloat16 [1024, 1024], replicated, may hold values from -0.1875 to 0.1875
- cross_key: bfloat16 [768, 1024], replicated, may hold values from -0.21875 to 0.21875
- cross_value: bfloat16 [768, 1024], replicated, may hold values from -0.21875 to 0.21875
- cross_output: bfloat16 [1024, 1024], replicated, may hold values from -0.5 to 0.5
- expand_weight: bfloat16 [1024, 4096], replicated, may hold values from -0.1875 to 0.1875
- reduce_weight: bfloat16 [4096, 1024], replicated, may hold values from -0.09375 to 0.09375
- cotangent: bfloat16 [32, 4, 128, 1024], P('row', 'view'), may hold values from -6 to 6
Outputs:
- layer_out: float32 [32, 4, 128, 1024], P('row', 'view')
- tokens_grad: float32 [32, 4, 128, 1024], P('row', 'view')
- patches_grad: float32 [32, 4, 256, 768], P('row', 'view')
- modulation_grad: float32 [16, 6144], P('view', 'row')
- query_grad: float32 [1024, 1024], P('view', 'row')
- key_grad: float32 [1024, 1024], P('view', 'row')
- value_grad: float32 [1024, 1024], P('view', 'row')
- output_grad: float32 [1024, 1024], P('view', 'row')
- cross_query_grad: float32 [1024, 1024], P('view', 'row')
- cross_key_grad: float32 [768, 1024], P('view', 'row')
- cross_value_grad: float32 [768, 1024], P('view', 'row')
- cross_output_grad: float32 [1024, 1024], P('view', 'row')
- expand_grad: float32 [1024, 4096], P('view', 'row')
- reduce_grad: float32 [4096, 1024], P('view', 'row')
The draws below stay inside these ranges and needn't reach their ends.
Inputs may be any that keep to these rules, and one draw needn't show every extreme that they name: `patch_counts`: each entry is 256 or 1024; every item has a view of each kind.
All inputs are finite; a program needn't handle non-finite values.
Results may differ from the reference program's by a relative error of at most 0.02.
Values may be sent and summed in bfloat16 or wider, within the bound.
No kernel may reach another device: no remote copies, remote signals or barrier semaphores. Data moves between devices by JAX's collectives and lax.ppermute only.
A program may use at most 320 MiB of HBM per device.

```python
import jax
import jax.numpy as jnp
from jax import lax

D = 1024
HEADS = 16
FF = 4096
DI = 768
TOK_DEV = 128
PATCHES = 1024
GROUP = 4
CAMS = 16
TRI = 2048
ITEMS = 8
ROW_BLOCKS = 32
PSH = 256
N_VIEW = 4


def draw_patch_counts(key, part):
    key = jax.random.fold_in(key, 11)
    first_key, second_key, third_key = jax.random.split(key, 3)
    full_view = jax.random.randint(first_key, (ITEMS, 1), 0, N_VIEW)
    offset = jax.random.randint(second_key, (ITEMS, 1), 1, N_VIEW)
    short_view = (full_view + offset) % N_VIEW
    coin_flips = jax.random.randint(third_key, (ITEMS, N_VIEW), 0, 2)
    view_ids = jnp.arange(N_VIEW)[None, :]
    chosen = jnp.where(view_ids == full_view, 1, jnp.where(view_ids == short_view, 0, coin_flips))
    return jnp.where(chosen == 1, PATCHES, PATCHES // 4).astype(jnp.int32)


def plant(values, stream_key, least, largest):
    place = [jax.random.randint(jax.random.fold_in(stream_key, axis), (), 0, length) for axis, length in enumerate(values.shape)]
    longest = values.shape.index(max(values.shape))
    next_to = place[:longest] + [(place[longest] + 1) % values.shape[longest]] + place[longest + 1:]
    return values.at[tuple(place)].set(least).at[tuple(next_to)].set(largest)


def level_of(key, shape, cuts, low, high):
    loudness = 1.0
    for position, shards_of in cuts:
        steps = jax.random.uniform(jax.random.fold_in(jax.random.fold_in(key, 6), position), (shards_of,), jnp.float32, low / len(cuts), high / len(cuts))
        loudness = loudness * jnp.repeat(jnp.exp(steps), shape[position] // shards_of).reshape((-1,) + (1,) * (len(shape) - 1 - position))
    return loudness


def scatter_about(stream_key, extent, width, limit, shards=(), kind=jnp.bfloat16):
    values = jax.random.normal(stream_key, extent, jnp.float32) * width
    if len(shards) > 0:
        values = level_of(stream_key, extent, shards, -0.22, 0.18) * values
    return jnp.clip(values, min=-limit, max=limit).astype(kind)


def setup_inputs(seed: int = 0) -> dict:
    key_of = jax.random.split(jax.random.key(seed), 17)
    tokens = scatter_about(key_of[0], (ROW_BLOCKS, N_VIEW, TOK_DEV, D), 1.0, 6.0, ((0, 32), (1, 4)))
    patches = scatter_about(key_of[1], (ROW_BLOCKS, N_VIEW, PSH, DI), 1.0, 6.0, ((0, 32), (1, 4)))
    patch_counts = draw_patch_counts(jax.random.fold_in(key_of[16], 71), 0)
    camera_ids = plant(jax.random.randint(key_of[3], (ITEMS,), 0, CAMS), jax.random.fold_in(key_of[3], 1), 0, CAMS - 1).astype(jnp.int32)
    modulation = scatter_about(key_of[4], (CAMS, 6 * D), 0.3, 1.5, (), jnp.float32)
    query_weight = scatter_about(key_of[5], (D, D), D ** -0.5, 0.1875)
    key_weight = scatter_about(key_of[6], (D, D), D ** -0.5, 0.1875)
    value_weight = scatter_about(key_of[7], (D, D), D ** -0.5, 0.1875)
    output_weight = scatter_about(key_of[8], (D, D), (D // 16) ** -0.5, 0.75)
    cross_query = scatter_about(key_of[9], (D, D), D ** -0.5, 0.1875)
    cross_key = scatter_about(key_of[10], (DI, D), DI ** -0.5, 0.21875)
    cross_value = scatter_about(key_of[11], (DI, D), DI ** -0.5, 0.21875)
    cross_output = scatter_about(key_of[12], (D, D), (D // 8) ** -0.5, 0.5)
    expand_weight = scatter_about(key_of[13], (D, FF), D ** -0.5, 0.1875)
    reduce_weight = scatter_about(key_of[14], (FF, D), FF ** -0.5, 0.09375)
    cotangent = scatter_about(key_of[15], (ROW_BLOCKS, N_VIEW, TOK_DEV, D), 1.0, 6.0, ((0, 32), (1, 4)))
    return dict(tokens=tokens, patches=patches, patch_counts=patch_counts, camera_ids=camera_ids, modulation=modulation, query_weight=query_weight, key_weight=key_weight, value_weight=value_weight, output_weight=output_weight, cross_query=cross_query, cross_key=cross_key, cross_value=cross_value, cross_output=cross_output, expand_weight=expand_weight, reduce_weight=reduce_weight, cotangent=cotangent)


highest = lax.Precision.HIGHEST

@jax.custom_vjp
def low(v):
    return lax.optimization_barrier(v.astype(jnp.bfloat16)).astype(jnp.float32)

@jax.custom_vjp
def low_back(v):
    return v

def low_keep(v):
    return (low(v), None)

def low_pass(kept, grad):
    return (grad,)

def back_keep(v):
    return (v, None)

def back_low(kept, grad):
    return (low(grad),)
low.defvjp(low_keep, low_pass)
low_back.defvjp(back_keep, back_low)

def low_both(value_in):
    return low_back(low(value_in))

def product(left, right):
    return jnp.dot(left, right, precision=highest)

def modulated(values_in, gain, shift):
    centred = values_in - lax.optimization_barrier(jnp.mean(values_in, -1, keepdims=True))
    spread = lax.optimization_barrier(jnp.mean(centred * centred, -1, keepdims=True))
    return centred * lax.rsqrt(spread + 1e-05) * (1.0 + gain) + shift

def item_layer(inputs, modulation, weights):
    token_rows, patch_rows, counts, ident = inputs
    query_weight, key_weight, value_weight, output_weight, cross_query, cross_key, cross_value, cross_output, expand_weight, reduce_weight = weights
    head_size = D // HEADS
    scale = head_size ** (-0.5)
    gains = modulation[ident].reshape(6, D)
    block_rows = TRI // GROUP
    attn_in = low(modulated(token_rows, gains[0], gains[1]))
    queries = low_both(product(attn_in, query_weight)).reshape(GROUP, block_rows, HEADS, head_size)
    keys = low_both(product(attn_in, key_weight)).reshape(TRI, HEADS, head_size)
    values = low_both(product(attn_in, value_weight)).reshape(TRI, HEADS, head_size)

    def self_block(query_block):
        raw = low_back(jnp.einsum('qhd,khd->hqk', query_block, keys, precision=highest))
        probs = jax.nn.softmax(raw * scale, -1)
        return jnp.einsum('hqk,khd->qhd', low(probs), values, precision=highest)
    self_out = lax.map(jax.checkpoint(self_block), queries).reshape(TRI, D)
    first_sum = token_rows + low_back(product(low_both(self_out), output_weight))
    cross_in = low(modulated(first_sum, gains[2], gains[3]))
    cross_queries = low_both(product(cross_in, cross_query)).reshape(GROUP, block_rows, HEADS, head_size)
    cross_keys = low_both(jnp.einsum('vpc,cd->vpd', patch_rows, cross_key, precision=highest)).reshape(N_VIEW, PATCHES, HEADS, head_size)
    cross_values = low_both(jnp.einsum('vpc,cd->vpd', patch_rows, cross_value, precision=highest)).reshape(N_VIEW, PATCHES, HEADS, head_size)
    valid = jnp.arange(PATCHES, dtype=jnp.int32)[None, :] < counts[:, None]

    def cross_block(query_block):
        raw = low_back(jnp.einsum('qhd,vkhd->vhqk', query_block, cross_keys, precision=highest))
        scores = jnp.where(valid[:, None, None, :], raw * scale, -1e+30)
        peak = lax.optimization_barrier(jnp.max(scores, -1, keepdims=True))
        powered = jnp.exp(scores - peak)
        row_total = lax.optimization_barrier(jnp.sum(powered, -1))
        numer = jnp.einsum('vhqk,vkhd->vqhd', low(powered), cross_values, precision=highest)
        peak = peak[..., 0]
        best = lax.optimization_barrier(jnp.max(peak, 0))
        weight = jnp.exp(peak - best)
        merged_total = lax.optimization_barrier(jnp.sum(weight * row_total, 0))
        merged = lax.optimization_barrier(jnp.sum(numer * jnp.transpose(weight, (0, 2, 1))[..., None], 0))
        return merged / merged_total.T[:, :, None]
    cross_out = lax.map(jax.checkpoint(cross_block), cross_queries).reshape(TRI, D)
    second_sum = first_sum + low_back(product(low_both(cross_out), cross_output))
    mlp_in = low(modulated(second_sum, gains[4], gains[5]))
    expanded = low_back(product(mlp_in, expand_weight))
    hidden = low_both(jax.nn.gelu(expanded, approximate=True))
    return second_sum + low_back(product(hidden, reduce_weight))

def reference(tokens, patches, patch_counts, camera_ids, modulation, query_weight, key_weight, value_weight, output_weight, cross_query, cross_key, cross_value, cross_output, expand_weight, reduce_weight, cotangent):
    token_items = tokens.astype(jnp.float32).reshape(ITEMS, TRI, D)
    patch_items = patches.astype(jnp.float32).reshape(ITEMS, GROUP, N_VIEW, PSH, DI)
    patch_items = jnp.transpose(patch_items, (0, 2, 1, 3, 4)).reshape(ITEMS, N_VIEW, PATCHES, DI)
    weights = tuple((matrix.astype(jnp.float32) for matrix in (query_weight, key_weight, value_weight, output_weight, cross_query, cross_key, cross_value, cross_output, expand_weight, reduce_weight)))

    def forward(token_part, patch_part, table, weight_set):

        def per_item(inputs):
            return item_layer(inputs, table, weight_set)
        return lax.map(jax.checkpoint(per_item), (token_part, patch_part, patch_counts, camera_ids))
    layer, pullback = jax.vjp(forward, token_items, patch_items, modulation, weights)
    token_grad, patch_grad, table_grad, weight_grads = pullback(cotangent.astype(jnp.float32).reshape(ITEMS, TRI, D))
    patch_grad = patch_grad.reshape(ITEMS, N_VIEW, GROUP, PSH, DI)
    patch_grad = jnp.transpose(patch_grad, (0, 2, 1, 3, 4)).reshape(ROW_BLOCKS, N_VIEW, PSH, DI)
    return (layer.reshape(ROW_BLOCKS, N_VIEW, TOK_DEV, D), token_grad.reshape(ROW_BLOCKS, N_VIEW, TOK_DEV, D), patch_grad, table_grad, weight_grads[0], weight_grads[1], weight_grads[2], weight_grads[3], weight_grads[4], weight_grads[5], weight_grads[6], weight_grads[7], weight_grads[8], weight_grads[9])
```

```python
from functools import partial
from itertools import product as every

import jax
import jax.numpy as jnp
from jax import lax
from jax.experimental import pallas as pl
from jax.experimental.pallas import tpu as pltpu
from jax.sharding import Mesh
from jax.sharding import PartitionSpec as P

HEADS = 16
HEAD = 64
TOK = 128
SLOTS = 256
BLOCKS = 16
LIVE_MAX = 13
EPS = 1e-05
LOG2E = 1.4426950408889634
FAR = -1e30

AXES = ("yh", "c", "x", "zh", "zl", "yl")
SIZES = (2, 2, 4, 2, 2, 2)
VIEW = ("yh", "c")
ROW = ("x", "zh", "zl", "yl")
ITEM = ("yh", "c", "zl", "yl")
ITEMS = ("x", "zh")
VMEM_BYTES = 56 * 1024 * 1024

bf16 = jnp.bfloat16
f32 = jnp.float32


def mm(left, right, lc=1, rc=0):
    return lax.dot_general(left, right, (((lc,), (rc,)), ((), ())), preferred_element_type=f32)


def swap(block, axes):
    return lax.all_to_all(block, axes, 0, 0, tiled=True)


def three_parts(row):
    high = row.astype(bf16)
    rest = row - high.astype(f32)
    middle = rest.astype(bf16)
    low = (rest - middle.astype(f32)).astype(bf16)
    return high, middle, low


def softmax_block(q, kt, v, o_ref, keep_ref, at, scale):
    s = mm(q, kt)
    m = jnp.max(s, 1, keepdims=True)
    p = jnp.exp2((s - m) * (scale * LOG2E))
    total = jnp.sum(p, 1, keepdims=True)
    o = mm(p.astype(bf16), v)[:, :HEAD] / total
    lse = m + jnp.log2(total) * (1.0 / (scale * LOG2E))
    packed = jnp.concatenate([o, jnp.broadcast_to(lse, o.shape)], 1).T
    for part in range(packed.shape[1] // TOK):
        piece = packed[:, part * TOK : (part + 1) * TOK]
        o_ref[at + part] = piece[:HEAD].astype(bf16)
        keep_ref[at + part] = piece[: HEAD + 8]


def backward_block(qts, dots, keeps, kt, k, vt, dk_acc, dv_acc, scale):
    q_rows, do_rows = [], []
    for qt, dot, keep in zip(qts, dots, keeps):
        lse = keep[HEAD : HEAD + 1]
        delta = jnp.sum(dot.astype(f32) * keep[:HEAD], 0, keepdims=True) * scale
        one = jnp.ones_like(lse)
        zero = jnp.zeros((HEAD - 4, TOK), f32)
        parts = [part.astype(f32) for part in three_parts(-lse)]
        q_rows.append(jnp.concatenate([qt.astype(f32), one] + parts + [zero], 0))
        parts = [part.astype(f32) for part in three_parts(-delta)]
        do_rows.append(jnp.concatenate([dot.astype(f32) * scale] + parts + [0.0 * one, zero], 0))
    q = jnp.concatenate([rows.T for rows in q_rows], 0).astype(bf16)
    do = jnp.concatenate([rows.T for rows in do_rows], 0).astype(bf16)
    p = jnp.exp2(mm(q, kt) * (scale * LOG2E))
    ds = (p * mm(do, vt)).astype(bf16)
    dq = mm(ds, k)
    dk_acc[...] += mm(jnp.concatenate(qts, 1), ds)
    dv_acc[...] += mm(jnp.concatenate(dots, 1), p.astype(bf16))
    return dq[:, :HEAD]


def store_blocks(ref, at, rows, value):
    turned = value.T
    for part in range(turned.shape[1] // TOK):
        ref[at + part, rows, :] = turned[:, part * TOK : (part + 1) * TOK].astype(ref.dtype)


def self_forward_kernel(qkv_ref, o_ref, keep_ref, kt, v, *, scale, step):
    for j in range(BLOCKS):
        cols = slice(j * TOK, (j + 1) * TOK)
        kt[:, cols] = qkv_ref[j, HEAD : 2 * HEAD, :]
        v[cols, :] = qkv_ref[j, 2 * HEAD :, :].T

    def one(i, carry):
        at = i * step
        q = jnp.concatenate([qkv_ref[at + n, :HEAD, :].T for n in range(step)], 0)
        softmax_block(q, kt[...], v[...], o_ref, keep_ref, at, scale)
        return carry

    lax.fori_loop(0, BLOCKS // step, one, 0)


def self_backward_kernel(qkv_ref, do_ref, keep_ref, out_ref, kt, k, vt, dk_acc, dv_acc, *, scale, step):
    ones = jnp.ones((HEAD, BLOCKS * TOK), bf16)
    row = lax.broadcasted_iota(jnp.int32, ones.shape, 0)
    kt[HEAD:, :] = jnp.where((row >= 1) & (row < 4), ones, 0)
    vt[HEAD:, :] = jnp.where(row < 3, ones, 0)
    for j in range(BLOCKS):
        cols = slice(j * TOK, (j + 1) * TOK)
        kt[:HEAD, cols] = qkv_ref[j, HEAD : 2 * HEAD, :]
        k[cols, :] = qkv_ref[j, HEAD : 2 * HEAD, :].T
        vt[:HEAD, cols] = qkv_ref[j, 2 * HEAD :, :]
    dk_acc[...] = jnp.zeros_like(dk_acc)
    dv_acc[...] = jnp.zeros_like(dv_acc)

    def one(i, carry):
        at = i * step
        qts = [qkv_ref[at + n, :HEAD, :] for n in range(step)]
        dots = [do_ref[at + n] for n in range(step)]
        keeps = [keep_ref[at + n] for n in range(step)]
        dq = backward_block(qts, dots, keeps, kt[...], k[...], vt[...], dk_acc, dv_acc, scale)
        store_blocks(out_ref, at, slice(0, HEAD), dq)
        return carry

    lax.fori_loop(0, BLOCKS // step, one, 0)
    for j in range(BLOCKS):
        cols = slice(j * TOK, (j + 1) * TOK)
        out_ref[j, HEAD : 2 * HEAD, :] = dk_acc[:, cols].astype(bf16)
        out_ref[j, 2 * HEAD :, :] = dv_acc[:, cols].astype(bf16)


def slot_block(kv_ref, index):
    return kv_ref[:, pl.ds(pl.multiple_of(index * SLOTS, SLOTS), SLOTS)]


def cross_forward_kernel(order_ref, live_ref, q_ref, kv_ref, o_ref, keep_ref, kt, v, *, scale, step):
    kt[HEAD:, :] = jnp.zeros((HEAD, LIVE_MAX * SLOTS), bf16)
    for t in range(LIVE_MAX):
        cols = slice(t * SLOTS, (t + 1) * SLOTS)
        block = slot_block(kv_ref, order_ref[t])
        kt[:HEAD, cols] = block[:HEAD]
        bias = jnp.where(t < live_ref[0], 0.0, FAR)
        row = lax.broadcasted_iota(jnp.int32, (16, SLOTS), 0)
        kt[HEAD : HEAD + 16, cols] = jnp.where(row == 0, bias, 0.0).astype(bf16)
        v[cols, :] = block[HEAD:].T
    one_row = jnp.where(lax.broadcasted_iota(jnp.int32, (HEAD, TOK), 0) == 0, 1.0, 0.0)

    def one(i, carry):
        at = i * step
        q = jnp.concatenate(
            [jnp.concatenate([q_ref[at + n].astype(f32), one_row], 0).T for n in range(step)], 0
        ).astype(bf16)
        softmax_block(q, kt[...], v[...], o_ref, keep_ref, at, scale)
        return carry

    lax.fori_loop(0, BLOCKS // step, one, 0)


def cross_backward_kernel(
    order_ref, live_ref, q_ref, do_ref, keep_ref, kv_ref, dq_ref, dkv_ref, kt, k, vt, dk_acc, dv_acc, *, scale, step
):
    shape = (HEAD, LIVE_MAX * SLOTS)
    row = lax.broadcasted_iota(jnp.int32, shape, 0)
    kt[HEAD:, :] = jnp.where((row >= 1) & (row < 4), 1.0, 0.0).astype(bf16)
    vt[HEAD:, :] = jnp.where(row < 3, 1.0, 0.0).astype(bf16)
    for t in range(LIVE_MAX):
        cols = slice(t * SLOTS, (t + 1) * SLOTS)
        block = slot_block(kv_ref, order_ref[t])
        kt[:HEAD, cols] = block[:HEAD]
        bias = jnp.where(t < live_ref[0], 0.0, FAR)
        row = lax.broadcasted_iota(jnp.int32, (16, SLOTS), 0)
        ones = jnp.where((row >= 1) & (row < 4), 1.0, 0.0)
        kt[HEAD : HEAD + 16, cols] = jnp.where(row == 0, bias, ones).astype(bf16)
        k[cols, :] = block[:HEAD].T
        vt[:HEAD, cols] = block[HEAD:]
    dk_acc[...] = jnp.zeros_like(dk_acc)
    dv_acc[...] = jnp.zeros_like(dv_acc)

    def one(i, carry):
        at = i * step
        qts = [q_ref[at + n] for n in range(step)]
        dots = [do_ref[at + n] for n in range(step)]
        keeps = [keep_ref[at + n] for n in range(step)]
        dq = backward_block(qts, dots, keeps, kt[...], k[...], vt[...], dk_acc, dv_acc, scale)
        store_blocks(dq_ref, at, slice(0, HEAD), dq)
        return carry

    lax.fori_loop(0, BLOCKS // step, one, 0)
    for t in range(LIVE_MAX):
        cols = slice(t * SLOTS, (t + 1) * SLOTS)
        dkv_ref[order_ref[t], :HEAD, :] = dk_acc[:, cols].astype(bf16)
        dkv_ref[order_ref[t], HEAD:, :] = dv_acc[:, cols].astype(bf16)
    for t in range(LIVE_MAX, BLOCKS):
        dkv_ref[order_ref[t]] = jnp.zeros((2 * HEAD, SLOTS), bf16)


def params():
    return pltpu.CompilerParams(vmem_limit_bytes=VMEM_BYTES)


def vmem(count):
    return [pl.BlockSpec(memory_space=pltpu.VMEM)] * count


def smem(count):
    return [pl.BlockSpec(memory_space=pltpu.SMEM)] * count


def cost(keys, products):
    flops = 2 * BLOCKS * TOK * keys * HEAD * products
    return pl.CostEstimate(flops=4 * flops, bytes_accessed=4 << 20, transcendentals=BLOCKS * TOK * keys)


OUT_T = jax.ShapeDtypeStruct((BLOCKS, HEAD, TOK), bf16)
KEEP_T = jax.ShapeDtypeStruct((BLOCKS, HEAD + 8, TOK), f32)


def self_forward(qkv, scale):
    keys = BLOCKS * TOK
    return pl.pallas_call(
        partial(self_forward_kernel, scale=scale, step=2),
        out_shape=(OUT_T, KEEP_T),
        in_specs=vmem(1),
        out_specs=tuple(vmem(2)),
        scratch_shapes=[pltpu.VMEM((HEAD, keys), bf16), pltpu.VMEM((keys, HEAD), bf16)],
        compiler_params=params(),
        cost_estimate=cost(keys, 2),
        name="self_forward",
    )(qkv)


def self_backward(qkv, do, keep, scale):
    keys = BLOCKS * TOK
    return pl.pallas_call(
        partial(self_backward_kernel, scale=scale, step=2),
        out_shape=jax.ShapeDtypeStruct((BLOCKS, 3 * HEAD, TOK), bf16),
        in_specs=vmem(3),
        out_specs=vmem(1)[0],
        scratch_shapes=[
            pltpu.VMEM((2 * HEAD, keys), bf16),
            pltpu.VMEM((keys, HEAD), bf16),
            pltpu.VMEM((2 * HEAD, keys), bf16),
            pltpu.VMEM((HEAD, keys), f32),
            pltpu.VMEM((HEAD, keys), f32),
        ],
        compiler_params=params(),
        cost_estimate=cost(keys, 5),
        name="self_backward",
    )(qkv, do, keep)


def cross_forward(order, live, q, kv, scale):
    keys = LIVE_MAX * SLOTS
    return pl.pallas_call(
        partial(cross_forward_kernel, scale=scale, step=2),
        out_shape=(OUT_T, KEEP_T),
        in_specs=smem(2) + vmem(2),
        out_specs=tuple(vmem(2)),
        scratch_shapes=[pltpu.VMEM((2 * HEAD, keys), bf16), pltpu.VMEM((keys, HEAD), bf16)],
        compiler_params=params(),
        cost_estimate=cost(keys, 2),
        name="cross_forward",
    )(order, live, q, kv)


def cross_backward(order, live, q, do, keep, kv, scale):
    keys = LIVE_MAX * SLOTS
    return pl.pallas_call(
        partial(cross_backward_kernel, scale=scale, step=2),
        out_shape=(OUT_T, jax.ShapeDtypeStruct((BLOCKS, 2 * HEAD, SLOTS), bf16)),
        in_specs=smem(2) + vmem(4),
        out_specs=tuple(vmem(2)),
        scratch_shapes=[
            pltpu.VMEM((2 * HEAD, keys), bf16),
            pltpu.VMEM((keys, HEAD), bf16),
            pltpu.VMEM((2 * HEAD, keys), bf16),
            pltpu.VMEM((HEAD, keys), f32),
            pltpu.VMEM((HEAD, keys), f32),
        ],
        compiler_params=params(),
        cost_estimate=cost(keys, 5),
        name="cross_backward",
    )(order, live, q, do, keep, kv)


def normed(v):
    centred = v - jnp.mean(v, -1, keepdims=True)
    spread = jnp.mean(centred * centred, -1, keepdims=True)
    r = lax.rsqrt(spread + EPS)
    return centred * r, r


def norm_backward(da, xh, r, gain):
    d = da * (1.0 + gain)
    along = jnp.mean(d * xh, -1, keepdims=True)
    back = r * (d - jnp.mean(d, -1, keepdims=True) - xh * along)
    return back, jnp.sum(da * xh, 0), jnp.sum(da, 0)


def over_item(turned, gathered):
    return lax.dot_general(turned, gathered, (((0, 2), (0, 1)), ((), ())), preferred_element_type=f32)


def column_pieces(grad_t):
    columns, rows = grad_t.shape
    pieces = grad_t.astype(bf16).reshape(2, columns // 2, 4, rows // 4).transpose(0, 2, 1, 3)
    pieces = pieces.reshape(8, columns // 2, rows // 4)
    return jnp.pad(pieces, ((0, 0), (0, 0), (0, 256 - rows // 4)))


def home_route():
    size = dict(zip(AXES, SIZES))
    place = lambda at: sum(at[a] * s for a, s in zip(AXES, (64, 32, 8, 4, 2, 1)))
    route = []
    for spot in every(*[range(size[a]) for a in AXES]):
        at = dict(zip(AXES, spot))
        p = at["x"] * 2 + at["zh"]
        to = dict(x=at["yh"] * 2 + at["c"], zh=at["zl"], zl=at["yl"], yl=p >> 2, yh=p >> 1 & 1, c=p & 1)
        route.append((place(at), place(to)))
    return route


def on_device(
    tokens, patches, patch_counts, camera_ids, modulation, query_weight, key_weight, value_weight, output_weight,
    cross_query, cross_key, cross_value, cross_output, expand_weight, reduce_weight, cotangent,
):
    width = tokens.shape[3]
    scale = HEAD**-0.5
    item = lax.axis_index(ITEMS)
    head = lax.axis_index(ITEM)
    view = lax.axis_index(VIEW)
    camera = lax.dynamic_index_in_dim(camera_ids, item, 0, keepdims=False)
    gains = lax.dynamic_index_in_dim(modulation, camera, 0, keepdims=False).reshape(6, width)
    counts = lax.dynamic_index_in_dim(patch_counts, item, 0, keepdims=False)

    x = tokens[0, 0].astype(f32)
    own_patches = patches[0, 0]
    grad_out = cotangent[0, 0]
    patches_all = lax.all_gather(own_patches, ITEM, axis=0, tiled=False)
    grad_out_all = lax.all_gather(grad_out, ITEM, axis=0, tiled=False)

    live = (jnp.arange(4)[None, :] * SLOTS < counts[:, None]).reshape(BLOCKS)
    n_live = jnp.sum(live.astype(jnp.int32))
    rank = jnp.where(live, jnp.cumsum(live) - 1, n_live + jnp.cumsum(~live) - 1)
    slot = jnp.arange(BLOCKS)
    order = jnp.sum(jnp.where(rank[None, :] == slot[:, None], slot[None, :], 0), 1).astype(jnp.int32)
    n_live = n_live.reshape(1)

    xh1, r1 = normed(x)
    a1 = (xh1 * (1.0 + gains[0]) + gains[1]).astype(bf16)

    def heads_of(weight, rows, rc=1, lc=0):
        return mm(weight, rows, lc, rc).astype(bf16).reshape(HEADS, HEAD, -1)

    qkv = swap(
        jnp.concatenate([heads_of(w, a1) for w in (query_weight, key_weight, value_weight)], 1), ITEM
    )
    o_t, keep_self = self_forward(qkv, scale)
    o1_t = swap(o_t, ITEM).reshape(width, TOK)
    first_sum = x + mm(o1_t, output_weight, 0, 0)
    xh2, r2 = normed(first_sum)
    a2 = (xh2 * (1.0 + gains[2]) + gains[3]).astype(bf16)
    qc = swap(heads_of(cross_query, a2), ITEM)

    own_columns = lambda w: lax.dynamic_slice_in_dim(w, head * HEAD, HEAD, 1)
    kv_weight = jnp.concatenate([own_columns(cross_key), own_columns(cross_value)], 1)
    kv = mm(kv_weight, patches_all.reshape(BLOCKS * SLOTS, -1), 0, 1).astype(bf16)
    oc_t, keep_cross = cross_forward(order, n_live, qc, kv, scale)
    oc1_t = swap(oc_t, ITEM).reshape(width, TOK)
    second_sum = first_sum + mm(oc1_t, cross_output, 0, 0)
    xh3, r3 = normed(second_sum)
    a3 = (xh3 * (1.0 + gains[4]) + gains[5]).astype(bf16)
    u_t = mm(expand_weight, a3, 0, 1)
    h32, gelu_pull = jax.vjp(partial(jax.nn.gelu, approximate=True), u_t)
    h_t = h32.astype(bf16)
    layer_out = second_sum + mm(h_t, reduce_weight, 0, 0)

    dh_t = mm(reduce_weight, grad_out, 1, 1).astype(bf16)
    du_t = gelu_pull(dh_t.astype(f32))[0].astype(bf16)
    da3 = mm(du_t, expand_weight, 0, 1)
    back3, dg3, db3 = norm_backward(da3, xh3, r3, gains[4])
    d_second = grad_out.astype(f32) + back3
    dy2 = d_second.astype(bf16)
    do_t = heads_of(cross_output, dy2, 1, 1)
    hidden = HEADS * HEAD // 4
    sent = jnp.concatenate([do_t, h_t.reshape(HEADS, hidden, TOK), du_t.reshape(HEADS, hidden, TOK)], 1)
    got = swap(sent, ITEM)
    do_c, h_all, du_all = got[:, :HEAD], got[:, HEAD : HEAD + hidden], got[:, HEAD + hidden :]
    acts = lax.all_gather(jnp.stack([a1, a2, a3, dy2]), ITEM, axis=0, tiled=False)
    a1_all, a2_all, a3_all, dy2_all = (acts[:, n] for n in range(4))

    dqc, dkv = cross_backward(order, n_live, qc, do_c, keep_cross, kv, scale)
    halves = dkv.reshape(BLOCKS, 2 * HEAD, 2, TOK).transpose(0, 2, 1, 3).reshape(BLOCKS, 4 * HEAD, TOK)
    got = swap(jnp.concatenate([dqc, halves], 1), ITEM)
    dqc_t = got[:, :HEAD].reshape(width, TOK)
    dkv_t = got[:, HEAD:].reshape(HEADS, 2, 2, HEAD, TOK).transpose(2, 0, 3, 1, 4).reshape(2, width, SLOTS)
    patches_grad = mm(dkv_t[0], cross_key, 0, 1) + mm(dkv_t[1], cross_value, 0, 1)
    da2 = mm(dqc_t, cross_query, 0, 1)
    back2, dg2, db2 = norm_backward(da2, xh2, r2, gains[2])
    d_first = d_second + back2
    dy1 = d_first.astype(bf16)
    dy1_all = lax.all_gather(dy1, ITEM, axis=0, tiled=False)
    do1 = swap(heads_of(output_weight, dy1, 1, 1), ITEM)
    dqkv = self_backward(qkv, do1, keep_self, scale)
    dqkv_t = swap(dqkv, ITEM)
    da1 = sum(
        mm(dqkv_t[:, n * HEAD : (n + 1) * HEAD].reshape(width, TOK), w, 0, 1)
        for n, w in enumerate((query_weight, key_weight, value_weight))
    )
    back1, dg1, db1 = norm_backward(da1, xh1, r1, gains[0])
    tokens_grad = d_first + back1

    qkv_grad = over_item(dqkv, a1_all)
    cq_grad = over_item(dqc, a2_all)
    ckv_grad = over_item(dkv, patches_all)
    e_grad = over_item(du_all, a3_all)
    turned = lambda gathered, block: lax.dot_general(
        gathered, block, (((0, 1), (0, 2)), ((), ())), preferred_element_type=f32
    )
    o_grad = turned(dy1_all, o_t)
    co_grad = turned(dy2_all, oc_t)
    r_grad = turned(grad_out_all, h_all)

    camera_grad = jnp.concatenate([dg1, db1, dg2, db2, dg3, db3]).reshape(8, 4, -1).transpose(1, 0, 2)
    camera_grad = swap(jnp.broadcast_to(camera_grad[None], (4,) + camera_grad.shape).reshape(16, 8, -1), ITEM)
    camera_grad = jnp.sum(camera_grad, 0)
    high = camera_grad.astype(bf16)
    low = (camera_grad - high.astype(f32)).astype(bf16)
    camera_rows = jnp.pad(jnp.stack([high, low], 1), ((0, 0), (0, 14), (0, 256 - camera_grad.shape[1])))

    pieces = [qkv_grad[n * HEAD : (n + 1) * HEAD] for n in range(3)]
    pieces += [cq_grad, ckv_grad[:HEAD], ckv_grad[HEAD:], e_grad]
    pieces = [column_pieces(piece) for piece in pieces]
    columns = sum(piece.shape[1] for piece in pieces)
    got = swap(jnp.concatenate(pieces + [camera_rows], 1), ITEMS).astype(f32)
    from_items = got[:, columns] + got[:, columns + 1]
    hits = camera_ids[None, :] == (view * 4 + jnp.arange(4))[:, None]
    modulation_grad = jnp.sum(jnp.where(hits[:, :, None], from_items[None], 0.0), 1)[:, :192]
    summed = lax.ppermute(jnp.sum(got[:, :columns], 0), AXES, home_route())

    row_grads = jnp.concatenate([o_grad, co_grad, r_grad], 1).astype(bf16).reshape(32, 32, -1)
    got = swap(row_grads, ROW).astype(f32)
    row_sums = jnp.sum(got.reshape((8, 4) + got.shape[1:]), 0)
    rows_of = lambda lo, hi: row_sums[:, :, lo:hi].transpose(0, 2, 1).reshape(4 * (hi - lo), 32)

    half = HEAD // 2
    column_outs = [summed[n * half : (n + 1) * half].T for n in range(6)]
    return (
        layer_out[None, None],
        tokens_grad[None, None],
        patches_grad[None, None],
        modulation_grad,
        column_outs[0],
        column_outs[1],
        column_outs[2],
        rows_of(0, HEAD),
        column_outs[3],
        column_outs[4][:192],
        column_outs[5][:192],
        rows_of(HEAD, 2 * HEAD),
        summed[6 * half :].T,
        rows_of(2 * HEAD, 2 * HEAD + hidden),
    )


def solution(mesh):
    fine = Mesh(mesh.devices.reshape(SIZES), AXES)
    split = P(ROW, VIEW, None, None)
    grads = P(VIEW, ROW)
    return jax.shard_map(
        on_device,
        mesh=fine,
        in_specs=(split, split) + (P(),) * 13 + (split,),
        out_specs=(split,) * 3 + (grads,) * 11,
        check_vma=False,
    )
```

```python
from functools import partial
from itertools import product as every

import jax
import jax.numpy as jnp
from jax import lax
from jax.experimental import pallas as pl
from jax.experimental.pallas import tpu as pltpu
from jax.sharding import Mesh
from jax.sharding import PartitionSpec as P

HEADS = 16
HEAD = 64
TOK = 128
SLOTS = 256
BLOCKS = 16
LIVE_MAX = 13
EPS = 1e-05
LOG2E = 1.4426950408889634
FAR = -1e30

AXES = ("yh", "c", "x", "zh", "zl", "yl")
SIZES = (2, 2, 4, 2, 2, 2)
VIEW = ("yh", "c")
ROW = ("x", "zh", "zl", "yl")
ITEM = ("yh", "c", "zl", "yl")
ITEMS = ("x", "zh")
VMEM_BYTES = 32 * 1024 * 1024

bf16 = jnp.bfloat16
f32 = jnp.float32


def mm(left, right, lc=1, rc=0):
    return lax.dot_general(left, right, (((lc,), (rc,)), ((), ())), preferred_element_type=f32)


def swap(block, axes):
    return lax.all_to_all(block, axes, 0, 0, tiled=True)


def three_parts(row):
    high = row.astype(bf16)
    rest = row - high.astype(f32)
    middle = rest.astype(bf16)
    low = (rest - middle.astype(f32)).astype(bf16)
    return high, middle, low


def softmax_block(q, kt, v, o_ref, keep_ref, at, scale):
    s = mm(q, kt)
    m = jnp.max(s, 1, keepdims=True)
    p = jnp.exp2((s - m) * (scale * LOG2E))
    total = jnp.sum(p, 1, keepdims=True)
    o = mm(p.astype(bf16), v)[:, :HEAD] / total
    lse = m + jnp.log2(total) * (1.0 / (scale * LOG2E))
    packed = jnp.concatenate([o, jnp.broadcast_to(lse, o.shape)], 1).T
    for part in range(packed.shape[1] // TOK):
        piece = packed[:, part * TOK : (part + 1) * TOK]
        o_ref[at + part] = piece[:HEAD].astype(bf16)
        keep_ref[at + part] = piece[: HEAD + 8]


def backward_block(qts, dots, keeps, kt, k, vt, dk_acc, dv_acc, scale):
    q_rows, do_rows = [], []
    for qt, dot, keep in zip(qts, dots, keeps):
        lse = keep[HEAD : HEAD + 1]
        delta = jnp.sum(dot.astype(f32) * keep[:HEAD], 0, keepdims=True) * scale
        one = jnp.ones_like(lse)
        zero = jnp.zeros((HEAD - 4, TOK), f32)
        parts = [part.astype(f32) for part in three_parts(-lse)]
        q_rows.append(jnp.concatenate([qt.astype(f32), one] + parts + [zero], 0))
        parts = [part.astype(f32) for part in three_parts(-delta)]
        do_rows.append(jnp.concatenate([dot.astype(f32) * scale] + parts + [0.0 * one, zero], 0))
    q = jnp.concatenate([rows.T for rows in q_rows], 0).astype(bf16)
    do = jnp.concatenate([rows.T for rows in do_rows], 0).astype(bf16)
    p = jnp.exp2(mm(q, kt) * (scale * LOG2E))
    ds = (p * mm(do, vt)).astype(bf16)
    dq = mm(ds, k)
    dk_acc[...] += mm(jnp.concatenate(qts, 1), ds)
    dv_acc[...] += mm(jnp.concatenate(dots, 1), p.astype(bf16))
    return dq[:, :HEAD]


def store_blocks(ref, at, rows, value):
    turned = value.T
    for part in range(turned.shape[1] // TOK):
        ref[at + part, rows, :] = turned[:, part * TOK : (part + 1) * TOK].astype(ref.dtype)


def self_forward_kernel(qkv_ref, o_ref, keep_ref, kt, v, *, scale, step):
    for j in range(BLOCKS):
        cols = slice(j * TOK, (j + 1) * TOK)
        kt[:, cols] = qkv_ref[j, HEAD : 2 * HEAD, :]
        v[cols, :] = qkv_ref[j, 2 * HEAD :, :].T

    def one(i, carry):
        at = i * step
        q = jnp.concatenate([qkv_ref[at + n, :HEAD, :].T for n in range(step)], 0)
        softmax_block(q, kt[...], v[...], o_ref, keep_ref, at, scale)
        return carry

    lax.fori_loop(0, BLOCKS // step, one, 0)


def self_backward_kernel(qkv_ref, do_ref, keep_ref, out_ref, kt, k, vt, dk_acc, dv_acc, *, scale, step):
    ones = jnp.ones((HEAD, BLOCKS * TOK), bf16)
    row = lax.broadcasted_iota(jnp.int32, ones.shape, 0)
    kt[HEAD:, :] = jnp.where((row >= 1) & (row < 4), ones, 0)
    vt[HEAD:, :] = jnp.where(row < 3, ones, 0)
    for j in range(BLOCKS):
        cols = slice(j * TOK, (j + 1) * TOK)
        kt[:HEAD, cols] = qkv_ref[j, HEAD : 2 * HEAD, :]
        k[cols, :] = qkv_ref[j, HEAD : 2 * HEAD, :].T
        vt[:HEAD, cols] = qkv_ref[j, 2 * HEAD :, :]
    dk_acc[...] = jnp.zeros_like(dk_acc)
    dv_acc[...] = jnp.zeros_like(dv_acc)

    def one(i, carry):
        at = i * step
        qts = [qkv_ref[at + n, :HEAD, :] for n in range(step)]
        dots = [do_ref[at + n] for n in range(step)]
        keeps = [keep_ref[at + n] for n in range(step)]
        dq = backward_block(qts, dots, keeps, kt[...], k[...], vt[...], dk_acc, dv_acc, scale)
        store_blocks(out_ref, at, slice(0, HEAD), dq)
        return carry

    lax.fori_loop(0, BLOCKS // step, one, 0)
    for j in range(BLOCKS):
        cols = slice(j * TOK, (j + 1) * TOK)
        out_ref[j, HEAD : 2 * HEAD, :] = dk_acc[:, cols].astype(bf16)
        out_ref[j, 2 * HEAD :, :] = dv_acc[:, cols].astype(bf16)


def slot_block(kv_ref, index):
    return kv_ref[:, pl.ds(pl.multiple_of(index * SLOTS, SLOTS), SLOTS)]


def cross_forward_kernel(order_ref, live_ref, q_ref, kv_ref, o_ref, keep_ref, kt, v, *, scale, step):
    kt[HEAD:, :] = jnp.zeros((HEAD, LIVE_MAX * SLOTS), bf16)
    for t in range(LIVE_MAX):
        cols = slice(t * SLOTS, (t + 1) * SLOTS)
        block = slot_block(kv_ref, order_ref[t])
        kt[:HEAD, cols] = block[:HEAD]
        bias = jnp.where(t < live_ref[0], 0.0, FAR)
        row = lax.broadcasted_iota(jnp.int32, (16, SLOTS), 0)
        kt[HEAD : HEAD + 16, cols] = jnp.where(row == 0, bias, 0.0).astype(bf16)
        v[cols, :] = block[HEAD:].T
    one_row = jnp.where(lax.broadcasted_iota(jnp.int32, (HEAD, TOK), 0) == 0, 1.0, 0.0)

    def one(i, carry):
        at = i * step
        q = jnp.concatenate(
            [jnp.concatenate([q_ref[at + n].astype(f32), one_row], 0).T for n in range(step)], 0
        ).astype(bf16)
        softmax_block(q, kt[...], v[...], o_ref, keep_ref, at, scale)
        return carry

    lax.fori_loop(0, BLOCKS // step, one, 0)


def cross_backward_kernel(
    order_ref, live_ref, q_ref, do_ref, keep_ref, kv_ref, dq_ref, dkv_ref, kt, k, vt, dk_acc, dv_acc, *, scale, step
):
    shape = (HEAD, LIVE_MAX * SLOTS)
    row = lax.broadcasted_iota(jnp.int32, shape, 0)
    kt[HEAD:, :] = jnp.where((row >= 1) & (row < 4), 1.0, 0.0).astype(bf16)
    vt[HEAD:, :] = jnp.where(row < 3, 1.0, 0.0).astype(bf16)
    for t in range(LIVE_MAX):
        cols = slice(t * SLOTS, (t + 1) * SLOTS)
        block = slot_block(kv_ref, order_ref[t])
        kt[:HEAD, cols] = block[:HEAD]
        bias = jnp.where(t < live_ref[0], 0.0, FAR)
        row = lax.broadcasted_iota(jnp.int32, (16, SLOTS), 0)
        ones = jnp.where((row >= 1) & (row < 4), 1.0, 0.0)
        kt[HEAD : HEAD + 16, cols] = jnp.where(row == 0, bias, ones).astype(bf16)
        k[cols, :] = block[:HEAD].T
        vt[:HEAD, cols] = block[HEAD:]
    dk_acc[...] = jnp.zeros_like(dk_acc)
    dv_acc[...] = jnp.zeros_like(dv_acc)

    def one(i, carry):
        at = i * step
        qts = [q_ref[at + n] for n in range(step)]
        dots = [do_ref[at + n] for n in range(step)]
        keeps = [keep_ref[at + n] for n in range(step)]
        dq = backward_block(qts, dots, keeps, kt[...], k[...], vt[...], dk_acc, dv_acc, scale)
        store_blocks(dq_ref, at, slice(0, HEAD), dq)
        return carry

    lax.fori_loop(0, BLOCKS // step, one, 0)
    for t in range(LIVE_MAX):
        cols = slice(t * SLOTS, (t + 1) * SLOTS)
        dkv_ref[order_ref[t], :HEAD, :] = dk_acc[:, cols].astype(bf16)
        dkv_ref[order_ref[t], HEAD:, :] = dv_acc[:, cols].astype(bf16)
    for t in range(LIVE_MAX, BLOCKS):
        dkv_ref[order_ref[t]] = jnp.zeros((2 * HEAD, SLOTS), bf16)


def params():
    return pltpu.CompilerParams(vmem_limit_bytes=VMEM_BYTES)


def vmem(count):
    return [pl.BlockSpec(memory_space=pltpu.VMEM)] * count


def smem(count):
    return [pl.BlockSpec(memory_space=pltpu.SMEM)] * count


def cost(keys, products):
    flops = 2 * BLOCKS * TOK * keys * HEAD * products
    return pl.CostEstimate(flops=4 * flops, bytes_accessed=4 << 20, transcendentals=BLOCKS * TOK * keys)


OUT_T = jax.ShapeDtypeStruct((BLOCKS, HEAD, TOK), bf16)
KEEP_T = jax.ShapeDtypeStruct((BLOCKS, HEAD + 8, TOK), f32)


def self_forward(qkv, scale):
    keys = BLOCKS * TOK
    return pl.pallas_call(
        partial(self_forward_kernel, scale=scale, step=2),
        out_shape=(OUT_T, KEEP_T),
        in_specs=vmem(1),
        out_specs=tuple(vmem(2)),
        scratch_shapes=[pltpu.VMEM((HEAD, keys), bf16), pltpu.VMEM((keys, HEAD), bf16)],
        compiler_params=params(),
        cost_estimate=cost(keys, 2),
        name="self_forward",
    )(qkv)


def self_backward(qkv, do, keep, scale):
    keys = BLOCKS * TOK
    return pl.pallas_call(
        partial(self_backward_kernel, scale=scale, step=2),
        out_shape=jax.ShapeDtypeStruct((BLOCKS, 3 * HEAD, TOK), bf16),
        in_specs=vmem(3),
        out_specs=vmem(1)[0],
        scratch_shapes=[
            pltpu.VMEM((2 * HEAD, keys), bf16),
            pltpu.VMEM((keys, HEAD), bf16),
            pltpu.VMEM((2 * HEAD, keys), bf16),
            pltpu.VMEM((HEAD, keys), f32),
            pltpu.VMEM((HEAD, keys), f32),
        ],
        compiler_params=params(),
        cost_estimate=cost(keys, 5),
        name="self_backward",
    )(qkv, do, keep)


def cross_forward(order, live, q, kv, scale):
    keys = LIVE_MAX * SLOTS
    return pl.pallas_call(
        partial(cross_forward_kernel, scale=scale, step=2),
        out_shape=(OUT_T, KEEP_T),
        in_specs=smem(2) + vmem(2),
        out_specs=tuple(vmem(2)),
        scratch_shapes=[pltpu.VMEM((2 * HEAD, keys), bf16), pltpu.VMEM((keys, HEAD), bf16)],
        compiler_params=params(),
        cost_estimate=cost(keys, 2),
        name="cross_forward",
    )(order, live, q, kv)


def cross_backward(order, live, q, do, keep, kv, scale):
    keys = LIVE_MAX * SLOTS
    return pl.pallas_call(
        partial(cross_backward_kernel, scale=scale, step=2),
        out_shape=(OUT_T, jax.ShapeDtypeStruct((BLOCKS, 2 * HEAD, SLOTS), bf16)),
        in_specs=smem(2) + vmem(4),
        out_specs=tuple(vmem(2)),
        scratch_shapes=[
            pltpu.VMEM((2 * HEAD, keys), bf16),
            pltpu.VMEM((keys, HEAD), bf16),
            pltpu.VMEM((2 * HEAD, keys), bf16),
            pltpu.VMEM((HEAD, keys), f32),
            pltpu.VMEM((HEAD, keys), f32),
        ],
        compiler_params=params(),
        cost_estimate=cost(keys, 5),
        name="cross_backward",
    )(order, live, q, do, keep, kv)


def normed(v):
    centred = v - jnp.mean(v, -1, keepdims=True)
    spread = jnp.mean(centred * centred, -1, keepdims=True)
    r = lax.rsqrt(spread + EPS)
    return centred * r, r


def norm_backward(da, xh, r, gain):
    d = da * (1.0 + gain)
    along = jnp.mean(d * xh, -1, keepdims=True)
    return r * (d - jnp.mean(d, -1, keepdims=True) - xh * along)


def token_rows(ref, lo, hi):
    block = ref[:, lo:hi, :]
    return block.reshape(HEADS * (hi - lo), block.shape[2]).T


def store_heads(ref, lo, value):
    turned = value.T.astype(bf16)
    ref[:, lo : lo + HEAD, :] = turned.reshape(HEADS, HEAD, turned.shape[1])


def load_all(pairs, sems):
    copies = [pltpu.make_async_copy(src, dst, sems.at[n]) for n, (src, dst) in enumerate(pairs)]
    for copy in copies:
        copy.start()
    return copies


def enter_kernel(camera_ref, x_ref, cot_ref, mod_ref, wq_any, wk_any, wv_any, sent_ref, acts_ref, gains_ref, wq, wk, wv, sems):
    copies = load_all(((wq_any, wq), (wk_any, wk), (wv_any, wv)), sems)
    row = mod_ref[pl.ds(camera_ref[0], 1), :]
    for n in range(6):
        gains_ref[n : n + 1, :] = row[:, n * WIDTH : (n + 1) * WIDTH]
    gains_ref[6:8, :] = jnp.zeros((2, WIDTH), f32)
    xh, _ = normed(x_ref[...].astype(f32))
    acts_ref[0] = cot_ref[...]
    acts_ref[1] = xh.astype(bf16)
    a1 = (xh * (1.0 + gains_ref[0:1, :]) + gains_ref[1:2, :]).astype(bf16)
    for n, (copy, w) in enumerate(zip(copies, (wq, wk, wv))):
        copy.wait()
        store_heads(sent_ref, n * HEAD, mm(a1, w[...]))


def middle_kernel(o_ref, x_ref, gains_ref, wo_any, wcq_any, first_ref, a2_ref, q_ref, wo, wcq, sems):
    copies = load_all(((wo_any, wo), (wcq_any, wcq)), sems)
    o1 = token_rows(o_ref, 0, HEAD)
    copies[0].wait()
    first = x_ref[...].astype(f32) + mm(o1, wo[...])
    first_ref[...] = first
    xh, _ = normed(first)
    a2 = (xh * (1.0 + gains_ref[2:3, :]) + gains_ref[3:4, :]).astype(bf16)
    a2_ref[...] = a2
    copies[1].wait()
    store_heads(q_ref, 0, mm(a2, wcq[...]))


def gelu_both(a3, cot, we, wr):
    u = mm(a3, we)
    square = u * u
    t = jnp.tanh(u * (GELU_A + GELU_A * GELU_B * square))
    h = (0.5 * u * (1.0 + t)).astype(bf16)
    dh = mm(cot, wr, 1, 1).astype(bf16).astype(f32)
    slope = 0.5 * (1.0 + t) + 0.5 * u * (1.0 - t * t) * (GELU_A + 3.0 * GELU_A * GELU_B * square)
    return h, (dh * slope).astype(bf16)


def mlp_kernel(
    oc_ref, first_ref, a2_ref, cot_ref, gains_ref, wco_ref, we_ref, wr_ref,
    out_ref, back_ref, acts_ref, do_ref, dgb_ref, a3, second, y, da3,
):
    step = pl.program_id(0)

    @pl.when(step == 0)
    def _():
        total = first_ref[...] + mm(token_rows(oc_ref, 0, HEAD), wco_ref[...])
        second[...] = total
        xh, _ = normed(total)
        a3[...] = (xh * (1.0 + gains_ref[4:5, :]) + gains_ref[5:6, :]).astype(bf16)
        y[...] = jnp.zeros_like(y)
        da3[...] = jnp.zeros_like(da3)

    h, du = gelu_both(a3[...], cot_ref[...], we_ref[...], wr_ref[...])
    y[...] += mm(h, wr_ref[...])
    da3[...] += mm(du, we_ref[...], 1, 1)

    @pl.when(step == pl.num_programs(0) - 1)
    def _():
        total = second[...]
        out_ref[...] = total + y[...]
        xh, r = normed(total)
        d = da3[...]
        dgb_ref[...] = jnp.zeros_like(dgb_ref)
        dgb_ref[0:1, :] = jnp.sum(d * xh, 0, keepdims=True)
        dgb_ref[1:2, :] = jnp.sum(d, 0, keepdims=True)
        back = cot_ref[...].astype(f32) + norm_backward(d, xh, r, gains_ref[4:5, :])
        back_ref[...] = back
        dy2 = back.astype(bf16)
        acts_ref[0] = a2_ref[...]
        acts_ref[1] = a3[...]
        acts_ref[2] = dy2
        store_heads(do_ref, 0, mm(dy2, wco_ref[...], 1, 1))


def return_kernel(dq_ref, first_ref, second_back_ref, gains_ref, wcq_any, wo_any, back_ref, dy_ref, do_ref, dgb_ref, wcq, wo, sems):
    copies = load_all(((wcq_any, wcq), (wo_any, wo)), sems)
    xh, r = normed(first_ref[...])
    dq = token_rows(dq_ref, 0, HEAD)
    copies[0].wait()
    da2 = mm(dq, wcq[...], 1, 1)
    dgb_ref[...] = jnp.zeros_like(dgb_ref)
    dgb_ref[0:1, :] = jnp.sum(da2 * xh, 0, keepdims=True)
    dgb_ref[1:2, :] = jnp.sum(da2, 0, keepdims=True)
    back = second_back_ref[...] + norm_backward(da2, xh, r, gains_ref[2:3, :])
    back_ref[...] = back
    dy1 = back.astype(bf16)
    dy_ref[...] = dy1
    copies[1].wait()
    store_heads(do_ref, 0, mm(dy1, wo[...], 1, 1))


def leave_kernel(got_ref, x_ref, back_ref, gains_ref, wq_any, wk_any, wv_any, out_ref, wq, wk, wv, sems):
    copies = load_all(((wq_any, wq), (wk_any, wk), (wv_any, wv)), sems)
    xh, r = normed(x_ref[...].astype(f32))
    da1 = jnp.zeros(out_ref.shape, f32)
    for n, (copy, w) in enumerate(zip(copies, (wq, wk, wv))):
        copy.wait()
        da1 += mm(token_rows(got_ref, n * HEAD, (n + 1) * HEAD), w[...], 1, 1)
    out_ref[...] = back_ref[...] + norm_backward(da1, xh, r, gains_ref[0:1, :])


def patches_kernel(got_ref, wk_ref, wv_ref, out_ref):
    dk = token_rows(got_ref, 0, HEAD)
    dv = token_rows(got_ref, HEAD, 2 * HEAD)
    out_ref[...] = mm(dk, wk_ref[...], 1, 1) + mm(dv, wv_ref[...], 1, 1)


def side_by_side(ref, lo, hi):
    return jnp.concatenate([ref[n, lo:hi, :] for n in range(ref.shape[0])], 1)


def one_above_other(ref):
    block = ref[...]
    return block.reshape(-1, block.shape[-1])


def store_columns(ref, at, grad_t):
    columns, rows = grad_t.shape[0] // 2, grad_t.shape[1] // 4
    for e in range(2):
        for v in range(4):
            piece = grad_t[e * columns : (e + 1) * columns, v * rows : (v + 1) * rows]
            if rows < 256:
                piece = jnp.concatenate([piece, jnp.zeros((columns, 256 - rows), f32)], 1)
            ref[e * 4 + v, at : at + columns, :] = piece.astype(bf16)


def early_kernel(
    head_ref, cot_ref, a2_ref, a3_ref, dqc_ref, dkv_ref, patches_ref, we_ref, wr_ref, col_ref, row_ref, e_acc, r_acc, q_acc, kv_acc
):
    step = pl.program_id(0)
    a3, cot = one_above_other(a3_ref), one_above_other(cot_ref)
    h, du = gelu_both(a3, cot, we_ref[...], wr_ref[...])
    r = mm(h.T, cot)
    e = mm(du.T, a3)
    q = mm(side_by_side(dqc_ref, 0, HEAD), one_above_other(a2_ref))
    kv = mm(side_by_side(dkv_ref, 0, 2 * HEAD), one_above_other(patches_ref))

    @pl.when(step == 0)
    def _():
        r_acc[...], e_acc[...], q_acc[...], kv_acc[...] = r, e, q, kv

    @pl.when(step > 0)
    def _():
        r_acc[...] += r
        e_acc[...] += e
        q_acc[...] += q
        kv_acc[...] += kv

    @pl.when(step == pl.num_programs(0) - 1)
    def _():
        store_columns(col_ref, 0, q_acc[...])
        store_columns(col_ref, 32, kv_acc[:HEAD, :])
        store_columns(col_ref, 64, kv_acc[HEAD:, :])
        store_columns(col_ref, 96, e_acc[...])
        row_ref[...] = r_acc[...].T.astype(bf16).reshape(row_ref.shape)


def late_kernel(dqkv_ref, xh_ref, wt_ref, gains_ref, col_ref, dgb_ref, qkv_acc, sums):
    step = pl.program_id(0)
    turned = side_by_side(dqkv_ref, 0, 3 * HEAD)
    qkv = mm(turned, one_above_other(xh_ref))
    total = jnp.broadcast_to(jnp.sum(turned.astype(f32), 1, keepdims=True), sums.shape)

    @pl.when(step == 0)
    def _():
        qkv_acc[...], sums[...] = qkv, total

    @pl.when(step > 0)
    def _():
        qkv_acc[...] += qkv
        sums[...] += total

    @pl.when(step == pl.num_programs(0) - 1)
    def _():
        moment = qkv_acc[...]
        count = sums[:, 0:1]
        weights = wt_ref[...].astype(f32)
        dgb_ref[...] = jnp.zeros_like(dgb_ref)
        dgb_ref[0:1, :] = jnp.sum(weights * moment, 0, keepdims=True)
        dgb_ref[1:2, :] = jnp.sum(weights * count, 0, keepdims=True)
        grad = moment * (1.0 + gains_ref[0:1, :]) + count * gains_ref[1:2, :]
        for n in range(3):
            store_columns(col_ref, n * 32, grad[n * HEAD : (n + 1) * HEAD])


def outputs_kernel(o_ref, dy1_ref, oc_ref, dy2_ref, row_ref, acc):
    step = pl.program_id(0)
    o = mm(side_by_side(o_ref, 0, HEAD), one_above_other(dy1_ref))
    oc = mm(side_by_side(oc_ref, 0, HEAD), one_above_other(dy2_ref))
    both = jnp.concatenate([o, oc], 0)

    @pl.when(step == 0)
    def _():
        acc[...] = both

    @pl.when(step > 0)
    def _():
        acc[...] += both

    @pl.when(step == pl.num_programs(0) - 1)
    def _():
        row_ref[...] = acc[...].T.astype(bf16).reshape(row_ref.shape)


WIDTH = 1024
HIDDEN = 4096
PATCH = 768
UNITS = HIDDEN // BLOCKS
GELU_A = 0.7978845608028654
GELU_B = 0.044715


def shaped(*shape, dtype=bf16):
    return jax.ShapeDtypeStruct(shape, dtype)


ANY = pl.BlockSpec(memory_space=pl.ANY)
V = pl.BlockSpec(memory_space=pltpu.VMEM)
S = pl.BlockSpec(memory_space=pltpu.SMEM)
MB = 1 << 20


def weight(rows=WIDTH, columns=WIDTH):
    return pltpu.VMEM((rows, columns), bf16)


def call(kernel, name, ins, outs, scratch, flops, traffic, limit=40):
    return pl.pallas_call(
        kernel,
        out_shape=outs,
        in_specs=ins,
        out_specs=jax.tree.map(lambda _: V, outs),
        scratch_shapes=scratch,
        compiler_params=pltpu.CompilerParams(vmem_limit_bytes=limit * MB),
        cost_estimate=pl.CostEstimate(flops=flops, bytes_accessed=traffic, transcendentals=0),
        name=name,
    )


TOKENS_F32 = shaped(TOK, WIDTH, dtype=f32)
TOKENS_BF16 = shaped(TOK, WIDTH)
ROWS_F32 = shaped(8, WIDTH, dtype=f32)
SQUARE = 2 * TOK * WIDTH * WIDTH


def enter(*args):
    return call(
        enter_kernel, "enter", [S, V, V, V, ANY, ANY, ANY],
        (shaped(BLOCKS, 3 * HEAD, TOK), shaped(2, TOK, WIDTH), ROWS_F32),
        [weight(), weight(), weight(), pltpu.SemaphoreType.DMA((3,))], 3 * SQUARE, 8 * MB,
    )(*args)


def middle(*args):
    return call(
        middle_kernel, "middle", [V, V, V, ANY, ANY], (TOKENS_F32, TOKENS_BF16, OUT_T),
        [weight(), weight(), pltpu.SemaphoreType.DMA((2,))], 2 * SQUARE, 6 * MB,
    )(*args)


def mlp(*args):
    steps = 8
    width = HIDDEN // steps
    whole = lambda *shape: pl.BlockSpec(shape, lambda i: (0,) * len(shape))
    outs = (TOKENS_F32, TOKENS_F32, shaped(3, TOK, WIDTH), OUT_T, ROWS_F32)
    out_specs = tuple(whole(*o.shape) for o in outs)
    tokens = whole(TOK, WIDTH)
    return pl.pallas_call(
        mlp_kernel,
        grid=(steps,),
        out_shape=outs,
        in_specs=[
            whole(BLOCKS, HEAD, TOK), tokens, tokens, tokens, whole(8, WIDTH), whole(WIDTH, WIDTH),
            pl.BlockSpec((WIDTH, width), lambda i: (0, i)), pl.BlockSpec((width, WIDTH), lambda i: (i, 0)),
        ],
        out_specs=out_specs,
        scratch_shapes=[
            pltpu.VMEM((TOK, WIDTH), bf16), pltpu.VMEM((TOK, WIDTH), f32),
            pltpu.VMEM((TOK, WIDTH), f32), pltpu.VMEM((TOK, WIDTH), f32),
        ],
        compiler_params=pltpu.CompilerParams(vmem_limit_bytes=40 * MB),
        cost_estimate=pl.CostEstimate(flops=18 * SQUARE, bytes_accessed=22 * MB, transcendentals=TOK * HIDDEN),
        name="mlp",
    )(*args)


def returned(*args):
    return call(
        return_kernel, "returned", [V, V, V, V, ANY, ANY], (TOKENS_F32, TOKENS_BF16, OUT_T, ROWS_F32),
        [weight(), weight(), pltpu.SemaphoreType.DMA((2,))], 2 * SQUARE, 6 * MB,
    )(*args)


def leave(*args):
    return call(
        leave_kernel, "leave", [V, V, V, V, ANY, ANY, ANY], TOKENS_F32,
        [weight(), weight(), weight(), pltpu.SemaphoreType.DMA((3,))], 3 * SQUARE, 8 * MB,
    )(*args)


def patches_back(*args):
    return call(
        patches_kernel, "patches_back", [V, V, V], shaped(SLOTS, PATCH, dtype=f32), [], 3 * SQUARE, 5 * MB
    )(*args)


STEPS = 4


def blocks_of(*shape, at=None):
    if at is None:
        return pl.BlockSpec((BLOCKS // STEPS,) + shape, lambda i: (i,) + (0,) * len(shape))
    return pl.BlockSpec((BLOCKS // STEPS, 1) + shape, lambda i: (i, at) + (0,) * len(shape))


def whole_block(*shape):
    return pl.BlockSpec(shape, lambda i: (0,) * len(shape))


def early_grads(head, first_acts, acts, dqc, dkv, patches_all, expand_weight, reduce_weight):
    outs = (shaped(8, 224, 256), shaped(32, 32, UNITS))
    by_head = lambda spec: pl.BlockSpec(spec.block_shape, lambda i, head: spec.index_map(i))
    ins = [
        blocks_of(TOK, WIDTH, at=0), blocks_of(TOK, WIDTH, at=0), blocks_of(TOK, WIDTH, at=1),
        blocks_of(HEAD, TOK), blocks_of(2 * HEAD, SLOTS), blocks_of(SLOTS, PATCH),
    ]
    own = [
        pl.BlockSpec((WIDTH, UNITS), lambda i, head: (0, head[0])),
        pl.BlockSpec((UNITS, WIDTH), lambda i, head: (head[0], 0)),
    ]
    return pl.pallas_call(
        early_kernel,
        grid_spec=pltpu.PrefetchScalarGridSpec(
            num_scalar_prefetch=1,
            grid=(STEPS,),
            in_specs=[by_head(spec) for spec in ins] + own,
            out_specs=tuple(by_head(whole_block(*o.shape)) for o in outs),
            scratch_shapes=[
                pltpu.VMEM((UNITS, WIDTH), f32), pltpu.VMEM((UNITS, WIDTH), f32),
                pltpu.VMEM((HEAD, WIDTH), f32), pltpu.VMEM((2 * HEAD, PATCH), f32),
            ],
        ),
        out_shape=outs,
        compiler_params=pltpu.CompilerParams(vmem_limit_bytes=40 * MB),
        cost_estimate=pl.CostEstimate(flops=20 * SQUARE, bytes_accessed=20 * MB, transcendentals=0),
        name="early_grads",
    )(head, first_acts, acts, acts, dqc, dkv, patches_all, expand_weight, reduce_weight)


def late_grads(dqkv, first_acts, weights_t, gains):
    outs = (shaped(8, 96, 256), ROWS_F32)
    return pl.pallas_call(
        late_kernel,
        grid=(STEPS,),
        out_shape=outs,
        in_specs=[blocks_of(3 * HEAD, TOK), blocks_of(TOK, WIDTH, at=1), whole_block(3 * HEAD, WIDTH), whole_block(8, WIDTH)],
        out_specs=tuple(whole_block(*o.shape) for o in outs),
        scratch_shapes=[pltpu.VMEM((3 * HEAD, WIDTH), f32), pltpu.VMEM((3 * HEAD, TOK), f32)],
        compiler_params=pltpu.CompilerParams(vmem_limit_bytes=40 * MB),
        cost_estimate=pl.CostEstimate(flops=4 * SQUARE, bytes_accessed=6 * MB, transcendentals=0),
        name="late_grads",
    )(dqkv, first_acts, weights_t, gains)


def output_grads(o_t, dy1_all, oc_t, acts):
    out = shaped(32, 32, 2 * HEAD)
    return pl.pallas_call(
        outputs_kernel,
        grid=(STEPS,),
        out_shape=out,
        in_specs=[blocks_of(HEAD, TOK), blocks_of(TOK, WIDTH), blocks_of(HEAD, TOK), blocks_of(TOK, WIDTH, at=2)],
        out_specs=whole_block(*out.shape),
        scratch_shapes=[pltpu.VMEM((2 * HEAD, WIDTH), f32)],
        compiler_params=pltpu.CompilerParams(vmem_limit_bytes=40 * MB),
        cost_estimate=pl.CostEstimate(flops=3 * SQUARE, bytes_accessed=9 * MB, transcendentals=0),
        name="output_grads",
    )(o_t, dy1_all, oc_t, acts)


def home_route():
    size = dict(zip(AXES, SIZES))
    place = lambda at: sum(at[a] * s for a, s in zip(AXES, (64, 32, 8, 4, 2, 1)))
    route = []
    for spot in every(*[range(size[a]) for a in AXES]):
        at = dict(zip(AXES, spot))
        p = at["x"] * 2 + at["zh"]
        to = dict(x=at["yh"] * 2 + at["c"], zh=at["zl"], zl=at["yl"], yl=p >> 2, yh=p >> 1 & 1, c=p & 1)
        route.append((place(at), place(to)))
    return route


def on_device(
    tokens, patches, patch_counts, camera_ids, modulation, query_weight, key_weight, value_weight, output_weight,
    cross_query, cross_key, cross_value, cross_output, expand_weight, reduce_weight, cotangent,
):
    scale = HEAD**-0.5
    item = lax.axis_index(ITEMS)
    head = lax.axis_index(ITEM)
    view = lax.axis_index(VIEW)
    camera = lax.dynamic_slice_in_dim(camera_ids, item, 1, 0)
    counts = lax.dynamic_index_in_dim(patch_counts, item, 0, keepdims=False)
    gather = lambda block: lax.all_gather(block, ITEM, axis=0, tiled=False)

    x = tokens[0, 0]
    grad_out = cotangent[0, 0]
    patches_all = gather(patches[0, 0])

    live = (jnp.arange(4)[None, :] * SLOTS < counts[:, None]).reshape(BLOCKS)
    n_live = jnp.sum(live.astype(jnp.int32))
    rank = jnp.where(live, jnp.cumsum(live) - 1, n_live + jnp.cumsum(~live) - 1)
    slot = jnp.arange(BLOCKS)
    order = jnp.sum(jnp.where(rank[None, :] == slot[:, None], slot[None, :], 0), 1).astype(jnp.int32)
    n_live = n_live.reshape(1)
    own_columns = lambda w: lax.dynamic_slice_in_dim(w, head * HEAD, HEAD, 1)
    kv_weight = jnp.concatenate([own_columns(cross_key), own_columns(cross_value)], 1)
    weights_t = jnp.concatenate([own_columns(w).T for w in (query_weight, key_weight, value_weight)], 0)

    after = lambda value, *others: lax.optimization_barrier((value,) + others)[0]
    sent, first_acts, gains = enter(camera, x, grad_out, modulation, query_weight, key_weight, value_weight)
    qkv, kv_weight, weights_t, order, n_live = lax.optimization_barrier(
        (swap(sent, ITEM), kv_weight, weights_t, order, n_live)
    )
    first_acts = gather(first_acts)
    o_t, keep_self = self_forward(qkv, scale)
    first_sum, a2, sent = middle(swap(o_t, ITEM), x, gains, output_weight, cross_query)
    qc = swap(sent, ITEM)
    kv = mm(kv_weight, patches_all.reshape(BLOCKS * SLOTS, -1), 0, 1).astype(bf16)
    oc_t, keep_cross = cross_forward(order, n_live, qc, kv, scale)
    layer_out, d_second, acts, sent, dgb3 = mlp(
        swap(oc_t, ITEM), first_sum, a2, grad_out, gains, cross_output, expand_weight, reduce_weight
    )
    do_c = swap(sent, ITEM)
    acts = gather(acts)

    dqc, dkv = cross_backward(order, n_live, qc, do_c, keep_cross, kv, scale)
    d_first, dy1, sent, dgb2 = returned(swap(dqc, ITEM), first_sum, d_second, gains, cross_query, output_weight)
    do1 = swap(sent, ITEM)
    dy1_all = gather(dy1)
    dkv_got = swap(after(dkv, do1), ITEM)
    dqkv = self_backward(qkv, do1, keep_self, scale)
    col_late, dgb1 = late_grads(dqkv, first_acts, weights_t, gains)
    dqkv, dkv_got = lax.optimization_barrier((dqkv, dkv_got))
    patches_grad = patches_back(dkv_got, cross_key, cross_value)
    col_early, row_early = early_grads(
        head.reshape(1), first_acts, acts, after(dqc, dqkv), dkv, patches_all, expand_weight, reduce_weight
    )
    row_late = output_grads(after(o_t, col_early), dy1_all, oc_t, acts)

    camera_grad = jnp.concatenate([dgb1[:2], dgb2[:2], dgb3[:2]], 0).reshape(8, 4, -1).transpose(1, 0, 2)
    camera_grad = camera_grad.reshape(4, -1, TOK)
    lines = camera_grad.shape[1]
    high = camera_grad.astype(bf16)
    low = (camera_grad - high.astype(f32)).astype(bf16)
    camera_grad = jnp.concatenate([high, low, jnp.zeros((4, 32 - 2 * lines, TOK), bf16)], 1)
    camera_grad = jnp.broadcast_to(camera_grad[None], (4,) + camera_grad.shape).reshape(BLOCKS, 32, TOK)
    got = swap(jnp.concatenate([dqkv, camera_grad], 1), ITEM)
    tokens_grad = leave(got, x, d_first, gains, query_weight, key_weight, value_weight)
    camera_sum = jnp.sum(got[:, 3 * HEAD :].astype(f32), 0)
    camera_sum = (camera_sum[:lines] + camera_sum[lines : 2 * lines]).reshape(8, -1)
    high = camera_sum.astype(bf16)
    low = (camera_sum - high.astype(f32)).astype(bf16)
    camera_rows = jnp.pad(jnp.stack([high, low], 1), ((0, 0), (0, 14), (0, 256 - camera_sum.shape[1])))

    columns = col_late.shape[1] + col_early.shape[1]
    got = swap(jnp.concatenate([col_late, col_early, camera_rows], 1), ITEMS).astype(f32)
    from_items = got[:, columns] + got[:, columns + 1]
    hits = camera_ids[None, :] == (view * 4 + jnp.arange(4))[:, None]
    modulation_grad = jnp.sum(jnp.where(hits[:, :, None], from_items[None], 0.0), 1)[:, :192]
    summed = lax.ppermute(jnp.sum(got[:, :columns], 0), AXES, home_route())

    got = swap(after(jnp.concatenate([row_early, row_late], 2), got), ROW).astype(f32)
    row_sums = jnp.sum(got.reshape((8, 4) + got.shape[1:]), 0)
    rows_of = lambda lo, hi: row_sums[:, :, lo:hi].transpose(0, 2, 1).reshape(4 * (hi - lo), 32)

    half = HEAD // 2
    column_outs = [summed[n * half : (n + 1) * half].T for n in range(6)]
    return (
        layer_out[None, None],
        tokens_grad[None, None],
        patches_grad[None, None],
        modulation_grad,
        column_outs[0],
        column_outs[1],
        column_outs[2],
        rows_of(UNITS, UNITS + HEAD),
        column_outs[3],
        column_outs[4][:192],
        column_outs[5][:192],
        rows_of(UNITS + HEAD, UNITS + 2 * HEAD),
        summed[6 * half :].T,
        rows_of(0, UNITS),
    )


def solution(mesh):
    fine = Mesh(mesh.devices.reshape(SIZES), AXES)
    split = P(ROW, VIEW, None, None)
    grads = P(VIEW, ROW)
    return jax.shard_map(
        on_device,
        mesh=fine,
        in_specs=(split, split) + (P(),) * 13 + (split,),
        out_specs=(split,) * 3 + (grads,) * 11,
        check_vma=False,
    )
```

```python
from functools import partial
from itertools import product as every

import jax
import jax.numpy as jnp
from jax import lax
from jax.experimental import pallas as pl
from jax.experimental.pallas import tpu as pltpu
from jax.sharding import Mesh
from jax.sharding import PartitionSpec as P

HEADS = 16
HEAD = 64
TOK = 128
SLOTS = 256
BLOCKS = 16
LIVE_MAX = 13
EPS = 1e-05
LOG2E = 1.4426950408889634
FAR = -1e30

AXES = ("yh", "c", "x", "zh", "zl", "yl")
SIZES = (2, 2, 4, 2, 2, 2)
VIEW = ("yh", "c")
ROW = ("x", "zh", "zl", "yl")
ITEM = ("yh", "c", "zl", "yl")
ITEMS = ("x", "zh")
GATHER = ("zl", "yl", "yh", "c")
VMEM_BYTES = 60 * 1024 * 1024

bf16 = jnp.bfloat16
f32 = jnp.float32


def mm(left, right, lc=1, rc=0):
    return lax.dot_general(left, right, (((lc,), (rc,)), ((), ())), preferred_element_type=f32)


def swap(block, axes):
    return lax.all_to_all(block, axes, 0, 0, tiled=True)


def three_parts(row):
    high = row.astype(bf16)
    rest = row - high.astype(f32)
    middle = rest.astype(bf16)
    low = (rest - middle.astype(f32)).astype(bf16)
    return high, middle, low


def softmax_block(q, kt, v, o_ref, keep_ref, at, scale):
    s = mm(q, kt)
    m = jnp.max(s, 1, keepdims=True)
    p = jnp.exp2((s - m) * (scale * LOG2E))
    total = jnp.sum(p, 1, keepdims=True)
    o = mm(p.astype(bf16), v)[:, :HEAD] / total
    lse = m + jnp.log2(total) * (1.0 / (scale * LOG2E))
    packed = jnp.concatenate([o, jnp.broadcast_to(lse, o.shape)], 1).T
    for part in range(packed.shape[1] // TOK):
        piece = packed[:, part * TOK : (part + 1) * TOK]
        o_ref[at + part] = piece[:HEAD].astype(bf16)
        keep_ref[at + part] = piece[: HEAD + 8]


def backward_block(qts, dots, keeps, kt, k, vt, dk_acc, dv_acc, scale):
    q_rows, do_rows = [], []
    for qt, dot, keep in zip(qts, dots, keeps):
        lse = keep[HEAD : HEAD + 1]
        delta = jnp.sum(dot.astype(f32) * keep[:HEAD], 0, keepdims=True) * scale
        one = jnp.ones_like(lse)
        zero = jnp.zeros((HEAD - 4, TOK), f32)
        parts = [part.astype(f32) for part in three_parts(-lse)]
        q_rows.append(jnp.concatenate([qt.astype(f32), one] + parts + [zero], 0))
        parts = [part.astype(f32) for part in three_parts(-delta)]
        do_rows.append(jnp.concatenate([dot.astype(f32) * scale] + parts + [0.0 * one, zero], 0))
    q = jnp.concatenate([rows.T for rows in q_rows], 0).astype(bf16)
    do = jnp.concatenate([rows.T for rows in do_rows], 0).astype(bf16)
    p = jnp.exp2(mm(q, kt) * (scale * LOG2E))
    ds = (p * mm(do, vt)).astype(bf16)
    dq = mm(ds, k)
    dk_acc[...] += mm(jnp.concatenate(qts, 1), ds)
    dv_acc[...] += mm(jnp.concatenate(dots, 1), p.astype(bf16))
    return dq[:, :HEAD]


def store_blocks(ref, at, rows, value):
    turned = value.T
    for part in range(turned.shape[1] // TOK):
        ref[at + part, rows, :] = turned[:, part * TOK : (part + 1) * TOK].astype(ref.dtype)


def self_forward_kernel(qkv_ref, o_ref, keep_ref, kt, v, *, scale, step):
    for j in range(BLOCKS):
        cols = slice(j * TOK, (j + 1) * TOK)
        kt[:, cols] = qkv_ref[j, HEAD : 2 * HEAD, :]
        v[cols, :] = qkv_ref[j, 2 * HEAD :, :].T

    def one(i, carry):
        at = i * step
        q = jnp.concatenate([qkv_ref[at + n, :HEAD, :].T for n in range(step)], 0)
        softmax_block(q, kt[...], v[...], o_ref, keep_ref, at, scale)
        return carry

    lax.fori_loop(0, BLOCKS // step, one, 0)


def self_backward_kernel(qkv_ref, do_ref, keep_ref, out_ref, kt, k, vt, dk_acc, dv_acc, *, scale, step):
    ones = jnp.ones((HEAD, BLOCKS * TOK), bf16)
    row = lax.broadcasted_iota(jnp.int32, ones.shape, 0)
    kt[HEAD:, :] = jnp.where((row >= 1) & (row < 4), ones, 0)
    vt[HEAD:, :] = jnp.where(row < 3, ones, 0)
    for j in range(BLOCKS):
        cols = slice(j * TOK, (j + 1) * TOK)
        kt[:HEAD, cols] = qkv_ref[j, HEAD : 2 * HEAD, :]
        k[cols, :] = qkv_ref[j, HEAD : 2 * HEAD, :].T
        vt[:HEAD, cols] = qkv_ref[j, 2 * HEAD :, :]
    dk_acc[...] = jnp.zeros_like(dk_acc)
    dv_acc[...] = jnp.zeros_like(dv_acc)

    def one(i, carry):
        at = i * step
        qts = [qkv_ref[at + n, :HEAD, :] for n in range(step)]
        dots = [do_ref[at + n, :HEAD, :] for n in range(step)]
        keeps = [keep_ref[at + n] for n in range(step)]
        dq = backward_block(qts, dots, keeps, kt[...], k[...], vt[...], dk_acc, dv_acc, scale)
        store_blocks(out_ref, at, slice(0, HEAD), dq)
        return carry

    lax.fori_loop(0, BLOCKS // step, one, 0)
    for j in range(BLOCKS):
        cols = slice(j * TOK, (j + 1) * TOK)
        out_ref[j, HEAD : 2 * HEAD, :] = dk_acc[:, cols].astype(bf16)
        out_ref[j, 2 * HEAD :, :] = dv_acc[:, cols].astype(bf16)


def slot_block(kv_ref, index):
    return kv_ref[:, pl.ds(pl.multiple_of(index * SLOTS, SLOTS), SLOTS)]


def own_place(index):
    return (index % 4) * 4 + index // 4


def cross_forward_kernel(order_ref, live_ref, q_ref, kv_ref, o_ref, keep_ref, kt, v, *, scale, step):
    kt[HEAD:, :] = jnp.zeros((HEAD, LIVE_MAX * SLOTS), bf16)
    for t in range(LIVE_MAX):
        cols = slice(t * SLOTS, (t + 1) * SLOTS)
        block = slot_block(kv_ref, order_ref[t])
        kt[:HEAD, cols] = block[:HEAD]
        bias = jnp.where(t < live_ref[0], 0.0, FAR)
        row = lax.broadcasted_iota(jnp.int32, (16, SLOTS), 0)
        kt[HEAD : HEAD + 16, cols] = jnp.where(row == 0, bias, 0.0).astype(bf16)
        v[cols, :] = block[HEAD:].T
    one_row = jnp.where(lax.broadcasted_iota(jnp.int32, (HEAD, TOK), 0) == 0, 1.0, 0.0)

    def one(i, carry):
        at = i * step
        q = jnp.concatenate(
            [jnp.concatenate([q_ref[at + n].astype(f32), one_row], 0).T for n in range(step)], 0
        ).astype(bf16)
        softmax_block(q, kt[...], v[...], o_ref, keep_ref, at, scale)
        return carry

    lax.fori_loop(0, BLOCKS // step, one, 0)


def cross_backward_kernel(
    order_ref, live_ref, q_ref, do_ref, keep_ref, kv_ref, dq_ref, dkv_ref, kt, k, vt, dk_acc, dv_acc, *, scale, step
):
    shape = (HEAD, LIVE_MAX * SLOTS)
    row = lax.broadcasted_iota(jnp.int32, shape, 0)
    kt[HEAD:, :] = jnp.where((row >= 1) & (row < 4), 1.0, 0.0).astype(bf16)
    vt[HEAD:, :] = jnp.where(row < 3, 1.0, 0.0).astype(bf16)
    for t in range(LIVE_MAX):
        cols = slice(t * SLOTS, (t + 1) * SLOTS)
        block = slot_block(kv_ref, order_ref[t])
        kt[:HEAD, cols] = block[:HEAD]
        bias = jnp.where(t < live_ref[0], 0.0, FAR)
        row = lax.broadcasted_iota(jnp.int32, (16, SLOTS), 0)
        ones = jnp.where((row >= 1) & (row < 4), 1.0, 0.0)
        kt[HEAD : HEAD + 16, cols] = jnp.where(row == 0, bias, ones).astype(bf16)
        k[cols, :] = block[:HEAD].T
        vt[:HEAD, cols] = block[HEAD:]
    dk_acc[...] = jnp.zeros_like(dk_acc)
    dv_acc[...] = jnp.zeros_like(dv_acc)

    def one(i, carry):
        at = i * step
        qts = [q_ref[at + n] for n in range(step)]
        dots = [do_ref[at + n] for n in range(step)]
        keeps = [keep_ref[at + n] for n in range(step)]
        dq = backward_block(qts, dots, keeps, kt[...], k[...], vt[...], dk_acc, dv_acc, scale)
        store_blocks(dq_ref, at, slice(0, HEAD), dq)
        return carry

    lax.fori_loop(0, BLOCKS // step, one, 0)
    for t in range(LIVE_MAX):
        cols = slice(t * SLOTS, (t + 1) * SLOTS)
        dkv_ref[own_place(order_ref[t]), :HEAD, :] = dk_acc[:, cols].astype(bf16)
        dkv_ref[own_place(order_ref[t]), HEAD:, :] = dv_acc[:, cols].astype(bf16)
    for t in range(LIVE_MAX, BLOCKS):
        dkv_ref[own_place(order_ref[t])] = jnp.zeros((2 * HEAD, SLOTS), bf16)


def params():
    return pltpu.CompilerParams(vmem_limit_bytes=VMEM_BYTES)


def vmem(count):
    return [pl.BlockSpec(memory_space=pltpu.VMEM)] * count


def smem(count):
    return [pl.BlockSpec(memory_space=pltpu.SMEM)] * count


def cost(keys, products):
    flops = 2 * BLOCKS * TOK * keys * HEAD * products
    return pl.CostEstimate(flops=4 * flops, bytes_accessed=4 << 20, transcendentals=BLOCKS * TOK * keys)


OUT_T = jax.ShapeDtypeStruct((BLOCKS, HEAD, TOK), bf16)
KEEP_T = jax.ShapeDtypeStruct((BLOCKS, HEAD + 8, TOK), f32)


def self_forward(qkv, scale):
    keys = BLOCKS * TOK
    return pl.pallas_call(
        partial(self_forward_kernel, scale=scale, step=2),
        out_shape=(OUT_T, KEEP_T),
        in_specs=vmem(1),
        out_specs=tuple(vmem(2)),
        scratch_shapes=[pltpu.VMEM((HEAD, keys), bf16), pltpu.VMEM((keys, HEAD), bf16)],
        compiler_params=params(),
        cost_estimate=cost(keys, 2),
        name="self_forward",
    )(qkv)


def self_backward(qkv, do, keep, scale):
    keys = BLOCKS * TOK
    return pl.pallas_call(
        partial(self_backward_kernel, scale=scale, step=2),
        out_shape=jax.ShapeDtypeStruct((BLOCKS, 3 * HEAD, TOK), bf16),
        in_specs=vmem(3),
        out_specs=vmem(1)[0],
        scratch_shapes=[
            pltpu.VMEM((2 * HEAD, keys), bf16),
            pltpu.VMEM((keys, HEAD), bf16),
            pltpu.VMEM((2 * HEAD, keys), bf16),
            pltpu.VMEM((HEAD, keys), f32),
            pltpu.VMEM((HEAD, keys), f32),
        ],
        compiler_params=params(),
        cost_estimate=cost(keys, 5),
        name="self_backward",
    )(qkv, do, keep)


def cross_forward(order, live, q, kv, scale):
    keys = LIVE_MAX * SLOTS
    return pl.pallas_call(
        partial(cross_forward_kernel, scale=scale, step=2),
        out_shape=(OUT_T, KEEP_T),
        in_specs=smem(2) + vmem(2),
        out_specs=tuple(vmem(2)),
        scratch_shapes=[pltpu.VMEM((2 * HEAD, keys), bf16), pltpu.VMEM((keys, HEAD), bf16)],
        compiler_params=params(),
        cost_estimate=cost(keys, 2),
        name="cross_forward",
    )(order, live, q, kv)


def cross_backward(order, live, q, do, keep, kv, scale):
    keys = LIVE_MAX * SLOTS
    return pl.pallas_call(
        partial(cross_backward_kernel, scale=scale, step=2),
        out_shape=(OUT_T, jax.ShapeDtypeStruct((BLOCKS, 2 * HEAD, SLOTS), bf16)),
        in_specs=smem(2) + vmem(4),
        out_specs=tuple(vmem(2)),
        scratch_shapes=[
            pltpu.VMEM((2 * HEAD, keys), bf16),
            pltpu.VMEM((keys, HEAD), bf16),
            pltpu.VMEM((2 * HEAD, keys), bf16),
            pltpu.VMEM((HEAD, keys), f32),
            pltpu.VMEM((HEAD, keys), f32),
        ],
        compiler_params=params(),
        cost_estimate=cost(keys, 5),
        name="cross_backward",
    )(order, live, q, do, keep, kv)


def normed(v):
    centred = v - jnp.mean(v, -1, keepdims=True)
    spread = jnp.mean(centred * centred, -1, keepdims=True)
    r = lax.rsqrt(spread + EPS)
    return centred * r, r


def norm_backward(da, xh, r, gain):
    d = da * (1.0 + gain)
    along = jnp.mean(d * xh, -1, keepdims=True)
    return r * (d - jnp.mean(d, -1, keepdims=True) - xh * along)


def token_rows(ref, lo, hi):
    block = ref[:, lo:hi, :]
    return block.reshape(HEADS * (hi - lo), block.shape[2]).T


def store_heads(ref, lo, value):
    turned = value.T.astype(bf16)
    ref[:, lo : lo + HEAD, :] = turned.reshape(HEADS, HEAD, turned.shape[1])


def load_all(pairs, sems):
    copies = [pltpu.make_async_copy(src, dst, sems.at[n]) for n, (src, dst) in enumerate(pairs)]
    for copy in copies:
        copy.start()
    return copies


def enter_kernel(camera_ref, x_ref, cot_ref, mod_ref, wq_any, wk_any, wv_any, sent_ref, acts_ref, gains_ref, wq, wk, wv, sems):
    copies = load_all(((wq_any, wq), (wk_any, wk), (wv_any, wv)), sems)
    row = mod_ref[pl.ds(camera_ref[0], 1), :]
    for n in range(6):
        gains_ref[n : n + 1, :] = row[:, n * WIDTH : (n + 1) * WIDTH]
    gains_ref[6:8, :] = jnp.zeros((2, WIDTH), f32)
    xh, _ = normed(x_ref[...].astype(f32))
    acts_ref[0] = cot_ref[...]
    acts_ref[1] = xh.astype(bf16)
    a1 = (xh * (1.0 + gains_ref[0:1, :]) + gains_ref[1:2, :]).astype(bf16)
    for n, (copy, w) in enumerate(zip(copies, (wq, wk, wv))):
        copy.wait()
        store_heads(sent_ref, n * HEAD, mm(a1, w[...]))


def middle_kernel(o_ref, x_ref, gains_ref, early_ref, wo_any, wcq_any, first_ref, acts_ref, q_ref, wo, wcq, sems):
    copies = load_all(((wo_any, wo), (wcq_any, wcq)), sems)
    o1 = token_rows(o_ref, 0, HEAD)
    acts_ref[0:2] = early_ref[...]
    acts_ref[2] = o1
    copies[0].wait()
    first = x_ref[...].astype(f32) + mm(o1, wo[...])
    first_ref[...] = first
    xh, _ = normed(first)
    a2 = (xh * (1.0 + gains_ref[2:3, :]) + gains_ref[3:4, :]).astype(bf16)
    acts_ref[3] = a2
    copies[1].wait()
    store_heads(q_ref, 0, mm(a2, wcq[...]))


def gelu_both(a3, cot, we, wr):
    u = mm(a3, we)
    square = u * u
    t = jnp.tanh(u * (GELU_A + GELU_A * GELU_B * square))
    h = (0.5 * u * (1.0 + t)).astype(bf16)
    dh = mm(cot, wr, 1, 1).astype(bf16).astype(f32)
    slope = 0.5 * (1.0 + t) + 0.5 * u * (1.0 - t * t) * (GELU_A + 3.0 * GELU_A * GELU_B * square)
    return h, (dh * slope).astype(bf16)


def mlp_kernel(
    oc_ref, first_ref, cot_ref, gains_ref, wco_ref, we_ref, wr_ref,
    out_ref, back_ref, acts_ref, do_ref, dgb_ref, a3, second, y, da3,
):
    step = pl.program_id(0)

    @pl.when(step == 0)
    def _():
        total = first_ref[...] + mm(token_rows(oc_ref, 0, HEAD), wco_ref[...])
        second[...] = total
        xh, _ = normed(total)
        a3[...] = (xh * (1.0 + gains_ref[4:5, :]) + gains_ref[5:6, :]).astype(bf16)
        y[...] = jnp.zeros_like(y)
        da3[...] = jnp.zeros_like(da3)

    h, du = gelu_both(a3[...], cot_ref[...], we_ref[...], wr_ref[...])
    y[...] += mm(h, wr_ref[...])
    da3[...] += mm(du, we_ref[...], 1, 1)

    @pl.when(step == pl.num_programs(0) - 1)
    def _():
        total = second[...]
        out_ref[...] = total + y[...]
        xh, r = normed(total)
        d = da3[...]
        dgb_ref[...] = jnp.zeros_like(dgb_ref)
        dgb_ref[0:1, :] = jnp.sum(d * xh, 0, keepdims=True)
        dgb_ref[1:2, :] = jnp.sum(d, 0, keepdims=True)
        back = cot_ref[...].astype(f32) + norm_backward(d, xh, r, gains_ref[4:5, :])
        back_ref[...] = back
        dy2 = back.astype(bf16)
        acts_ref[0] = a3[...]
        acts_ref[1] = dy2
        store_heads(do_ref, 0, mm(dy2, wco_ref[...], 1, 1))


def return_kernel(dq_ref, first_ref, second_back_ref, gains_ref, wcq_any, wo_any, back_ref, sent_ref, dgb_ref, wcq, wo, sems):
    copies = load_all(((wcq_any, wcq), (wo_any, wo)), sems)
    xh, r = normed(first_ref[...])
    dq = token_rows(dq_ref, 0, HEAD)
    copies[0].wait()
    da2 = mm(dq, wcq[...], 1, 1)
    dgb_ref[...] = jnp.zeros_like(dgb_ref)
    dgb_ref[0:1, :] = jnp.sum(da2 * xh, 0, keepdims=True)
    dgb_ref[1:2, :] = jnp.sum(da2, 0, keepdims=True)
    back = second_back_ref[...] + norm_backward(da2, xh, r, gains_ref[2:3, :])
    back_ref[...] = back
    dy1 = back.astype(bf16)
    store_heads(sent_ref, HEAD, back)
    copies[1].wait()
    store_heads(sent_ref, 0, mm(dy1, wo[...], 1, 1))


def leave_kernel(got_ref, x_ref, back_ref, gains_ref, wq_any, wk_any, wv_any, out_ref, camera_ref, wq, wk, wv, sems):
    copies = load_all(((wq_any, wq), (wk_any, wk), (wv_any, wv)), sems)
    lines = got_ref[0, 3 * HEAD :, :].astype(f32)
    for n in range(1, BLOCKS):
        lines += got_ref[n, 3 * HEAD :, :].astype(f32)
    camera_ref[...] = lines[:16] + lines[16:]
    xh, r = normed(x_ref[...].astype(f32))
    da1 = jnp.zeros(out_ref.shape, f32)
    for n, (copy, w) in enumerate(zip(copies, (wq, wk, wv))):
        copy.wait()
        da1 += mm(token_rows(got_ref, n * HEAD, (n + 1) * HEAD), w[...], 1, 1)
    out_ref[...] = back_ref[...] + norm_backward(da1, xh, r, gains_ref[0:1, :])


def patches_kernel(got_ref, wk_ref, wv_ref, out_ref):
    dk = token_rows(got_ref, 0, HEAD)
    dv = token_rows(got_ref, HEAD, 2 * HEAD)
    out_ref[...] = mm(dk, wk_ref[...], 1, 1) + mm(dv, wv_ref[...], 1, 1)


def side_by_side(ref, lo, hi):
    return jnp.concatenate([ref[n, lo:hi, :] for n in range(ref.shape[0])], 1)


def one_above_other(ref):
    block = ref[...]
    return block.reshape(-1, block.shape[-1])


def store_columns(ref, at, grad_t):
    columns, rows = grad_t.shape[0] // 2, grad_t.shape[1] // 4
    for e in range(2):
        for v in range(4):
            piece = grad_t[e * columns : (e + 1) * columns, v * rows : (v + 1) * rows]
            if rows < 256:
                piece = jnp.concatenate([piece, jnp.zeros((columns, 256 - rows), f32)], 1)
            ref[e * 4 + v, at : at + columns, :] = piece.astype(bf16)


def add_up(step, accs, terms):
    @pl.when(step == 0)
    def _():
        for acc, term in zip(accs, terms):
            acc[...] = term

    @pl.when(step > 0)
    def _():
        for acc, term in zip(accs, terms):
            acc[...] += term


def cross_grads_kernel(dqc_ref, a2_ref, dkv_ref, patches_ref, col_ref, q_acc, kv_acc):
    step = pl.program_id(0)
    q = mm(side_by_side(dqc_ref, 0, HEAD), one_above_other(a2_ref))
    kv = mm(side_by_side(dkv_ref, 0, 2 * HEAD), one_above_other(patches_ref))
    add_up(step, (q_acc, kv_acc), (q, kv))

    @pl.when(step == pl.num_programs(0) - 1)
    def _():
        store_columns(col_ref, 0, q_acc[...])
        store_columns(col_ref, 32, kv_acc[:HEAD, :])
        store_columns(col_ref, 64, kv_acc[HEAD:, :])


def hidden_grads_kernel(
    head_ref, cot_ref, o1_ref, a3_ref, dy2_ref, do_ref, oc_ref, we_ref, wr_ref, col_ref, row_ref, e_acc, r_acc, o_acc, oc_acc
):
    step = pl.program_id(0)
    a3, cot = one_above_other(a3_ref), one_above_other(cot_ref)
    h, du = gelu_both(a3, cot, we_ref[...], wr_ref[...])
    e = mm(du.T, a3)
    r = mm(h.T, cot)
    o = mm(side_by_side(do_ref, HEAD, 2 * HEAD), one_above_other(o1_ref))
    oc = mm(side_by_side(oc_ref, 0, HEAD), one_above_other(dy2_ref))
    add_up(step, (e_acc, r_acc, o_acc, oc_acc), (e, r, o, oc))

    @pl.when(step == pl.num_programs(0) - 1)
    def _():
        store_columns(col_ref, 0, o_acc[...])
        store_columns(col_ref, 32, e_acc[...])
        rows = jnp.concatenate([r_acc[...], oc_acc[...], jnp.zeros((HEAD, WIDTH), f32)], 0)
        row_ref[...] = rows.T.astype(bf16).reshape(row_ref.shape)


def late_kernel(dqkv_ref, xh_ref, wt_ref, gains_ref, dgb2_ref, dgb3_ref, col_ref, sent_ref, qkv_acc, sums):
    step = pl.program_id(0)
    turned = side_by_side(dqkv_ref, 0, 3 * HEAD)
    qkv = mm(turned, one_above_other(xh_ref))
    total = jnp.broadcast_to(jnp.sum(turned.astype(f32), 1, keepdims=True), sums.shape)
    add_up(step, (qkv_acc, sums), (qkv, total))
    blocks = dqkv_ref.shape[0]
    for n in range(blocks):
        sent_ref[step * blocks + n, : 3 * HEAD, :] = dqkv_ref[n]

    @pl.when(step == pl.num_programs(0) - 1)
    def _():
        moment = qkv_acc[...]
        count = sums[:, 0:1]
        weights = wt_ref[...].astype(f32)
        grad = moment * (1.0 + gains_ref[0:1, :]) + count * gains_ref[1:2, :]
        for n in range(3):
            store_columns(col_ref, n * 32, grad[n * HEAD : (n + 1) * HEAD])
        dg1 = jnp.sum(weights * moment, 0, keepdims=True)
        db1 = jnp.sum(weights * count, 0, keepdims=True)
        flat = jnp.concatenate([dg1, db1] + [ref[n : n + 1, :] for ref in (dgb2_ref, dgb3_ref) for n in range(2)], 1)
        chunk = flat.shape[1] // 32
        fill = jnp.zeros((1, 2 * TOK - chunk), f32)
        for b in range(4):
            lines = []
            for i in range(8):
                at = (i * 4 + b) * chunk
                line = jnp.concatenate([flat[:, at : at + chunk], fill], 1)
                lines += [line[:, :TOK], line[:, TOK:]]
            lines = jnp.concatenate(lines, 0)
            high = lines.astype(bf16)
            both = jnp.concatenate([high, (lines - high.astype(f32)).astype(bf16)], 0)
            for v in range(4):
                sent_ref[v * 4 + b, 3 * HEAD :, :] = both


def add_items_kernel(got_ref, out_ref):
    total = got_ref[0].astype(f32)
    for n in range(1, 8):
        total += got_ref[n].astype(f32)
    out_ref[...] = total


def finish_columns_kernel(in_ref, *out_refs):
    at = 0
    for ref in out_refs[:-1]:
        columns, rows = ref.shape
        ref[...] = in_ref[at : at + columns, :rows]
        at += columns
    out_refs[-1][...] = in_ref[at:, :].T


def finish_rows_kernel(camera_ref, view_ref, got_ref, r_ref, oc_ref, modulation_ref):
    units = r_ref.shape[1] // 4
    for s in range(4):
        total = got_ref[s].astype(f32)
        for n in range(1, 8):
            total += got_ref[n * 4 + s].astype(f32)
        r_ref[:, s * units : (s + 1) * units] = total[:, :units]
        oc_ref[:, s * HEAD : (s + 1) * HEAD] = total[:, units : units + HEAD]
    rows = [jnp.zeros((16, HEAD), f32) for _ in range(4)]
    for n in range(8):
        part = sum(got_ref[n * 4 + s, 0:16, units + HEAD : units + 2 * HEAD].astype(f32) for s in range(4))
        for k in range(4):
            rows[k] += jnp.where(camera_ref[n] == view_ref[0] * 4 + k, part, 0.0)
    for k in range(4):
        for n in range(3):
            modulation_ref[k : k + 1, n * HEAD : (n + 1) * HEAD] = rows[k][n : n + 1] + rows[k][n + 3 : n + 4]


WIDTH = 1024
HIDDEN = 4096
PATCH = 768
UNITS = HIDDEN // BLOCKS
GELU_A = 0.7978845608028654
GELU_B = 0.044715


def shaped(*shape, dtype=bf16):
    return jax.ShapeDtypeStruct(shape, dtype)


ANY = pl.BlockSpec(memory_space=pl.ANY)
V = pl.BlockSpec(memory_space=pltpu.VMEM)
S = pl.BlockSpec(memory_space=pltpu.SMEM)
MB = 1 << 20


def weight(rows=WIDTH, columns=WIDTH):
    return pltpu.VMEM((rows, columns), bf16)


def call(kernel, name, ins, outs, scratch, flops, traffic):
    return pl.pallas_call(
        kernel,
        out_shape=outs,
        in_specs=ins,
        out_specs=jax.tree.map(lambda _: V, outs),
        scratch_shapes=scratch,
        compiler_params=pltpu.CompilerParams(vmem_limit_bytes=VMEM_BYTES),
        cost_estimate=pl.CostEstimate(flops=flops, bytes_accessed=traffic, transcendentals=0),
        name=name,
    )


TOKENS_F32 = shaped(TOK, WIDTH, dtype=f32)
TOKENS_BF16 = shaped(TOK, WIDTH)
ROWS_F32 = shaped(8, WIDTH, dtype=f32)
SQUARE = 2 * TOK * WIDTH * WIDTH


def enter(*args):
    return call(
        enter_kernel, "enter", [S, V, V, V, ANY, ANY, ANY],
        (shaped(BLOCKS, 3 * HEAD, TOK), shaped(2, TOK, WIDTH), ROWS_F32),
        [weight(), weight(), weight(), pltpu.SemaphoreType.DMA((3,))], 3 * SQUARE, 8 * MB,
    )(*args)


def middle(*args):
    return call(
        middle_kernel, "middle", [V, V, V, V, ANY, ANY], (TOKENS_F32, shaped(4, TOK, WIDTH), OUT_T),
        [weight(), weight(), pltpu.SemaphoreType.DMA((2,))], 2 * SQUARE, 6 * MB,
    )(*args)


def mlp(*args):
    steps = 8
    width = HIDDEN // steps
    whole = lambda *shape: pl.BlockSpec(shape, lambda i: (0,) * len(shape))
    outs = (TOKENS_F32, TOKENS_F32, shaped(2, TOK, WIDTH), OUT_T, ROWS_F32)
    out_specs = tuple(whole(*o.shape) for o in outs)
    tokens = whole(TOK, WIDTH)
    return pl.pallas_call(
        mlp_kernel,
        grid=(steps,),
        out_shape=outs,
        in_specs=[
            whole(BLOCKS, HEAD, TOK), tokens, tokens, whole(8, WIDTH), whole(WIDTH, WIDTH),
            pl.BlockSpec((WIDTH, width), lambda i: (0, i)), pl.BlockSpec((width, WIDTH), lambda i: (i, 0)),
        ],
        out_specs=out_specs,
        scratch_shapes=[
            pltpu.VMEM((TOK, WIDTH), bf16), pltpu.VMEM((TOK, WIDTH), f32),
            pltpu.VMEM((TOK, WIDTH), f32), pltpu.VMEM((TOK, WIDTH), f32),
        ],
        compiler_params=pltpu.CompilerParams(vmem_limit_bytes=VMEM_BYTES),
        cost_estimate=pl.CostEstimate(flops=18 * SQUARE, bytes_accessed=22 * MB, transcendentals=TOK * HIDDEN),
        name="mlp",
    )(*args)


def returned(*args):
    return call(
        return_kernel, "returned", [V, V, V, V, ANY, ANY], (TOKENS_F32, shaped(BLOCKS, 2 * HEAD, TOK), ROWS_F32),
        [weight(), weight(), pltpu.SemaphoreType.DMA((2,))], 2 * SQUARE, 6 * MB,
    )(*args)


def leave(*args):
    return call(
        leave_kernel, "leave", [V, V, V, V, ANY, ANY, ANY], (TOKENS_F32, shaped(16, TOK, dtype=f32)),
        [weight(), weight(), weight(), pltpu.SemaphoreType.DMA((3,))], 3 * SQUARE, 8 * MB,
    )(*args)


def patches_back(*args):
    return call(
        patches_kernel, "patches_back", [V, V, V], shaped(SLOTS, PATCH, dtype=f32), [], 3 * SQUARE, 5 * MB
    )(*args)


STEPS = 4


def blocks_of(*shape):
    return pl.BlockSpec((BLOCKS // STEPS,) + shape, lambda i: (i,) + (0,) * len(shape))


def gathered(*shape, at=None):
    plane = () if at is None else (at,)
    return pl.BlockSpec((4, 1) + (1,) * len(plane) + shape, lambda i: (0, i) + plane + (0,) * len(shape))


def whole_block(*shape):
    return pl.BlockSpec(shape, lambda i: (0,) * len(shape))


def cross_grads(dqc, acts, dkv, patches_all):
    out = shaped(8, 96, 256)
    return pl.pallas_call(
        cross_grads_kernel,
        grid=(STEPS,),
        out_shape=out,
        in_specs=[blocks_of(HEAD, TOK), gathered(TOK, WIDTH, at=3), blocks_of(2 * HEAD, SLOTS), gathered(SLOTS, PATCH)],
        out_specs=whole_block(*out.shape),
        scratch_shapes=[pltpu.VMEM((HEAD, WIDTH), f32), pltpu.VMEM((2 * HEAD, PATCH), f32)],
        compiler_params=pltpu.CompilerParams(vmem_limit_bytes=VMEM_BYTES),
        cost_estimate=pl.CostEstimate(flops=6 * SQUARE, bytes_accessed=12 * MB, transcendentals=0),
        name="cross_grads",
    )(dqc, acts, dkv, patches_all)


def hidden_grads(head, acts, late_acts, do1, oc_t, expand_weight, reduce_weight):
    outs = (shaped(8, 160, 256), shaped(32, 32, UNITS + 2 * HEAD))
    by_head = lambda spec: pl.BlockSpec(spec.block_shape, lambda i, head: spec.index_map(i))
    ins = [
        gathered(TOK, WIDTH, at=0), gathered(TOK, WIDTH, at=2), gathered(TOK, WIDTH, at=0),
        gathered(TOK, WIDTH, at=1), blocks_of(2 * HEAD, TOK), blocks_of(HEAD, TOK),
    ]
    own = [
        pl.BlockSpec((WIDTH, UNITS), lambda i, head: (0, head[0])),
        pl.BlockSpec((UNITS, WIDTH), lambda i, head: (head[0], 0)),
    ]
    return pl.pallas_call(
        hidden_grads_kernel,
        grid_spec=pltpu.PrefetchScalarGridSpec(
            num_scalar_prefetch=1,
            grid=(STEPS,),
            in_specs=[by_head(spec) for spec in ins] + own,
            out_specs=tuple(by_head(whole_block(*o.shape)) for o in outs),
            scratch_shapes=[
                pltpu.VMEM((UNITS, WIDTH), f32), pltpu.VMEM((UNITS, WIDTH), f32),
                pltpu.VMEM((HEAD, WIDTH), f32), pltpu.VMEM((HEAD, WIDTH), f32),
            ],
        ),
        out_shape=outs,
        compiler_params=pltpu.CompilerParams(vmem_limit_bytes=VMEM_BYTES),
        cost_estimate=pl.CostEstimate(flops=20 * SQUARE, bytes_accessed=20 * MB, transcendentals=0),
        name="hidden_grads",
    )(head, acts, acts, late_acts, late_acts, do1, oc_t, expand_weight, reduce_weight)


def late_grads(dqkv, acts, weights_t, gains, dgb2, dgb3):
    outs = (shaped(8, 96, 256), shaped(BLOCKS, 3 * HEAD + 32, TOK))
    return pl.pallas_call(
        late_kernel,
        grid=(STEPS,),
        out_shape=outs,
        in_specs=[blocks_of(3 * HEAD, TOK), gathered(TOK, WIDTH, at=1), whole_block(3 * HEAD, WIDTH)]
        + [whole_block(8, WIDTH)] * 3,
        out_specs=tuple(whole_block(*o.shape) for o in outs),
        scratch_shapes=[pltpu.VMEM((3 * HEAD, WIDTH), f32), pltpu.VMEM((3 * HEAD, TOK), f32)],
        compiler_params=pltpu.CompilerParams(vmem_limit_bytes=VMEM_BYTES),
        cost_estimate=pl.CostEstimate(flops=4 * SQUARE, bytes_accessed=6 * MB, transcendentals=0),
        name="late_grads",
    )(dqkv, acts, weights_t, gains, dgb2, dgb3)


def add_items(got):
    return call(add_items_kernel, "add_items", [V], shaped(*got.shape[1:], dtype=f32), [], MB, 2 * MB)(got)


def finish_columns(summed):
    small = [(32, 256)] * 4 + [(32, 192)] * 2 + [(32, 256), (256, 128)]
    outs = tuple(shaped(*shape, dtype=f32) for shape in small)
    return call(finish_columns_kernel, "finish_columns", [V], outs, [], MB, MB)(summed)


def finish_rows(camera_ids, view, got):
    outs = (shaped(32, HIDDEN // 4, dtype=f32), shaped(32, 256, dtype=f32), shaped(4, 192, dtype=f32))
    return call(finish_rows_kernel, "finish_rows", [S, S, V], outs, [], MB, 2 * MB)(camera_ids, view, got)


def home_route():
    size = dict(zip(AXES, SIZES))
    place = lambda at: sum(at[a] * s for a, s in zip(AXES, (64, 32, 8, 4, 2, 1)))
    route = []
    for spot in every(*[range(size[a]) for a in AXES]):
        at = dict(zip(AXES, spot))
        p = at["x"] * 2 + at["zh"]
        to = dict(x=at["yh"] * 2 + at["c"], zh=at["zl"], zl=at["yl"], yl=p >> 2, yh=p >> 1 & 1, c=p & 1)
        route.append((place(at), place(to)))
    return route


def on_device(
    tokens, patches, patch_counts, camera_ids, modulation, query_weight, key_weight, value_weight, output_weight,
    cross_query, cross_key, cross_value, cross_output, expand_weight, reduce_weight, cotangent,
):
    scale = HEAD**-0.5
    item = lax.axis_index(ITEMS)
    head = lax.axis_index(ITEM)
    view = lax.axis_index(VIEW)
    camera = lax.dynamic_slice_in_dim(camera_ids, item, 1, 0)
    counts = lax.dynamic_index_in_dim(patch_counts, item, 0, keepdims=False)
    gather = lambda block: lax.all_gather(block, GATHER, axis=0, tiled=False).reshape((4, 4) + block.shape)

    x = tokens[0, 0]
    grad_out = cotangent[0, 0]
    patches_all = gather(patches[0, 0])

    live = (jnp.arange(4)[:, None] * SLOTS < counts[None, :]).reshape(BLOCKS)
    n_live = jnp.sum(live.astype(jnp.int32))
    rank = jnp.where(live, jnp.cumsum(live) - 1, n_live + jnp.cumsum(~live) - 1)
    slot = jnp.arange(BLOCKS)
    order = jnp.sum(jnp.where(rank[None, :] == slot[:, None], slot[None, :], 0), 1).astype(jnp.int32)
    n_live = n_live.reshape(1)
    own_columns = lambda w: lax.dynamic_slice_in_dim(w, head * HEAD, HEAD, 1)
    kv_weight = jnp.concatenate([own_columns(cross_key), own_columns(cross_value)], 1)
    weights_t = jnp.concatenate([own_columns(w).T for w in (query_weight, key_weight, value_weight)], 0)

    after = lambda value, *others: lax.optimization_barrier((value,) + others)[0]
    sent, first_acts, gains = enter(camera, x, grad_out, modulation, query_weight, key_weight, value_weight)
    qkv, kv_weight, weights_t, order, n_live = lax.optimization_barrier(
        (swap(sent, ITEM), kv_weight, weights_t, order, n_live)
    )
    o_t, keep_self = self_forward(qkv, scale)
    first_sum, acts, sent = middle(swap(o_t, ITEM), x, gains, first_acts, output_weight, cross_query)
    qc = swap(sent, ITEM)
    acts = gather(acts)
    kv = mm(kv_weight, patches_all.reshape(BLOCKS * SLOTS, -1), 0, 1).astype(bf16)
    oc_t, keep_cross = cross_forward(order, n_live, qc, kv, scale)
    layer_out, d_second, late_acts, sent, dgb3 = mlp(
        swap(oc_t, ITEM), first_sum, grad_out, gains, cross_output, expand_weight, reduce_weight
    )
    do_c = swap(sent, ITEM)
    late_acts = gather(late_acts)
    dqc, dkv = cross_backward(order, n_live, qc, do_c, keep_cross, kv, scale)
    d_first, sent, dgb2 = returned(swap(dqc, ITEM), first_sum, d_second, gains, cross_query, output_weight)
    do1, col_cross = lax.optimization_barrier((swap(sent, ITEM), cross_grads(dqc, acts, dkv, patches_all)))
    dkv_got = swap(after(dkv, do1), ITEM)
    dqkv = self_backward(qkv, do1, keep_self, scale)
    col_late, sent = late_grads(dqkv, acts, weights_t, gains, dgb2, dgb3)
    sent, dkv_got = lax.optimization_barrier((sent, dkv_got))
    col_hidden, row = hidden_grads(
        head.reshape(1), acts, late_acts, after(do1, sent), oc_t, expand_weight, reduce_weight
    )
    got, col_hidden, row = lax.optimization_barrier((swap(sent, ITEM), col_hidden, row))
    columns = swap(jnp.concatenate([col_late, col_cross, col_hidden], 1), ITEMS)
    tokens_grad, camera_sum = leave(got, x, d_first, gains, query_weight, key_weight, value_weight)
    patches_grad = patches_back(dkv_got, cross_key, cross_value)

    camera_sum = camera_sum.reshape(8, -1)[:, : 3 * HEAD]
    high = camera_sum.astype(bf16)
    low = (camera_sum - high.astype(f32)).astype(bf16)
    lines = jnp.concatenate([high.reshape(8, 3, HEAD), low.reshape(8, 3, HEAD)], 1)
    mine = jnp.arange(4) == lax.axis_index(("zl", "yl"))
    lines = jnp.where(mine[None, :, None, None], lines[:, None], 0).astype(bf16).reshape(32, 6, HEAD)
    row = row + jnp.pad(lines, ((0, 0), (0, 26), (UNITS + HEAD, 0)))

    columns, row = lax.optimization_barrier((columns, row))
    rows = swap(row, ROW)
    summed = lax.ppermute(add_items(columns), AXES, home_route())
    *turned, e_grad = finish_columns(summed)
    q_grad, k_grad, v_grad, cq_grad, ck_grad, cv_grad, o_grad = (grad.T for grad in turned)
    r_grad, co_grad, modulation_grad = finish_rows(camera_ids, view.reshape(1), rows)
    return (
        layer_out[None, None],
        tokens_grad[None, None],
        patches_grad[None, None],
        modulation_grad,
        q_grad,
        k_grad,
        v_grad,
        o_grad,
        cq_grad,
        ck_grad,
        cv_grad,
        co_grad.T,
        e_grad,
        r_grad.T,
    )


def solution(mesh):
    fine = Mesh(mesh.devices.reshape(SIZES), AXES)
    split = P(ROW, VIEW, None, None)
    grads = P(VIEW, ROW)
    return jax.shard_map(
        on_device,
        mesh=fine,
        in_specs=(split, split) + (P(),) * 13 + (split,),
        out_specs=(split,) * 3 + (grads,) * 11,
        check_vma=False,
    )
```

```python
from functools import partial
from itertools import product as every

import jax
import jax.numpy as jnp
from jax import lax
from jax.experimental import pallas as pl
from jax.experimental.pallas import tpu as pltpu
from jax.sharding import Mesh
from jax.sharding import PartitionSpec as P

HEADS = 16
HEAD = 64
TOK = 128
SLOTS = 256
BLOCKS = 16
LIVE_MAX = 13
EPS = 1e-05
LOG2E = 1.4426950408889634
FAR = -1e30

AXES = ("yh", "c", "x", "zh", "zl", "yl")
SIZES = (2, 2, 4, 2, 2, 2)
VIEW = ("yh", "c")
ROW = ("x", "zh", "zl", "yl")
ITEM = ("yh", "c", "zl", "yl")
ITEMS = ("x", "zh")
GATHER = ("zl", "yl", "yh", "c")
VMEM_BYTES = 60 * 1024 * 1024

bf16 = jnp.bfloat16
f32 = jnp.float32


def mm(left, right, lc=1, rc=0):
    return lax.dot_general(left, right, (((lc,), (rc,)), ((), ())), preferred_element_type=f32)


def swap(block, axes):
    return lax.all_to_all(block, axes, 0, 0, tiled=True)


def three_parts(row):
    high = row.astype(bf16)
    rest = row - high.astype(f32)
    middle = rest.astype(bf16)
    low = (rest - middle.astype(f32)).astype(bf16)
    return high, middle, low


CHAINS, ROWS = 8, 2
BACK_CHAINS, BACK_ROWS = 8, 1
DEPTH = 3 * HEAD


def scaled(turned, factor):
    value = turned.astype(f32) * factor
    high = value.astype(bf16)
    low = value - high.astype(f32)
    return jnp.concatenate([high.astype(f32), low], 0)


def softmax_block(q, kt, v, o_ref, keep_ref, at):
    s = mm(q, kt)
    m = jnp.max(s, 1, keepdims=True)
    p = jnp.exp2(s - m)
    o = mm(p.astype(bf16), v)
    total = o[:, HEAD : HEAD + 1]
    o = o[:, :HEAD] / total
    lse = m + jnp.log2(total)
    packed = jnp.concatenate([o, jnp.broadcast_to(lse, o.shape)], 1).T
    for part in range(packed.shape[1] // TOK):
        piece = packed[:, part * TOK : (part + 1) * TOK]
        o_ref[at + part] = piece[:HEAD].astype(bf16)
        keep_ref[at + part] = piece[: HEAD + 8]


def backward_block(qts, dots, keeps, kt, k, vt, dk_acc, dv_acc, scale):
    q_rows, do_rows = [], []
    for qt, dot, keep in zip(qts, dots, keeps):
        lse = keep[HEAD : HEAD + 1]
        delta = jnp.sum(dot.astype(f32) * keep[:HEAD], 0, keepdims=True) * scale
        one = jnp.ones_like(lse)
        zero = jnp.zeros((HEAD - 4, TOK), f32)
        parts = [part.astype(f32) for part in three_parts(-lse)]
        q_rows.append(jnp.concatenate([scaled(qt, scale * LOG2E), one] + parts + [zero], 0))
        parts = [part.astype(f32) for part in three_parts(-delta)]
        do_rows.append(jnp.concatenate([dot.astype(f32) * scale] + parts + [0.0 * one, zero], 0))
    q = jnp.concatenate([rows.T for rows in q_rows], 0).astype(bf16)
    do = jnp.concatenate([rows.T for rows in do_rows], 0).astype(bf16)
    p = jnp.exp2(mm(q, kt))
    ds = (p * mm(do, vt)).astype(bf16)
    dq = mm(ds, k)
    dk_acc[...] += mm(jnp.concatenate(qts, 1), ds)
    dv_acc[...] += mm(jnp.concatenate(dots, 1), p.astype(bf16))
    return dq[:, :HEAD]


def store_blocks(ref, at, rows, value):
    turned = value.T
    for part in range(turned.shape[1] // TOK):
        ref[at + part, rows, :] = turned[:, part * TOK : (part + 1) * TOK].astype(ref.dtype)


def with_ones(rows):
    ones = jnp.where(lax.broadcasted_iota(jnp.int32, rows.shape, 1) == 0, 1.0, 0.0).astype(bf16)
    return jnp.concatenate([rows, ones], 1)


def self_forward_kernel(qkv_ref, o_ref, keep_ref, kt, v, *, scale):
    for j in range(BLOCKS):
        cols = slice(j * TOK, (j + 1) * TOK)
        kt[:HEAD, cols] = qkv_ref[j, HEAD : 2 * HEAD, :]
        kt[HEAD:, cols] = qkv_ref[j, HEAD : 2 * HEAD, :]
        v[cols, :] = with_ones(qkv_ref[j, 2 * HEAD :, :].T)

    def one(i, carry):
        for c in range(CHAINS):
            at = (i * CHAINS + c) * ROWS
            q = jnp.concatenate([scaled(qkv_ref[at + n, :HEAD, :], scale * LOG2E).T for n in range(ROWS)], 0).astype(bf16)
            softmax_block(q, kt[...], v[...], o_ref, keep_ref, at)
        return carry

    lax.fori_loop(0, BLOCKS // (ROWS * CHAINS), one, 0)


def self_backward_kernel(qkv_ref, do_ref, keep_ref, out_ref, kt, k, vt, dk_acc, dv_acc, *, scale):
    row = lax.broadcasted_iota(jnp.int32, (HEAD, BLOCKS * TOK), 0)
    kt[2 * HEAD :, :] = jnp.where((row >= 1) & (row < 4), 1.0, 0.0).astype(bf16)
    vt[HEAD:, :] = jnp.where(row < 3, 1.0, 0.0).astype(bf16)
    for j in range(BLOCKS):
        cols = slice(j * TOK, (j + 1) * TOK)
        kt[:HEAD, cols] = qkv_ref[j, HEAD : 2 * HEAD, :]
        kt[HEAD : 2 * HEAD, cols] = qkv_ref[j, HEAD : 2 * HEAD, :]
        k[cols, :] = kt[: 2 * HEAD, cols].T
        vt[:HEAD, cols] = qkv_ref[j, 2 * HEAD :, :]
    dk_acc[...] = jnp.zeros_like(dk_acc)
    dv_acc[...] = jnp.zeros_like(dv_acc)

    def one(i, carry):
        for c in range(BACK_CHAINS):
            at = (i * BACK_CHAINS + c) * BACK_ROWS
            qts = [qkv_ref[at + n, :HEAD, :] for n in range(BACK_ROWS)]
            dots = [do_ref[at + n, :HEAD, :] for n in range(BACK_ROWS)]
            keeps = [keep_ref[at + n] for n in range(BACK_ROWS)]
            dq = backward_block(qts, dots, keeps, kt[...], k[...], vt[...], dk_acc, dv_acc, scale)
            store_blocks(out_ref, at, slice(0, HEAD), dq)
        return carry

    lax.fori_loop(0, BLOCKS // (BACK_CHAINS * BACK_ROWS), one, 0)
    for j in range(BLOCKS):
        cols = slice(j * TOK, (j + 1) * TOK)
        out_ref[j, HEAD : 2 * HEAD, :] = dk_acc[:, cols].astype(bf16)
        out_ref[j, 2 * HEAD :, :] = dv_acc[:, cols].astype(bf16)


def slot_block(kv_ref, index):
    return kv_ref[:, pl.ds(pl.multiple_of(index * SLOTS, SLOTS), SLOTS)]


def own_place(index):
    return (index % 4) * 4 + index // 4


def cross_forward_kernel(order_ref, live_ref, q_ref, kv_ref, o_ref, keep_ref, kt, v, *, scale):
    for t in range(LIVE_MAX):
        cols = slice(t * SLOTS, (t + 1) * SLOTS)
        block = slot_block(kv_ref, order_ref[t])
        kt[:HEAD, cols] = block[:HEAD]
        kt[HEAD : 2 * HEAD, cols] = block[:HEAD]
        bias = jnp.where(t < live_ref[0], 0.0, FAR)
        row = lax.broadcasted_iota(jnp.int32, (HEAD, SLOTS), 0)
        kt[2 * HEAD :, cols] = jnp.where(row == 0, bias, 0.0).astype(bf16)
        v[cols, :] = with_ones(block[HEAD:].T)
    one_row = jnp.where(lax.broadcasted_iota(jnp.int32, (HEAD, TOK), 0) == 0, 1.0, 0.0)

    def one(i, carry):
        for c in range(CHAINS):
            at = (i * CHAINS + c) * ROWS
            q = jnp.concatenate(
                [jnp.concatenate([scaled(q_ref[at + n], scale * LOG2E), one_row], 0).T for n in range(ROWS)], 0
            ).astype(bf16)
            softmax_block(q, kt[...], v[...], o_ref, keep_ref, at)
        return carry

    lax.fori_loop(0, BLOCKS // (ROWS * CHAINS), one, 0)


def cross_backward_kernel(
    order_ref, live_ref, q_ref, do_ref, keep_ref, kv_ref, dq_ref, dkv_ref, kt, k, vt, dk_acc, dv_acc, *, scale
):
    shape = (HEAD, LIVE_MAX * SLOTS)
    row = lax.broadcasted_iota(jnp.int32, shape, 0)
    vt[HEAD:, :] = jnp.where(row < 3, 1.0, 0.0).astype(bf16)
    for t in range(LIVE_MAX):
        cols = slice(t * SLOTS, (t + 1) * SLOTS)
        block = slot_block(kv_ref, order_ref[t])
        kt[:HEAD, cols] = block[:HEAD]
        kt[HEAD : 2 * HEAD, cols] = block[:HEAD]
        bias = jnp.where(t < live_ref[0], 0.0, FAR)
        row = lax.broadcasted_iota(jnp.int32, (HEAD, SLOTS), 0)
        ones = jnp.where((row >= 1) & (row < 4), 1.0, 0.0)
        kt[2 * HEAD :, cols] = jnp.where(row == 0, bias, ones).astype(bf16)
        k[cols, :] = kt[: 2 * HEAD, cols].T
        vt[:HEAD, cols] = block[HEAD:]
    dk_acc[...] = jnp.zeros_like(dk_acc)
    dv_acc[...] = jnp.zeros_like(dv_acc)

    def one(i, carry):
        for c in range(BACK_CHAINS):
            at = (i * BACK_CHAINS + c) * BACK_ROWS
            qts = [q_ref[at + n] for n in range(BACK_ROWS)]
            dots = [do_ref[at + n] for n in range(BACK_ROWS)]
            keeps = [keep_ref[at + n] for n in range(BACK_ROWS)]
            dq = backward_block(qts, dots, keeps, kt[...], k[...], vt[...], dk_acc, dv_acc, scale)
            store_blocks(dq_ref, at, slice(0, HEAD), dq)
        return carry

    lax.fori_loop(0, BLOCKS // (BACK_CHAINS * BACK_ROWS), one, 0)
    for t in range(LIVE_MAX):
        cols = slice(t * SLOTS, (t + 1) * SLOTS)
        dkv_ref[own_place(order_ref[t]), :HEAD, :] = dk_acc[:, cols].astype(bf16)
        dkv_ref[own_place(order_ref[t]), HEAD:, :] = dv_acc[:, cols].astype(bf16)
    for t in range(LIVE_MAX, BLOCKS):
        dkv_ref[own_place(order_ref[t])] = jnp.zeros((2 * HEAD, SLOTS), bf16)


def params():
    return pltpu.CompilerParams(vmem_limit_bytes=VMEM_BYTES)


def vmem(count):
    return [pl.BlockSpec(memory_space=pltpu.VMEM)] * count


def smem(count):
    return [pl.BlockSpec(memory_space=pltpu.SMEM)] * count


def cost(keys, products):
    flops = 2 * BLOCKS * TOK * keys * HEAD * products
    return pl.CostEstimate(flops=4 * flops, bytes_accessed=4 << 20, transcendentals=BLOCKS * TOK * keys)


OUT_T = jax.ShapeDtypeStruct((BLOCKS, HEAD, TOK), bf16)
KEEP_T = jax.ShapeDtypeStruct((BLOCKS, HEAD + 8, TOK), f32)


def self_forward(qkv, scale):
    keys = BLOCKS * TOK
    return pl.pallas_call(
        partial(self_forward_kernel, scale=scale),
        out_shape=(OUT_T, KEEP_T),
        in_specs=vmem(1),
        out_specs=tuple(vmem(2)),
        scratch_shapes=[pltpu.VMEM((2 * HEAD, keys), bf16), pltpu.VMEM((keys, 2 * HEAD), bf16)],
        compiler_params=params(),
        cost_estimate=cost(keys, 2),
        name="self_forward",
    )(qkv)


def self_backward(qkv, do, keep, scale):
    keys = BLOCKS * TOK
    return pl.pallas_call(
        partial(self_backward_kernel, scale=scale),
        out_shape=jax.ShapeDtypeStruct((BLOCKS, 3 * HEAD, TOK), bf16),
        in_specs=vmem(3),
        out_specs=vmem(1)[0],
        scratch_shapes=[
            pltpu.VMEM((DEPTH, keys), bf16),
            pltpu.VMEM((keys, 2 * HEAD), bf16),
            pltpu.VMEM((2 * HEAD, keys), bf16),
            pltpu.VMEM((HEAD, keys), f32),
            pltpu.VMEM((HEAD, keys), f32),
        ],
        compiler_params=params(),
        cost_estimate=cost(keys, 5),
        name="self_backward",
    )(qkv, do, keep)


def cross_forward(order, live, q, kv, scale):
    keys = LIVE_MAX * SLOTS
    return pl.pallas_call(
        partial(cross_forward_kernel, scale=scale),
        out_shape=(OUT_T, KEEP_T),
        in_specs=smem(2) + vmem(2),
        out_specs=tuple(vmem(2)),
        scratch_shapes=[pltpu.VMEM((DEPTH, keys), bf16), pltpu.VMEM((keys, 2 * HEAD), bf16)],
        compiler_params=params(),
        cost_estimate=cost(keys, 2),
        name="cross_forward",
    )(order, live, q, kv)


def cross_backward(order, live, q, do, keep, kv, scale):
    keys = LIVE_MAX * SLOTS
    return pl.pallas_call(
        partial(cross_backward_kernel, scale=scale),
        out_shape=(OUT_T, jax.ShapeDtypeStruct((BLOCKS, 2 * HEAD, SLOTS), bf16)),
        in_specs=smem(2) + vmem(4),
        out_specs=tuple(vmem(2)),
        scratch_shapes=[
            pltpu.VMEM((DEPTH, keys), bf16),
            pltpu.VMEM((keys, 2 * HEAD), bf16),
            pltpu.VMEM((2 * HEAD, keys), bf16),
            pltpu.VMEM((HEAD, keys), f32),
            pltpu.VMEM((HEAD, keys), f32),
        ],
        compiler_params=params(),
        cost_estimate=cost(keys, 5),
        name="cross_backward",
    )(order, live, q, do, keep, kv)


def normed(v):
    centred = v - jnp.mean(v, -1, keepdims=True)
    spread = jnp.mean(centred * centred, -1, keepdims=True)
    r = lax.rsqrt(spread + EPS)
    return centred * r, r


def norm_backward(da, xh, r, gain):
    d = da * (1.0 + gain)
    along = jnp.mean(d * xh, -1, keepdims=True)
    return r * (d - jnp.mean(d, -1, keepdims=True) - xh * along)


def token_rows(ref, lo, hi):
    block = ref[:, lo:hi, :]
    return block.reshape(HEADS * (hi - lo), block.shape[2]).T


def store_heads(ref, lo, value):
    turned = value.T.astype(bf16)
    ref[:, lo : lo + HEAD, :] = turned.reshape(HEADS, HEAD, turned.shape[1])


def load_all(pairs, sems):
    copies = [pltpu.make_async_copy(src, dst, sems.at[n]) for n, (src, dst) in enumerate(pairs)]
    for copy in copies:
        copy.start()
    return copies


def enter_kernel(item_ref, camera_ref, x_ref, cot_ref, mod_ref, wq_any, wk_any, wv_any, sent_ref, acts_ref, gains_ref, wq, wk, wv, sems):
    copies = load_all(((wq_any, wq), (wk_any, wk), (wv_any, wv)), sems)
    row = mod_ref[pl.ds(camera_ref[item_ref[0]], 1), :]
    for n in range(6):
        gains_ref[n : n + 1, :] = row[:, n * WIDTH : (n + 1) * WIDTH]
    gains_ref[6:8, :] = jnp.zeros((2, WIDTH), f32)
    xh, _ = normed(x_ref[...].astype(f32))
    acts_ref[0] = cot_ref[...]
    acts_ref[1] = x_ref[...]
    a1 = (xh * (1.0 + gains_ref[0:1, :]) + gains_ref[1:2, :]).astype(bf16)
    for n, (copy, w) in enumerate(zip(copies, (wq, wk, wv))):
        copy.wait()
        store_heads(sent_ref, n * HEAD, mm(a1, w[...]))


def middle_kernel(o_ref, x_ref, gains_ref, early_ref, wo_any, wcq_any, first_ref, acts_ref, q_ref, wo, wcq, sems):
    copies = load_all(((wo_any, wo), (wcq_any, wcq)), sems)
    o1 = token_rows(o_ref, 0, HEAD)
    acts_ref[0:2] = early_ref[...]
    acts_ref[2] = o1
    copies[0].wait()
    first = x_ref[...].astype(f32) + mm(o1, wo[...])
    first_ref[...] = first
    xh, _ = normed(first)
    a2 = (xh * (1.0 + gains_ref[2:3, :]) + gains_ref[3:4, :]).astype(bf16)
    copies[1].wait()
    store_heads(q_ref, 0, mm(a2, wcq[...]))


def gelu_both(a3, cot, we, wr):
    u = mm(a3, we)
    square = u * u
    t = jnp.tanh(u * (GELU_A + GELU_A * GELU_B * square))
    h = (0.5 * u * (1.0 + t)).astype(bf16)
    dh = mm(cot, wr, 1, 1).astype(bf16).astype(f32)
    slope = 0.5 * (1.0 + t) + 0.5 * u * (1.0 - t * t) * (GELU_A + 3.0 * GELU_A * GELU_B * square)
    return h, (dh * slope).astype(bf16)


def mlp_kernel(
    oc_ref, first_ref, cot_ref, gains_ref, wco_ref, we_ref, wr_ref,
    out_ref, back_ref, acts_ref, do_ref, dgb_ref, a3, second, y, da3,
):
    step = pl.program_id(0)

    @pl.when(step == 0)
    def _():
        total = first_ref[...] + mm(token_rows(oc_ref, 0, HEAD), wco_ref[...])
        second[...] = total
        xh, _ = normed(total)
        a3[...] = (xh * (1.0 + gains_ref[4:5, :]) + gains_ref[5:6, :]).astype(bf16)
        y[...] = jnp.zeros_like(y)
        da3[...] = jnp.zeros_like(da3)

    h, du = gelu_both(a3[...], cot_ref[...], we_ref[...], wr_ref[...])
    y[...] += mm(h, wr_ref[...])
    da3[...] += mm(du, we_ref[...], 1, 1)

    @pl.when(step == pl.num_programs(0) - 1)
    def _():
        total = second[...]
        out_ref[...] = total + y[...]
        xh, r = normed(total)
        d = da3[...]
        dgb_ref[...] = jnp.zeros_like(dgb_ref)
        dgb_ref[0:1, :] = jnp.sum(d * xh, 0, keepdims=True)
        dgb_ref[1:2, :] = jnp.sum(d, 0, keepdims=True)
        back = cot_ref[...].astype(f32) + norm_backward(d, xh, r, gains_ref[4:5, :])
        back_ref[...] = back
        dy2 = back.astype(bf16)
        acts_ref[0] = a3[...]
        acts_ref[1] = dy2
        store_heads(do_ref, 0, mm(dy2, wco_ref[...], 1, 1))


def return_kernel(dq_ref, first_ref, second_back_ref, gains_ref, wcq_any, wo_any, back_ref, sent_ref, dgb_ref, wcq, wo, sems):
    copies = load_all(((wcq_any, wcq), (wo_any, wo)), sems)
    xh, r = normed(first_ref[...])
    dq = token_rows(dq_ref, 0, HEAD)
    copies[0].wait()
    da2 = mm(dq, wcq[...], 1, 1)
    dgb_ref[...] = jnp.zeros_like(dgb_ref)
    dgb_ref[0:1, :] = jnp.sum(da2 * xh, 0, keepdims=True)
    dgb_ref[1:2, :] = jnp.sum(da2, 0, keepdims=True)
    back = second_back_ref[...] + norm_backward(da2, xh, r, gains_ref[2:3, :])
    back_ref[...] = back
    dy1 = back.astype(bf16)
    store_heads(sent_ref, HEAD, back)
    copies[1].wait()
    store_heads(sent_ref, 0, mm(dy1, wo[...], 1, 1))


def leave_kernel(got_ref, x_ref, back_ref, gains_ref, wq_any, wk_any, wv_any, out_ref, camera_ref, wq, wk, wv, sems):
    copies = load_all(((wq_any, wq), (wk_any, wk), (wv_any, wv)), sems)
    lines = got_ref[0, 3 * HEAD :, :].astype(f32)
    for n in range(1, BLOCKS):
        lines += got_ref[n, 3 * HEAD :, :].astype(f32)
    camera_ref[...] = lines[:16] + lines[16:]
    xh, r = normed(x_ref[...].astype(f32))
    da1 = jnp.zeros(out_ref.shape, f32)
    for n, (copy, w) in enumerate(zip(copies, (wq, wk, wv))):
        copy.wait()
        da1 += mm(token_rows(got_ref, n * HEAD, (n + 1) * HEAD), w[...], 1, 1)
    out_ref[...] = back_ref[...] + norm_backward(da1, xh, r, gains_ref[0:1, :])


def patches_kernel(got_ref, wk_ref, wv_ref, out_ref):
    dk = token_rows(got_ref, 0, HEAD)
    dv = token_rows(got_ref, HEAD, 2 * HEAD)
    out_ref[...] = mm(dk, wk_ref[...], 1, 1) + mm(dv, wv_ref[...], 1, 1)


def side_by_side(ref, lo, hi):
    return jnp.concatenate([ref[n, lo:hi, :] for n in range(ref.shape[0])], 1)


def one_above_other(ref):
    block = ref[...]
    return block.reshape(-1, block.shape[-1])


def store_columns(ref, at, grad_t):
    columns, rows = grad_t.shape[0] // 2, grad_t.shape[1] // 4
    for e in range(2):
        for v in range(4):
            piece = grad_t[e * columns : (e + 1) * columns, v * rows : (v + 1) * rows]
            if rows < 256:
                piece = jnp.concatenate([piece, jnp.zeros((columns, 256 - rows), f32)], 1)
            ref[e * 4 + v, at : at + columns, :] = piece.astype(bf16)


def add_up(step, accs, terms):
    @pl.when(step == 0)
    def _():
        for acc, term in zip(accs, terms):
            acc[...] = term

    @pl.when(step > 0)
    def _():
        for acc, term in zip(accs, terms):
            acc[...] += term


def cross_grads_kernel(dqc_ref, x_ref, o1_ref, gains_ref, wo_ref, dkv_ref, patches_ref, col_ref, q_acc, kv_acc):
    step = pl.program_id(0)
    first = one_above_other(x_ref).astype(f32) + mm(one_above_other(o1_ref), wo_ref[...])
    a2 = (normed(first)[0] * (1.0 + gains_ref[2:3, :]) + gains_ref[3:4, :]).astype(bf16)
    q = mm(side_by_side(dqc_ref, 0, HEAD), a2)
    kv = mm(side_by_side(dkv_ref, 0, 2 * HEAD), one_above_other(patches_ref))
    add_up(step, (q_acc, kv_acc), (q, kv))

    @pl.when(step == pl.num_programs(0) - 1)
    def _():
        store_columns(col_ref, 0, q_acc[...])
        store_columns(col_ref, 32, kv_acc[:HEAD, :])
        store_columns(col_ref, 64, kv_acc[HEAD:, :])


def hidden_grads_kernel(
    head_ref, cot_ref, o1_ref, a3_ref, dy2_ref, do_ref, oc_ref, we_ref, wr_ref, late_ref, cross_ref,
    col_ref, row_ref, e_acc, r_acc, o_acc, oc_acc,
):
    step = pl.program_id(0)
    a3, cot = one_above_other(a3_ref), one_above_other(cot_ref)
    h, du = gelu_both(a3, cot, we_ref[...], wr_ref[...])
    e = mm(du.T, a3)
    r = mm(h.T, cot)
    o = mm(side_by_side(do_ref, HEAD, 2 * HEAD), one_above_other(o1_ref))
    oc = mm(side_by_side(oc_ref, 0, HEAD), one_above_other(dy2_ref))
    add_up(step, (e_acc, r_acc, o_acc, oc_acc), (e, r, o, oc))

    @pl.when(step == pl.num_programs(0) - 1)
    def _():
        col_ref[:, :96, :] = late_ref[...]
        col_ref[:, 96:192, :] = cross_ref[...]
        store_columns(col_ref, 192, o_acc[...])
        store_columns(col_ref, 224, e_acc[...])
        rows = jnp.concatenate([r_acc[...], oc_acc[...], jnp.zeros((HEAD, WIDTH), f32)], 0)
        row_ref[...] = rows.T.astype(bf16).reshape(row_ref.shape)


def late_kernel(dqkv_ref, x_ref, wt_ref, gains_ref, dgb2_ref, dgb3_ref, col_ref, sent_ref, qkv_acc, sums):
    step = pl.program_id(0)
    turned = side_by_side(dqkv_ref, 0, 3 * HEAD)
    xh = normed(one_above_other(x_ref).astype(f32))[0].astype(bf16)
    qkv = mm(turned, xh)
    total = jnp.broadcast_to(jnp.sum(turned.astype(f32), 1, keepdims=True), sums.shape)
    add_up(step, (qkv_acc, sums), (qkv, total))
    blocks = dqkv_ref.shape[0]
    for n in range(blocks):
        sent_ref[step * blocks + n, : 3 * HEAD, :] = dqkv_ref[n]

    @pl.when(step == pl.num_programs(0) - 1)
    def _():
        moment = qkv_acc[...]
        count = sums[:, 0:1]
        weights = wt_ref[...].astype(f32)
        grad = moment * (1.0 + gains_ref[0:1, :]) + count * gains_ref[1:2, :]
        for n in range(3):
            store_columns(col_ref, n * 32, grad[n * HEAD : (n + 1) * HEAD])
        dg1 = jnp.sum(weights * moment, 0, keepdims=True)
        db1 = jnp.sum(weights * count, 0, keepdims=True)
        flat = jnp.concatenate([dg1, db1] + [ref[n : n + 1, :] for ref in (dgb2_ref, dgb3_ref) for n in range(2)], 1)
        chunk = flat.shape[1] // 32
        fill = jnp.zeros((1, 2 * TOK - chunk), f32)
        for b in range(4):
            lines = []
            for i in range(8):
                at = (i * 4 + b) * chunk
                line = jnp.concatenate([flat[:, at : at + chunk], fill], 1)
                lines += [line[:, :TOK], line[:, TOK:]]
            lines = jnp.concatenate(lines, 0)
            high = lines.astype(bf16)
            both = jnp.concatenate([high, (lines - high.astype(f32)).astype(bf16)], 0)
            for v in range(4):
                sent_ref[v * 4 + b, 3 * HEAD :, :] = both


def add_items_kernel(got_ref, out_ref):
    total = got_ref[0].astype(f32)
    for n in range(1, 8):
        total += got_ref[n].astype(f32)
    out_ref[...] = total.astype(bf16)


def finish_columns_kernel(in_ref, *out_refs):
    at = 0
    for ref in out_refs[:-1]:
        columns, rows = ref.shape
        ref[...] = in_ref[at : at + columns, :rows].astype(f32)
        at += columns
    out_refs[-1][...] = in_ref[at:, :].astype(f32).T


def finish_rows_kernel(camera_ref, view_ref, got_ref, r_ref, oc_ref, modulation_ref):
    units = r_ref.shape[1] // 4
    for s in range(4):
        total = got_ref[s].astype(f32)
        for n in range(1, 8):
            total += got_ref[n * 4 + s].astype(f32)
        r_ref[:, s * units : (s + 1) * units] = total[:, :units]
        oc_ref[:, s * HEAD : (s + 1) * HEAD] = total[:, units : units + HEAD]
    rows = [jnp.zeros((16, HEAD), f32) for _ in range(4)]
    for n in range(8):
        part = sum(got_ref[n * 4 + s, 0:16, units + HEAD : units + 2 * HEAD].astype(f32) for s in range(4))
        for k in range(4):
            rows[k] += jnp.where(camera_ref[n] == view_ref[0] * 4 + k, part, 0.0)
    for k in range(4):
        for n in range(3):
            modulation_ref[k : k + 1, n * HEAD : (n + 1) * HEAD] = rows[k][n : n + 1] + rows[k][n + 3 : n + 4]


WIDTH = 1024
HIDDEN = 4096
PATCH = 768
UNITS = HIDDEN // BLOCKS
GELU_A = 0.7978845608028654
GELU_B = 0.044715


def shaped(*shape, dtype=bf16):
    return jax.ShapeDtypeStruct(shape, dtype)


ANY = pl.BlockSpec(memory_space=pl.ANY)
V = pl.BlockSpec(memory_space=pltpu.VMEM)
S = pl.BlockSpec(memory_space=pltpu.SMEM)
MB = 1 << 20


def weight(rows=WIDTH, columns=WIDTH):
    return pltpu.VMEM((rows, columns), bf16)


def call(kernel, name, ins, outs, scratch, flops, traffic):
    return pl.pallas_call(
        kernel,
        out_shape=outs,
        in_specs=ins,
        out_specs=jax.tree.map(lambda _: V, outs),
        scratch_shapes=scratch,
        compiler_params=pltpu.CompilerParams(vmem_limit_bytes=VMEM_BYTES),
        cost_estimate=pl.CostEstimate(flops=flops, bytes_accessed=traffic, transcendentals=0),
        name=name,
    )


TOKENS_F32 = shaped(TOK, WIDTH, dtype=f32)
TOKENS_BF16 = shaped(TOK, WIDTH)
ROWS_F32 = shaped(8, WIDTH, dtype=f32)
SQUARE = 2 * TOK * WIDTH * WIDTH


def enter(*args):
    return call(
        enter_kernel, "enter", [S, S, V, V, V, ANY, ANY, ANY],
        (shaped(BLOCKS, 3 * HEAD, TOK), shaped(2, TOK, WIDTH), ROWS_F32),
        [weight(), weight(), weight(), pltpu.SemaphoreType.DMA((3,))], 3 * SQUARE, 8 * MB,
    )(*args)


def middle(*args):
    return call(
        middle_kernel, "middle", [V, V, V, V, ANY, ANY], (TOKENS_F32, shaped(3, TOK, WIDTH), OUT_T),
        [weight(), weight(), pltpu.SemaphoreType.DMA((2,))], 2 * SQUARE, 6 * MB,
    )(*args)


def mlp(*args):
    steps = 8
    width = HIDDEN // steps
    whole = lambda *shape: pl.BlockSpec(shape, lambda i: (0,) * len(shape))
    outs = (TOKENS_F32, TOKENS_F32, shaped(2, TOK, WIDTH), OUT_T, ROWS_F32)
    out_specs = tuple(whole(*o.shape) for o in outs)
    tokens = whole(TOK, WIDTH)
    return pl.pallas_call(
        mlp_kernel,
        grid=(steps,),
        out_shape=outs,
        in_specs=[
            whole(BLOCKS, HEAD, TOK), tokens, tokens, whole(8, WIDTH), whole(WIDTH, WIDTH),
            pl.BlockSpec((WIDTH, width), lambda i: (0, i)), pl.BlockSpec((width, WIDTH), lambda i: (i, 0)),
        ],
        out_specs=out_specs,
        scratch_shapes=[
            pltpu.VMEM((TOK, WIDTH), bf16), pltpu.VMEM((TOK, WIDTH), f32),
            pltpu.VMEM((TOK, WIDTH), f32), pltpu.VMEM((TOK, WIDTH), f32),
        ],
        compiler_params=pltpu.CompilerParams(vmem_limit_bytes=VMEM_BYTES),
        cost_estimate=pl.CostEstimate(flops=18 * SQUARE, bytes_accessed=22 * MB, transcendentals=TOK * HIDDEN),
        name="mlp",
    )(*args)


def returned(*args):
    return call(
        return_kernel, "returned", [V, V, V, V, ANY, ANY], (TOKENS_F32, shaped(BLOCKS, 2 * HEAD, TOK), ROWS_F32),
        [weight(), weight(), pltpu.SemaphoreType.DMA((2,))], 2 * SQUARE, 6 * MB,
    )(*args)


def leave(*args):
    return call(
        leave_kernel, "leave", [V, V, V, V, ANY, ANY, ANY], (TOKENS_F32, shaped(16, TOK, dtype=f32)),
        [weight(), weight(), weight(), pltpu.SemaphoreType.DMA((3,))], 3 * SQUARE, 8 * MB,
    )(*args)


def patches_back(*args):
    return call(
        patches_kernel, "patches_back", [V, V, V], shaped(SLOTS, PATCH, dtype=f32), [], 3 * SQUARE, 5 * MB
    )(*args)


STEPS = 4


def blocks_of(*shape):
    return pl.BlockSpec((BLOCKS // STEPS,) + shape, lambda i: (i,) + (0,) * len(shape))


def gathered(*shape, at=None):
    plane = () if at is None else (at,)
    return pl.BlockSpec((4, 1) + (1,) * len(plane) + shape, lambda i: (0, i) + plane + (0,) * len(shape))


def whole_block(*shape):
    return pl.BlockSpec(shape, lambda i: (0,) * len(shape))


def cross_grads(dqc, acts, gains, output_weight, dkv, patches_all):
    out = shaped(8, 96, 256)
    return pl.pallas_call(
        cross_grads_kernel,
        grid=(STEPS,),
        out_shape=out,
        in_specs=[
            blocks_of(HEAD, TOK), gathered(TOK, WIDTH, at=1), gathered(TOK, WIDTH, at=2), whole_block(8, WIDTH),
            whole_block(WIDTH, WIDTH), blocks_of(2 * HEAD, SLOTS), gathered(SLOTS, PATCH),
        ],
        out_specs=whole_block(*out.shape),
        scratch_shapes=[pltpu.VMEM((HEAD, WIDTH), f32), pltpu.VMEM((2 * HEAD, PATCH), f32)],
        compiler_params=pltpu.CompilerParams(vmem_limit_bytes=VMEM_BYTES),
        cost_estimate=pl.CostEstimate(flops=22 * SQUARE, bytes_accessed=18 * MB, transcendentals=0),
        name="cross_grads",
    )(dqc, acts, acts, gains, output_weight, dkv, patches_all)


def hidden_grads(head, acts, late_acts, do1, oc_t, expand_weight, reduce_weight, col_late, col_cross):
    outs = (shaped(8, 352, 256), shaped(32, 32, UNITS + 2 * HEAD))
    by_head = lambda spec: pl.BlockSpec(spec.block_shape, lambda i, head: spec.index_map(i))
    ins = [
        gathered(TOK, WIDTH, at=0), gathered(TOK, WIDTH, at=2), gathered(TOK, WIDTH, at=0),
        gathered(TOK, WIDTH, at=1), blocks_of(2 * HEAD, TOK), blocks_of(HEAD, TOK),
    ]
    own = [
        pl.BlockSpec((WIDTH, UNITS), lambda i, head: (0, head[0])),
        pl.BlockSpec((UNITS, WIDTH), lambda i, head: (head[0], 0)),
        by_head(whole_block(8, 96, 256)), by_head(whole_block(8, 96, 256)),
    ]
    return pl.pallas_call(
        hidden_grads_kernel,
        grid_spec=pltpu.PrefetchScalarGridSpec(
            num_scalar_prefetch=1,
            grid=(STEPS,),
            in_specs=[by_head(spec) for spec in ins] + own,
            out_specs=tuple(by_head(whole_block(*o.shape)) for o in outs),
            scratch_shapes=[
                pltpu.VMEM((UNITS, WIDTH), f32), pltpu.VMEM((UNITS, WIDTH), f32),
                pltpu.VMEM((HEAD, WIDTH), f32), pltpu.VMEM((HEAD, WIDTH), f32),
            ],
        ),
        out_shape=outs,
        compiler_params=pltpu.CompilerParams(vmem_limit_bytes=VMEM_BYTES),
        cost_estimate=pl.CostEstimate(flops=20 * SQUARE, bytes_accessed=20 * MB, transcendentals=0),
        name="hidden_grads",
    )(head, acts, acts, late_acts, late_acts, do1, oc_t, expand_weight, reduce_weight, col_late, col_cross)


def late_grads(dqkv, acts, weights_t, gains, dgb2, dgb3):
    outs = (shaped(8, 96, 256), shaped(BLOCKS, 3 * HEAD + 32, TOK))
    return pl.pallas_call(
        late_kernel,
        grid=(STEPS,),
        out_shape=outs,
        in_specs=[blocks_of(3 * HEAD, TOK), gathered(TOK, WIDTH, at=1), whole_block(3 * HEAD, WIDTH)]
        + [whole_block(8, WIDTH)] * 3,
        out_specs=tuple(whole_block(*o.shape) for o in outs),
        scratch_shapes=[pltpu.VMEM((3 * HEAD, WIDTH), f32), pltpu.VMEM((3 * HEAD, TOK), f32)],
        compiler_params=pltpu.CompilerParams(vmem_limit_bytes=VMEM_BYTES),
        cost_estimate=pl.CostEstimate(flops=4 * SQUARE, bytes_accessed=6 * MB, transcendentals=0),
        name="late_grads",
    )(dqkv, acts, weights_t, gains, dgb2, dgb3)


def add_items(got):
    return call(add_items_kernel, "add_items", [V], shaped(*got.shape[1:]), [], MB, 2 * MB)(got)


def finish_columns(summed):
    small = [(32, 256)] * 4 + [(32, 192)] * 2 + [(32, 256), (256, 128)]
    outs = tuple(shaped(*shape, dtype=f32) for shape in small)
    return call(finish_columns_kernel, "finish_columns", [V], outs, [], MB, MB)(summed)


def finish_rows(camera_ids, view, got):
    outs = (shaped(32, HIDDEN // 4, dtype=f32), shaped(32, 256, dtype=f32), shaped(4, 192, dtype=f32))
    return call(finish_rows_kernel, "finish_rows", [S, S, V], outs, [], MB, 2 * MB)(camera_ids, view, got)


def home_route():
    size = dict(zip(AXES, SIZES))
    place = lambda at: sum(at[a] * s for a, s in zip(AXES, (64, 32, 8, 4, 2, 1)))
    route = []
    for spot in every(*[range(size[a]) for a in AXES]):
        at = dict(zip(AXES, spot))
        p = at["x"] * 2 + at["zh"]
        to = dict(x=at["yh"] * 2 + at["c"], zh=at["zl"], zl=at["yl"], yl=p >> 2, yh=p >> 1 & 1, c=p & 1)
        route.append((place(at), place(to)))
    return route


def on_device(
    tokens, patches, patch_counts, camera_ids, modulation, query_weight, key_weight, value_weight, output_weight,
    cross_query, cross_key, cross_value, cross_output, expand_weight, reduce_weight, cotangent,
):
    scale = HEAD**-0.5
    item = lax.axis_index(ITEMS)
    head = lax.axis_index(ITEM)
    view = lax.axis_index(VIEW)
    counts = lax.dynamic_index_in_dim(patch_counts, item, 0, keepdims=False)
    gather = lambda block: lax.all_gather(block, GATHER, axis=0, tiled=False).reshape((4, 4) + block.shape)

    x = tokens[0, 0]
    grad_out = cotangent[0, 0]
    patches_all = gather(patches[0, 0])

    live = (jnp.arange(4)[:, None] * SLOTS < counts[None, :]).reshape(BLOCKS)
    n_live = jnp.sum(live.astype(jnp.int32))
    rank = jnp.where(live, jnp.cumsum(live) - 1, n_live + jnp.cumsum(~live) - 1)
    slot = jnp.arange(BLOCKS)
    order = jnp.sum(jnp.where(rank[None, :] == slot[:, None], slot[None, :], 0), 1).astype(jnp.int32)
    n_live = n_live.reshape(1)
    own_columns = lambda w: lax.dynamic_slice_in_dim(w, head * HEAD, HEAD, 1)
    kv_weight = jnp.concatenate([own_columns(cross_key), own_columns(cross_value)], 1)
    weights_t = jnp.concatenate([own_columns(w).T for w in (query_weight, key_weight, value_weight)], 0)

    after = lambda value, *others: lax.optimization_barrier((value,) + others)[0]
    sent, first_acts, gains = enter(item.reshape(1), camera_ids, x, grad_out, modulation, query_weight, key_weight, value_weight)
    qkv, kv_weight, weights_t, order, n_live = lax.optimization_barrier(
        (swap(sent, ITEM), kv_weight, weights_t, order, n_live)
    )
    o_t, keep_self = self_forward(qkv, scale)
    first_sum, acts, sent = middle(swap(o_t, ITEM), x, gains, first_acts, output_weight, cross_query)
    qc = swap(sent, ITEM)
    acts = gather(acts)
    kv = mm(kv_weight, patches_all.reshape(BLOCKS * SLOTS, -1), 0, 1).astype(bf16)
    oc_t, keep_cross = cross_forward(order, n_live, qc, kv, scale)
    layer_out, d_second, late_acts, sent, dgb3 = mlp(
        swap(oc_t, ITEM), first_sum, grad_out, gains, cross_output, expand_weight, reduce_weight
    )
    do_c = swap(sent, ITEM)
    late_acts = gather(late_acts)
    dqc, dkv = cross_backward(order, n_live, qc, do_c, keep_cross, kv, scale)
    d_first, sent, dgb2 = returned(swap(dqc, ITEM), first_sum, d_second, gains, cross_query, output_weight)
    do1, col_cross = lax.optimization_barrier((swap(sent, ITEM), cross_grads(dqc, acts, gains, output_weight, dkv, patches_all)))
    dkv_got = swap(after(dkv, do1), ITEM)
    dqkv = self_backward(qkv, do1, keep_self, scale)
    col_late, sent = late_grads(dqkv, acts, weights_t, gains, dgb2, dgb3)
    sent, dkv_got = lax.optimization_barrier((sent, dkv_got))
    columns, row = hidden_grads(
        head.reshape(1), acts, late_acts, after(do1, sent), oc_t, expand_weight, reduce_weight, col_late, col_cross
    )
    got, columns, row = lax.optimization_barrier((swap(sent, ITEM), columns, row))
    columns = swap(columns, ITEMS)
    tokens_grad, camera_sum = leave(got, x, d_first, gains, query_weight, key_weight, value_weight)
    patches_grad = patches_back(dkv_got, cross_key, cross_value)

    camera_sum = camera_sum.reshape(8, -1)[:, : 3 * HEAD]
    high = camera_sum.astype(bf16)
    low = (camera_sum - high.astype(f32)).astype(bf16)
    lines = jnp.concatenate([high.reshape(8, 3, HEAD), low.reshape(8, 3, HEAD)], 1)
    mine = jnp.arange(4) == lax.axis_index(("zl", "yl"))
    lines = jnp.where(mine[None, :, None, None], lines[:, None], 0).astype(bf16).reshape(32, 6, HEAD)
    row = row + jnp.pad(lines, ((0, 0), (0, 26), (UNITS + HEAD, 0)))

    columns, row = lax.optimization_barrier((columns, row))
    rows = swap(row, ROW)
    summed = lax.ppermute(add_items(columns), AXES, home_route())
    *turned, e_grad = finish_columns(summed)
    q_grad, k_grad, v_grad, cq_grad, ck_grad, cv_grad, o_grad = (grad.T for grad in turned)
    r_grad, co_grad, modulation_grad = finish_rows(camera_ids, view.reshape(1), rows)
    return (
        layer_out[None, None],
        tokens_grad[None, None],
        patches_grad[None, None],
        modulation_grad,
        q_grad,
        k_grad,
        v_grad,
        o_grad,
        cq_grad,
        ck_grad,
        cv_grad,
        co_grad.T,
        e_grad,
        r_grad.T,
    )


def solution(mesh):
    fine = Mesh(mesh.devices.reshape(SIZES), AXES)
    split = P(ROW, VIEW, None, None)
    grads = P(VIEW, ROW)
    return jax.shard_map(
        on_device,
        mesh=fine,
        in_specs=(split, split) + (P(),) * 13 + (split,),
        out_specs=(split,) * 3 + (grads,) * 11,
        check_vma=False,
    )
```

```python
from functools import partial
from itertools import product as every

import jax
import jax.numpy as jnp
from jax import lax
from jax.experimental import pallas as pl
from jax.experimental.pallas import tpu as pltpu
from jax.sharding import Mesh
from jax.sharding import PartitionSpec as P

HEADS = 16
HEAD = 64
TOK = 128
SLOTS = 256
BLOCKS = 16
LIVE_MAX = 13
EPS = 1e-05
LOG2E = 1.4426950408889634
FAR = -1e30

AXES = ("yh", "c", "x", "zh", "zl", "yl")
SIZES = (2, 2, 4, 2, 2, 2)
VIEW = ("yh", "c")
ROW = ("x", "zh", "zl", "yl")
ITEM = ("yh", "c", "zl", "yl")
ITEMS = ("x", "zh")
GATHER = ("zl", "yl", "yh", "c")
VMEM_BYTES = 60 * 1024 * 1024

bf16 = jnp.bfloat16
f32 = jnp.float32


def mm(left, right, lc=1, rc=0):
    return lax.dot_general(left, right, (((lc,), (rc,)), ((), ())), preferred_element_type=f32)


def swap(block, axes):
    return lax.all_to_all(block, axes, 0, 0, tiled=True)


def three_parts(row):
    high = row.astype(bf16)
    rest = row - high.astype(f32)
    middle = rest.astype(bf16)
    low = (rest - middle.astype(f32)).astype(bf16)
    return high, middle, low


CHAINS, ROWS = 8, 2
BACK_CHAINS, BACK_ROWS = 8, 1
DEPTH = 3 * HEAD


def scaled(turned, factor):
    value = turned.astype(f32) * factor
    high = value.astype(bf16)
    low = value - high.astype(f32)
    return jnp.concatenate([high.astype(f32), low], 0)


def softmax_block(q, kt, v, o_ref, keep_ref, at):
    s = mm(q, kt)
    m = jnp.max(s, 1, keepdims=True)
    p = jnp.exp2(s - m)
    o = mm(p.astype(bf16), v)
    total = o[:, HEAD : HEAD + 1]
    o = o[:, :HEAD] / total
    lse = m + jnp.log2(total)
    packed = jnp.concatenate([o, jnp.broadcast_to(lse, o.shape)], 1).T
    for part in range(packed.shape[1] // TOK):
        piece = packed[:, part * TOK : (part + 1) * TOK]
        o_ref[at + part] = piece[:HEAD].astype(bf16)
        keep_ref[at + part] = piece[: HEAD + 8]


def backward_block(qts, dots, keeps, kt, k, vt, dk_acc, dv_acc, scale):
    q_rows, do_rows = [], []
    for qt, dot, keep in zip(qts, dots, keeps):
        lse = keep[HEAD : HEAD + 1]
        delta = jnp.sum(dot.astype(f32) * keep[:HEAD], 0, keepdims=True) * scale
        one = jnp.ones_like(lse)
        zero = jnp.zeros((HEAD - 4, TOK), f32)
        parts = [part.astype(f32) for part in three_parts(-lse)]
        q_rows.append(jnp.concatenate([scaled(qt, scale * LOG2E), one] + parts + [zero], 0))
        parts = [part.astype(f32) for part in three_parts(-delta)]
        do_rows.append(jnp.concatenate([dot.astype(f32) * scale] + parts + [0.0 * one, zero], 0))
    q = jnp.concatenate([rows.T for rows in q_rows], 0).astype(bf16)
    do = jnp.concatenate([rows.T for rows in do_rows], 0).astype(bf16)
    p = jnp.exp2(mm(q, kt))
    ds = (p * mm(do, vt)).astype(bf16)
    dq = mm(ds, k)
    dk_acc[...] += mm(jnp.concatenate(qts, 1), ds)
    dv_acc[...] += mm(jnp.concatenate(dots, 1), p.astype(bf16))
    return dq[:, :HEAD]


def store_blocks(ref, at, rows, value):
    turned = value.T
    for part in range(turned.shape[1] // TOK):
        ref[at + part, rows, :] = turned[:, part * TOK : (part + 1) * TOK].astype(ref.dtype)


def with_ones(rows):
    ones = jnp.where(lax.broadcasted_iota(jnp.int32, rows.shape, 1) == 0, 1.0, 0.0).astype(bf16)
    return jnp.concatenate([rows, ones], 1)


def self_forward_kernel(qkv_ref, o_ref, keep_ref, kt, v, *, scale):
    for j in range(BLOCKS):
        cols = slice(j * TOK, (j + 1) * TOK)
        kt[:HEAD, cols] = qkv_ref[j, HEAD : 2 * HEAD, :]
        kt[HEAD:, cols] = qkv_ref[j, HEAD : 2 * HEAD, :]
        v[cols, :] = with_ones(qkv_ref[j, 2 * HEAD :, :].T)

    def one(i, carry):
        for c in range(CHAINS):
            at = (i * CHAINS + c) * ROWS
            q = jnp.concatenate([scaled(qkv_ref[at + n, :HEAD, :], scale * LOG2E).T for n in range(ROWS)], 0).astype(bf16)
            softmax_block(q, kt[...], v[...], o_ref, keep_ref, at)
        return carry

    lax.fori_loop(0, BLOCKS // (ROWS * CHAINS), one, 0)


def self_backward_kernel(qkv_ref, do_ref, keep_ref, out_ref, kt, k, vt, dk_acc, dv_acc, *, scale):
    row = lax.broadcasted_iota(jnp.int32, (HEAD, BLOCKS * TOK), 0)
    kt[2 * HEAD :, :] = jnp.where((row >= 1) & (row < 4), 1.0, 0.0).astype(bf16)
    vt[HEAD:, :] = jnp.where(row < 3, 1.0, 0.0).astype(bf16)
    for j in range(BLOCKS):
        cols = slice(j * TOK, (j + 1) * TOK)
        kt[:HEAD, cols] = qkv_ref[j, HEAD : 2 * HEAD, :]
        kt[HEAD : 2 * HEAD, cols] = qkv_ref[j, HEAD : 2 * HEAD, :]
        k[cols, :] = kt[: 2 * HEAD, cols].T
        vt[:HEAD, cols] = qkv_ref[j, 2 * HEAD :, :]
    dk_acc[...] = jnp.zeros_like(dk_acc)
    dv_acc[...] = jnp.zeros_like(dv_acc)

    def one(i, carry):
        for c in range(BACK_CHAINS):
            at = (i * BACK_CHAINS + c) * BACK_ROWS
            qts = [qkv_ref[at + n, :HEAD, :] for n in range(BACK_ROWS)]
            dots = [do_ref[at + n, :HEAD, :] for n in range(BACK_ROWS)]
            keeps = [keep_ref[at + n] for n in range(BACK_ROWS)]
            dq = backward_block(qts, dots, keeps, kt[...], k[...], vt[...], dk_acc, dv_acc, scale)
            store_blocks(out_ref, at, slice(0, HEAD), dq)
        return carry

    lax.fori_loop(0, BLOCKS // (BACK_CHAINS * BACK_ROWS), one, 0)
    for j in range(BLOCKS):
        cols = slice(j * TOK, (j + 1) * TOK)
        out_ref[j, HEAD : 2 * HEAD, :] = dk_acc[:, cols].astype(bf16)
        out_ref[j, 2 * HEAD :, :] = dv_acc[:, cols].astype(bf16)


def slot_block(kv_ref, index):
    return kv_ref[:, pl.ds(pl.multiple_of(index * SLOTS, SLOTS), SLOTS)]


def own_place(index):
    return (index % 4) * 4 + index // 4


def cross_forward_kernel(order_ref, live_ref, q_ref, kv_ref, o_ref, keep_ref, kt, v, *, scale):
    for t in range(LIVE_MAX):
        cols = slice(t * SLOTS, (t + 1) * SLOTS)
        block = slot_block(kv_ref, order_ref[t])
        kt[:HEAD, cols] = block[:HEAD]
        kt[HEAD : 2 * HEAD, cols] = block[:HEAD]
        bias = jnp.where(t < live_ref[0], 0.0, FAR)
        row = lax.broadcasted_iota(jnp.int32, (HEAD, SLOTS), 0)
        kt[2 * HEAD :, cols] = jnp.where(row == 0, bias, 0.0).astype(bf16)
        v[cols, :] = with_ones(block[HEAD:].T)
    one_row = jnp.where(lax.broadcasted_iota(jnp.int32, (HEAD, TOK), 0) == 0, 1.0, 0.0)

    def one(i, carry):
        for c in range(CHAINS):
            at = (i * CHAINS + c) * ROWS
            q = jnp.concatenate(
                [jnp.concatenate([scaled(q_ref[at + n], scale * LOG2E), one_row], 0).T for n in range(ROWS)], 0
            ).astype(bf16)
            softmax_block(q, kt[...], v[...], o_ref, keep_ref, at)
        return carry

    lax.fori_loop(0, BLOCKS // (ROWS * CHAINS), one, 0)


def cross_backward_kernel(
    order_ref, live_ref, q_ref, do_ref, keep_ref, kv_ref, dq_ref, dkv_ref, kt, k, vt, dk_acc, dv_acc, *, scale
):
    shape = (HEAD, LIVE_MAX * SLOTS)
    row = lax.broadcasted_iota(jnp.int32, shape, 0)
    vt[HEAD:, :] = jnp.where(row < 3, 1.0, 0.0).astype(bf16)
    for t in range(LIVE_MAX):
        cols = slice(t * SLOTS, (t + 1) * SLOTS)
        block = slot_block(kv_ref, order_ref[t])
        kt[:HEAD, cols] = block[:HEAD]
        kt[HEAD : 2 * HEAD, cols] = block[:HEAD]
        bias = jnp.where(t < live_ref[0], 0.0, FAR)
        row = lax.broadcasted_iota(jnp.int32, (HEAD, SLOTS), 0)
        ones = jnp.where((row >= 1) & (row < 4), 1.0, 0.0)
        kt[2 * HEAD :, cols] = jnp.where(row == 0, bias, ones).astype(bf16)
        k[cols, :] = kt[: 2 * HEAD, cols].T
        vt[:HEAD, cols] = block[HEAD:]
    dk_acc[...] = jnp.zeros_like(dk_acc)
    dv_acc[...] = jnp.zeros_like(dv_acc)

    def one(i, carry):
        for c in range(BACK_CHAINS):
            at = (i * BACK_CHAINS + c) * BACK_ROWS
            qts = [q_ref[at + n] for n in range(BACK_ROWS)]
            dots = [do_ref[at + n] for n in range(BACK_ROWS)]
            keeps = [keep_ref[at + n] for n in range(BACK_ROWS)]
            dq = backward_block(qts, dots, keeps, kt[...], k[...], vt[...], dk_acc, dv_acc, scale)
            store_blocks(dq_ref, at, slice(0, HEAD), dq)
        return carry

    lax.fori_loop(0, BLOCKS // (BACK_CHAINS * BACK_ROWS), one, 0)
    for t in range(LIVE_MAX):
        cols = slice(t * SLOTS, (t + 1) * SLOTS)
        dkv_ref[own_place(order_ref[t]), :HEAD, :] = dk_acc[:, cols].astype(bf16)
        dkv_ref[own_place(order_ref[t]), HEAD:, :] = dv_acc[:, cols].astype(bf16)
    for t in range(LIVE_MAX, BLOCKS):
        dkv_ref[own_place(order_ref[t])] = jnp.zeros((2 * HEAD, SLOTS), bf16)


def params():
    return pltpu.CompilerParams(vmem_limit_bytes=40 << 20)


def vmem(count):
    return [pl.BlockSpec(memory_space=pltpu.VMEM)] * count


def smem(count):
    return [pl.BlockSpec(memory_space=pltpu.SMEM)] * count


def cost(keys, products):
    flops = 2 * BLOCKS * TOK * keys * HEAD * products
    return pl.CostEstimate(flops=4 * flops, bytes_accessed=4 << 20, transcendentals=BLOCKS * TOK * keys)


OUT_T = jax.ShapeDtypeStruct((BLOCKS, HEAD, TOK), bf16)
KEEP_T = jax.ShapeDtypeStruct((BLOCKS, HEAD + 8, TOK), f32)


def self_forward(qkv, scale):
    keys = BLOCKS * TOK
    return pl.pallas_call(
        partial(self_forward_kernel, scale=scale),
        out_shape=(OUT_T, KEEP_T),
        in_specs=vmem(1),
        out_specs=tuple(vmem(2)),
        scratch_shapes=[pltpu.VMEM((2 * HEAD, keys), bf16), pltpu.VMEM((keys, 2 * HEAD), bf16)],
        compiler_params=params(),
        cost_estimate=cost(keys, 2),
        name="self_forward",
    )(qkv)


def self_backward(qkv, do, keep, scale):
    keys = BLOCKS * TOK
    return pl.pallas_call(
        partial(self_backward_kernel, scale=scale),
        out_shape=jax.ShapeDtypeStruct((BLOCKS, 3 * HEAD, TOK), bf16),
        in_specs=vmem(3),
        out_specs=vmem(1)[0],
        scratch_shapes=[
            pltpu.VMEM((DEPTH, keys), bf16),
            pltpu.VMEM((keys, 2 * HEAD), bf16),
            pltpu.VMEM((2 * HEAD, keys), bf16),
            pltpu.VMEM((HEAD, keys), f32),
            pltpu.VMEM((HEAD, keys), f32),
        ],
        compiler_params=params(),
        cost_estimate=cost(keys, 5),
        name="self_backward",
    )(qkv, do, keep)


def cross_forward(order, live, q, kv, scale):
    keys = LIVE_MAX * SLOTS
    return pl.pallas_call(
        partial(cross_forward_kernel, scale=scale),
        out_shape=(OUT_T, KEEP_T),
        in_specs=smem(2) + vmem(2),
        out_specs=tuple(vmem(2)),
        scratch_shapes=[pltpu.VMEM((DEPTH, keys), bf16), pltpu.VMEM((keys, 2 * HEAD), bf16)],
        compiler_params=params(),
        cost_estimate=cost(keys, 2),
        name="cross_forward",
    )(order, live, q, kv)


def cross_backward(order, live, q, do, keep, kv, scale):
    keys = LIVE_MAX * SLOTS
    return pl.pallas_call(
        partial(cross_backward_kernel, scale=scale),
        out_shape=(OUT_T, jax.ShapeDtypeStruct((BLOCKS, 2 * HEAD, SLOTS), bf16)),
        in_specs=smem(2) + vmem(4),
        out_specs=tuple(vmem(2)),
        scratch_shapes=[
            pltpu.VMEM((DEPTH, keys), bf16),
            pltpu.VMEM((keys, 2 * HEAD), bf16),
            pltpu.VMEM((2 * HEAD, keys), bf16),
            pltpu.VMEM((HEAD, keys), f32),
            pltpu.VMEM((HEAD, keys), f32),
        ],
        compiler_params=params(),
        cost_estimate=cost(keys, 5),
        name="cross_backward",
    )(order, live, q, do, keep, kv)


def normed(v):
    centred = v - jnp.mean(v, -1, keepdims=True)
    spread = jnp.mean(centred * centred, -1, keepdims=True)
    r = lax.rsqrt(spread + EPS)
    return centred * r, r


def norm_backward(da, xh, r, gain):
    d = da * (1.0 + gain)
    along = jnp.mean(d * xh, -1, keepdims=True)
    return r * (d - jnp.mean(d, -1, keepdims=True) - xh * along)


def token_rows(ref, lo, hi):
    block = ref[:, lo:hi, :]
    return block.reshape(HEADS * (hi - lo), block.shape[2]).T


def store_heads(ref, lo, value):
    turned = value.T.astype(bf16)
    ref[:, lo : lo + HEAD, :] = turned.reshape(HEADS, HEAD, turned.shape[1])


def load_all(pairs, sems):
    copies = [pltpu.make_async_copy(src, dst, sems.at[n]) for n, (src, dst) in enumerate(pairs)]
    for copy in copies:
        copy.start()
    return copies


def enter_kernel(item_ref, camera_ref, x_ref, cot_ref, mod_ref, wq_any, wk_any, wv_any, sent_ref, acts_ref, gains_ref, wq, wk, wv, sems):
    copies = load_all(((wq_any, wq), (wk_any, wk), (wv_any, wv)), sems)
    row = mod_ref[pl.ds(camera_ref[item_ref[0]], 1), :]
    for n in range(6):
        gains_ref[n : n + 1, :] = row[:, n * WIDTH : (n + 1) * WIDTH]
    gains_ref[6:8, :] = jnp.zeros((2, WIDTH), f32)
    xh, _ = normed(x_ref[...].astype(f32))
    acts_ref[0] = cot_ref[...]
    acts_ref[1] = x_ref[...]
    a1 = (xh * (1.0 + gains_ref[0:1, :]) + gains_ref[1:2, :]).astype(bf16)
    for n, (copy, w) in enumerate(zip(copies, (wq, wk, wv))):
        copy.wait()
        store_heads(sent_ref, n * HEAD, mm(a1, w[...]))


def middle_kernel(o_ref, x_ref, gains_ref, early_ref, wo_any, wcq_any, first_ref, acts_ref, q_ref, wo, wcq, sems):
    copies = load_all(((wo_any, wo), (wcq_any, wcq)), sems)
    o1 = token_rows(o_ref, 0, HEAD)
    acts_ref[0:2] = early_ref[...]
    acts_ref[2] = o1
    copies[0].wait()
    first = x_ref[...].astype(f32) + mm(o1, wo[...])
    first_ref[...] = first
    xh, _ = normed(first)
    a2 = (xh * (1.0 + gains_ref[2:3, :]) + gains_ref[3:4, :]).astype(bf16)
    copies[1].wait()
    store_heads(q_ref, 0, mm(a2, wcq[...]))


def gelu_both(a3, cot, we, wr):
    u = mm(a3, we)
    square = u * u
    t = jnp.tanh(u * (GELU_A + GELU_A * GELU_B * square))
    h = (0.5 * u * (1.0 + t)).astype(bf16)
    dh = mm(cot, wr, 1, 1).astype(bf16).astype(f32)
    slope = 0.5 * (1.0 + t) + 0.5 * u * (1.0 - t * t) * (GELU_A + 3.0 * GELU_A * GELU_B * square)
    return h, (dh * slope).astype(bf16)


def mlp_kernel(
    oc_ref, first_ref, cot_ref, gains_ref, wco_ref, we_ref, wr_ref,
    out_ref, back_ref, acts_ref, do_ref, dgb_ref, a3, second, y, da3,
):
    step = pl.program_id(0)

    @pl.when(step == 0)
    def _():
        total = first_ref[...] + mm(token_rows(oc_ref, 0, HEAD), wco_ref[...])
        second[...] = total
        xh, _ = normed(total)
        a3[...] = (xh * (1.0 + gains_ref[4:5, :]) + gains_ref[5:6, :]).astype(bf16)
        y[...] = jnp.zeros_like(y)
        da3[...] = jnp.zeros_like(da3)

    h, du = gelu_both(a3[...], cot_ref[...], we_ref[...], wr_ref[...])
    y[...] += mm(h, wr_ref[...])
    da3[...] += mm(du, we_ref[...], 1, 1)

    @pl.when(step == pl.num_programs(0) - 1)
    def _():
        total = second[...]
        out_ref[...] = total + y[...]
        xh, r = normed(total)
        d = da3[...]
        dgb_ref[...] = jnp.zeros_like(dgb_ref)
        dgb_ref[0:1, :] = jnp.sum(d * xh, 0, keepdims=True)
        dgb_ref[1:2, :] = jnp.sum(d, 0, keepdims=True)
        back = cot_ref[...].astype(f32) + norm_backward(d, xh, r, gains_ref[4:5, :])
        back_ref[...] = back
        dy2 = back.astype(bf16)
        acts_ref[0] = a3[...]
        acts_ref[1] = dy2
        store_heads(do_ref, 0, mm(dy2, wco_ref[...], 1, 1))


def return_kernel(dq_ref, first_ref, second_back_ref, gains_ref, wcq_any, wo_any, back_ref, sent_ref, dgb_ref, wcq, wo, sems):
    copies = load_all(((wcq_any, wcq), (wo_any, wo)), sems)
    xh, r = normed(first_ref[...])
    dq = token_rows(dq_ref, 0, HEAD)
    copies[0].wait()
    da2 = mm(dq, wcq[...], 1, 1)
    dgb_ref[...] = jnp.zeros_like(dgb_ref)
    dgb_ref[0:1, :] = jnp.sum(da2 * xh, 0, keepdims=True)
    dgb_ref[1:2, :] = jnp.sum(da2, 0, keepdims=True)
    back = second_back_ref[...] + norm_backward(da2, xh, r, gains_ref[2:3, :])
    back_ref[...] = back
    dy1 = back.astype(bf16)
    store_heads(sent_ref, HEAD, back)
    copies[1].wait()
    store_heads(sent_ref, 0, mm(dy1, wo[...], 1, 1))


def leave_kernel(got_ref, x_ref, back_ref, gains_ref, wq_any, wk_any, wv_any, out_ref, camera_ref, wq, wk, wv, sems):
    copies = load_all(((wq_any, wq), (wk_any, wk), (wv_any, wv)), sems)
    lines = got_ref[0, 3 * HEAD :, :].astype(f32)
    for n in range(1, BLOCKS):
        lines += got_ref[n, 3 * HEAD :, :].astype(f32)
    camera_ref[...] = lines[:16] + lines[16:]
    xh, r = normed(x_ref[...].astype(f32))
    da1 = jnp.zeros(out_ref.shape, f32)
    for n, (copy, w) in enumerate(zip(copies, (wq, wk, wv))):
        copy.wait()
        da1 += mm(token_rows(got_ref, n * HEAD, (n + 1) * HEAD), w[...], 1, 1)
    out_ref[...] = back_ref[...] + norm_backward(da1, xh, r, gains_ref[0:1, :])


def patches_kernel(got_ref, wk_ref, wv_ref, out_ref):
    dk = token_rows(got_ref, 0, HEAD)
    dv = token_rows(got_ref, HEAD, 2 * HEAD)
    out_ref[...] = mm(dk, wk_ref[...], 1, 1) + mm(dv, wv_ref[...], 1, 1)


def side_by_side(ref, lo, hi):
    return jnp.concatenate([ref[n, lo:hi, :] for n in range(ref.shape[0])], 1)


def one_above_other(ref):
    block = ref[...]
    return block.reshape(-1, block.shape[-1])


def store_columns(ref, at, grad_t):
    columns, rows = grad_t.shape[0] // 2, grad_t.shape[1] // 4
    for e in range(2):
        for v in range(4):
            piece = grad_t[e * columns : (e + 1) * columns, v * rows : (v + 1) * rows]
            if rows < 256:
                piece = jnp.concatenate([piece, jnp.zeros((columns, 256 - rows), f32)], 1)
            ref[e * 4 + v, at : at + columns, :] = piece.astype(bf16)


def add_up(step, accs, terms):
    @pl.when(step == 0)
    def _():
        for acc, term in zip(accs, terms):
            acc[...] = term

    @pl.when(step > 0)
    def _():
        for acc, term in zip(accs, terms):
            acc[...] += term


def cross_grads_kernel(dqc_ref, x_ref, o1_ref, gains_ref, wo_ref, dkv_ref, patches_ref, col_ref, q_acc, kv_acc):
    step = pl.program_id(0)
    first = one_above_other(x_ref).astype(f32) + mm(one_above_other(o1_ref), wo_ref[...])
    a2 = (normed(first)[0] * (1.0 + gains_ref[2:3, :]) + gains_ref[3:4, :]).astype(bf16)
    q = mm(side_by_side(dqc_ref, 0, HEAD), a2)
    kv = mm(side_by_side(dkv_ref, 0, 2 * HEAD), one_above_other(patches_ref))
    add_up(step, (q_acc, kv_acc), (q, kv))

    @pl.when(step == pl.num_programs(0) - 1)
    def _():
        store_columns(col_ref, 0, q_acc[...])
        store_columns(col_ref, 32, kv_acc[:HEAD, :])
        store_columns(col_ref, 64, kv_acc[HEAD:, :])


def hidden_grads_kernel(
    head_ref, cot_ref, o1_ref, a3_ref, dy2_ref, do_ref, oc_ref, we_ref, wr_ref, late_ref, cross_ref,
    col_ref, row_ref, e_acc, r_acc, o_acc, oc_acc,
):
    step = pl.program_id(0)
    a3, cot = one_above_other(a3_ref), one_above_other(cot_ref)
    h, du = gelu_both(a3, cot, we_ref[...], wr_ref[...])
    e = mm(du.T, a3)
    r = mm(h.T, cot)
    o = mm(side_by_side(do_ref, HEAD, 2 * HEAD), one_above_other(o1_ref))
    oc = mm(side_by_side(oc_ref, 0, HEAD), one_above_other(dy2_ref))
    add_up(step, (e_acc, r_acc, o_acc, oc_acc), (e, r, o, oc))

    @pl.when(step == pl.num_programs(0) - 1)
    def _():
        col_ref[:, :96, :] = late_ref[...]
        col_ref[:, 96:192, :] = cross_ref[...]
        store_columns(col_ref, 192, o_acc[...])
        store_columns(col_ref, 224, e_acc[...])
        rows = jnp.concatenate([r_acc[...], oc_acc[...], jnp.zeros((HEAD, WIDTH), f32)], 0)
        row_ref[...] = rows.T.astype(bf16).reshape(row_ref.shape)


def late_kernel(dqkv_ref, x_ref, wt_ref, gains_ref, dgb2_ref, dgb3_ref, col_ref, sent_ref, qkv_acc, sums):
    step = pl.program_id(0)
    turned = side_by_side(dqkv_ref, 0, 3 * HEAD)
    xh = normed(one_above_other(x_ref).astype(f32))[0].astype(bf16)
    qkv = mm(turned, xh)
    total = jnp.broadcast_to(jnp.sum(turned.astype(f32), 1, keepdims=True), sums.shape)
    add_up(step, (qkv_acc, sums), (qkv, total))
    blocks = dqkv_ref.shape[0]
    for n in range(blocks):
        sent_ref[step * blocks + n, : 3 * HEAD, :] = dqkv_ref[n]

    @pl.when(step == pl.num_programs(0) - 1)
    def _():
        moment = qkv_acc[...]
        count = sums[:, 0:1]
        weights = wt_ref[...].astype(f32)
        grad = moment * (1.0 + gains_ref[0:1, :]) + count * gains_ref[1:2, :]
        for n in range(3):
            store_columns(col_ref, n * 32, grad[n * HEAD : (n + 1) * HEAD])
        dg1 = jnp.sum(weights * moment, 0, keepdims=True)
        db1 = jnp.sum(weights * count, 0, keepdims=True)
        flat = jnp.concatenate([dg1, db1] + [ref[n : n + 1, :] for ref in (dgb2_ref, dgb3_ref) for n in range(2)], 1)
        chunk = flat.shape[1] // 32
        fill = jnp.zeros((1, 2 * TOK - chunk), f32)
        for b in range(4):
            lines = []
            for i in range(8):
                at = (i * 4 + b) * chunk
                line = jnp.concatenate([flat[:, at : at + chunk], fill], 1)
                lines += [line[:, :TOK], line[:, TOK:]]
            lines = jnp.concatenate(lines, 0)
            high = lines.astype(bf16)
            both = jnp.concatenate([high, (lines - high.astype(f32)).astype(bf16)], 0)
            for v in range(4):
                sent_ref[v * 4 + b, 3 * HEAD :, :] = both


def add_items_kernel(got_ref, out_ref):
    total = got_ref[0].astype(f32)
    for n in range(1, 8):
        total += got_ref[n].astype(f32)
    out_ref[...] = total.astype(bf16)


def finish_columns_kernel(in_ref, *out_refs):
    at = 0
    for ref in out_refs[:-1]:
        columns, rows = ref.shape
        ref[...] = in_ref[at : at + columns, :rows].astype(f32)
        at += columns
    out_refs[-1][...] = in_ref[at:, :].astype(f32).T


def finish_rows_kernel(camera_ref, view_ref, got_ref, r_ref, oc_ref, modulation_ref):
    units = r_ref.shape[1] // 4
    for s in range(4):
        total = got_ref[s].astype(f32)
        for n in range(1, 8):
            total += got_ref[n * 4 + s].astype(f32)
        r_ref[:, s * units : (s + 1) * units] = total[:, :units]
        oc_ref[:, s * HEAD : (s + 1) * HEAD] = total[:, units : units + HEAD]
    rows = [jnp.zeros((16, HEAD), f32) for _ in range(4)]
    for n in range(8):
        part = sum(got_ref[n * 4 + s, 0:16, units + HEAD : units + 2 * HEAD].astype(f32) for s in range(4))
        for k in range(4):
            rows[k] += jnp.where(camera_ref[n] == view_ref[0] * 4 + k, part, 0.0)
    for k in range(4):
        for n in range(3):
            modulation_ref[k : k + 1, n * HEAD : (n + 1) * HEAD] = rows[k][n : n + 1] + rows[k][n + 3 : n + 4]


WIDTH = 1024
HIDDEN = 4096
PATCH = 768
UNITS = HIDDEN // BLOCKS
GELU_A = 0.7978845608028654
GELU_B = 0.044715


def shaped(*shape, dtype=bf16):
    return jax.ShapeDtypeStruct(shape, dtype)


ANY = pl.BlockSpec(memory_space=pl.ANY)
V = pl.BlockSpec(memory_space=pltpu.VMEM)
S = pl.BlockSpec(memory_space=pltpu.SMEM)
MB = 1 << 20


def weight(rows=WIDTH, columns=WIDTH):
    return pltpu.VMEM((rows, columns), bf16)


def call(kernel, name, ins, outs, scratch, flops, traffic, limit=60):
    return pl.pallas_call(
        kernel,
        out_shape=outs,
        in_specs=ins,
        out_specs=jax.tree.map(lambda _: V, outs),
        scratch_shapes=scratch,
        compiler_params=pltpu.CompilerParams(vmem_limit_bytes=limit * MB),
        cost_estimate=pl.CostEstimate(flops=flops, bytes_accessed=traffic, transcendentals=0),
        name=name,
    )


TOKENS_F32 = shaped(TOK, WIDTH, dtype=f32)
TOKENS_BF16 = shaped(TOK, WIDTH)
ROWS_F32 = shaped(8, WIDTH, dtype=f32)
SQUARE = 2 * TOK * WIDTH * WIDTH


def enter(*args):
    return call(
        enter_kernel, "enter", [S, S, V, V, V, ANY, ANY, ANY],
        (shaped(BLOCKS, 3 * HEAD, TOK), shaped(2, TOK, WIDTH), ROWS_F32),
        [weight(), weight(), weight(), pltpu.SemaphoreType.DMA((3,))], 3 * SQUARE, 8 * MB,
    )(*args)


def middle(*args):
    return call(
        middle_kernel, "middle", [V, V, V, V, ANY, ANY], (TOKENS_F32, shaped(3, TOK, WIDTH), OUT_T),
        [weight(), weight(), pltpu.SemaphoreType.DMA((2,))], 2 * SQUARE, 6 * MB, 24,
    )(*args)


def mlp(*args):
    steps = 4
    width = HIDDEN // steps
    whole = lambda *shape: pl.BlockSpec(shape, lambda i: (0,) * len(shape))
    outs = (TOKENS_F32, TOKENS_F32, shaped(2, TOK, WIDTH), OUT_T, ROWS_F32)
    out_specs = tuple(whole(*o.shape) for o in outs)
    tokens = whole(TOK, WIDTH)
    return pl.pallas_call(
        mlp_kernel,
        grid=(steps,),
        out_shape=outs,
        in_specs=[
            whole(BLOCKS, HEAD, TOK), tokens, tokens, whole(8, WIDTH), whole(WIDTH, WIDTH),
            pl.BlockSpec((WIDTH, width), lambda i: (0, i)), pl.BlockSpec((width, WIDTH), lambda i: (i, 0)),
        ],
        out_specs=out_specs,
        scratch_shapes=[
            pltpu.VMEM((TOK, WIDTH), bf16), pltpu.VMEM((TOK, WIDTH), f32),
            pltpu.VMEM((TOK, WIDTH), f32), pltpu.VMEM((TOK, WIDTH), f32),
        ],
        compiler_params=pltpu.CompilerParams(vmem_limit_bytes=VMEM_BYTES),
        cost_estimate=pl.CostEstimate(flops=18 * SQUARE, bytes_accessed=22 * MB, transcendentals=TOK * HIDDEN),
        name="mlp",
    )(*args)


def returned(*args):
    return call(
        return_kernel, "returned", [V, V, V, V, ANY, ANY], (TOKENS_F32, shaped(BLOCKS, 2 * HEAD, TOK), ROWS_F32),
        [weight(), weight(), pltpu.SemaphoreType.DMA((2,))], 2 * SQUARE, 6 * MB, 24,
    )(*args)


def leave(*args):
    return call(
        leave_kernel, "leave", [V, V, V, V, ANY, ANY, ANY], (TOKENS_F32, shaped(16, TOK, dtype=f32)),
        [weight(), weight(), weight(), pltpu.SemaphoreType.DMA((3,))], 3 * SQUARE, 8 * MB,
    )(*args)


def patches_back(*args):
    return call(
        patches_kernel, "patches_back", [V, V, V], shaped(SLOTS, PATCH, dtype=f32), [], 3 * SQUARE, 5 * MB
    )(*args)


STEPS = 4


def blocks_of(*shape):
    return pl.BlockSpec((BLOCKS // STEPS,) + shape, lambda i: (i,) + (0,) * len(shape))


def gathered(*shape, at=None):
    plane = () if at is None else (at,)
    return pl.BlockSpec((4, 1) + (1,) * len(plane) + shape, lambda i: (0, i) + plane + (0,) * len(shape))


def whole_block(*shape):
    return pl.BlockSpec(shape, lambda i: (0,) * len(shape))


def cross_grads(dqc, acts, gains, output_weight, dkv, patches_all):
    out = shaped(8, 96, 256)
    return pl.pallas_call(
        cross_grads_kernel,
        grid=(STEPS,),
        out_shape=out,
        in_specs=[
            blocks_of(HEAD, TOK), gathered(TOK, WIDTH, at=1), gathered(TOK, WIDTH, at=2), whole_block(8, WIDTH),
            whole_block(WIDTH, WIDTH), blocks_of(2 * HEAD, SLOTS), gathered(SLOTS, PATCH),
        ],
        out_specs=whole_block(*out.shape),
        scratch_shapes=[pltpu.VMEM((HEAD, WIDTH), f32), pltpu.VMEM((2 * HEAD, PATCH), f32)],
        compiler_params=pltpu.CompilerParams(vmem_limit_bytes=VMEM_BYTES),
        cost_estimate=pl.CostEstimate(flops=22 * SQUARE, bytes_accessed=18 * MB, transcendentals=0),
        name="cross_grads",
    )(dqc, acts, acts, gains, output_weight, dkv, patches_all)


def hidden_grads(head, acts, late_acts, do1, oc_t, expand_weight, reduce_weight, col_late, col_cross):
    outs = (shaped(8, 352, 256), shaped(32, 32, UNITS + 2 * HEAD))
    by_head = lambda spec: pl.BlockSpec(spec.block_shape, lambda i, head: spec.index_map(i))
    ins = [
        gathered(TOK, WIDTH, at=0), gathered(TOK, WIDTH, at=2), gathered(TOK, WIDTH, at=0),
        gathered(TOK, WIDTH, at=1), blocks_of(2 * HEAD, TOK), blocks_of(HEAD, TOK),
    ]
    own = [
        pl.BlockSpec((WIDTH, UNITS), lambda i, head: (0, head[0])),
        pl.BlockSpec((UNITS, WIDTH), lambda i, head: (head[0], 0)),
        by_head(whole_block(8, 96, 256)), by_head(whole_block(8, 96, 256)),
    ]
    return pl.pallas_call(
        hidden_grads_kernel,
        grid_spec=pltpu.PrefetchScalarGridSpec(
            num_scalar_prefetch=1,
            grid=(STEPS,),
            in_specs=[by_head(spec) for spec in ins] + own,
            out_specs=tuple(by_head(whole_block(*o.shape)) for o in outs),
            scratch_shapes=[
                pltpu.VMEM((UNITS, WIDTH), f32), pltpu.VMEM((UNITS, WIDTH), f32),
                pltpu.VMEM((HEAD, WIDTH), f32), pltpu.VMEM((HEAD, WIDTH), f32),
            ],
        ),
        out_shape=outs,
        compiler_params=pltpu.CompilerParams(vmem_limit_bytes=VMEM_BYTES),
        cost_estimate=pl.CostEstimate(flops=20 * SQUARE, bytes_accessed=20 * MB, transcendentals=0),
        name="hidden_grads",
    )(head, acts, acts, late_acts, late_acts, do1, oc_t, expand_weight, reduce_weight, col_late, col_cross)


def late_grads(dqkv, acts, weights_t, gains, dgb2, dgb3):
    outs = (shaped(8, 96, 256), shaped(BLOCKS, 3 * HEAD + 32, TOK))
    return pl.pallas_call(
        late_kernel,
        grid=(STEPS,),
        out_shape=outs,
        in_specs=[blocks_of(3 * HEAD, TOK), gathered(TOK, WIDTH, at=1), whole_block(3 * HEAD, WIDTH)]
        + [whole_block(8, WIDTH)] * 3,
        out_specs=tuple(whole_block(*o.shape) for o in outs),
        scratch_shapes=[pltpu.VMEM((3 * HEAD, WIDTH), f32), pltpu.VMEM((3 * HEAD, TOK), f32)],
        compiler_params=pltpu.CompilerParams(vmem_limit_bytes=VMEM_BYTES),
        cost_estimate=pl.CostEstimate(flops=4 * SQUARE, bytes_accessed=6 * MB, transcendentals=0),
        name="late_grads",
    )(dqkv, acts, weights_t, gains, dgb2, dgb3)


def add_items(got):
    return call(add_items_kernel, "add_items", [V], shaped(*got.shape[1:]), [], MB, 2 * MB, 16)(got)


def finish_columns(summed):
    small = [(32, 256)] * 4 + [(32, 192)] * 2 + [(32, 256), (256, 128)]
    outs = tuple(shaped(*shape, dtype=f32) for shape in small)
    return call(finish_columns_kernel, "finish_columns", [V], outs, [], MB, MB, 16)(summed)


def finish_rows(camera_ids, view, got):
    outs = (shaped(32, HIDDEN // 4, dtype=f32), shaped(32, 256, dtype=f32), shaped(4, 192, dtype=f32))
    return call(finish_rows_kernel, "finish_rows", [S, S, V], outs, [], MB, 2 * MB, 16)(camera_ids, view, got)


def home_route():
    size = dict(zip(AXES, SIZES))
    place = lambda at: sum(at[a] * s for a, s in zip(AXES, (64, 32, 8, 4, 2, 1)))
    route = []
    for spot in every(*[range(size[a]) for a in AXES]):
        at = dict(zip(AXES, spot))
        p = at["x"] * 2 + at["zh"]
        to = dict(x=at["yh"] * 2 + at["c"], zh=at["zl"], zl=at["yl"], yl=p >> 2, yh=p >> 1 & 1, c=p & 1)
        route.append((place(at), place(to)))
    return route


def on_device(
    tokens, patches, patch_counts, camera_ids, modulation, query_weight, key_weight, value_weight, output_weight,
    cross_query, cross_key, cross_value, cross_output, expand_weight, reduce_weight, cotangent,
):
    scale = HEAD**-0.5
    item = lax.axis_index(ITEMS)
    head = lax.axis_index(ITEM)
    view = lax.axis_index(VIEW)
    counts = lax.dynamic_index_in_dim(patch_counts, item, 0, keepdims=False)
    gather = lambda block: lax.all_gather(block, GATHER, axis=0, tiled=False).reshape((4, 4) + block.shape)

    x = tokens[0, 0]
    grad_out = cotangent[0, 0]
    patches_all = gather(patches[0, 0])

    live = (jnp.arange(4)[:, None] * SLOTS < counts[None, :]).reshape(BLOCKS)
    n_live = jnp.sum(live.astype(jnp.int32))
    rank = jnp.where(live, jnp.cumsum(live) - 1, n_live + jnp.cumsum(~live) - 1)
    slot = jnp.arange(BLOCKS)
    order = jnp.sum(jnp.where(rank[None, :] == slot[:, None], slot[None, :], 0), 1).astype(jnp.int32)
    n_live = n_live.reshape(1)
    own_columns = lambda w: lax.dynamic_slice_in_dim(w, head * HEAD, HEAD, 1)
    kv_weight = jnp.concatenate([own_columns(cross_key), own_columns(cross_value)], 1)
    weights_t = jnp.concatenate([own_columns(w).T for w in (query_weight, key_weight, value_weight)], 0)

    after = lambda value, *others: lax.optimization_barrier((value,) + others)[0]
    sent, first_acts, gains = enter(item.reshape(1), camera_ids, x, grad_out, modulation, query_weight, key_weight, value_weight)
    qkv, kv_weight, weights_t, order, n_live = lax.optimization_barrier(
        (swap(sent, ITEM), kv_weight, weights_t, order, n_live)
    )
    o_t, keep_self = self_forward(qkv, scale)
    first_sum, acts, sent = middle(swap(o_t, ITEM), x, gains, first_acts, output_weight, cross_query)
    qc = swap(sent, ITEM)
    acts = gather(acts)
    kv = mm(kv_weight, patches_all.reshape(BLOCKS * SLOTS, -1), 0, 1).astype(bf16)
    oc_t, keep_cross = cross_forward(order, n_live, qc, kv, scale)
    layer_out, d_second, late_acts, sent, dgb3 = mlp(
        swap(oc_t, ITEM), first_sum, grad_out, gains, cross_output, expand_weight, reduce_weight
    )
    do_c = swap(sent, ITEM)
    late_acts = gather(late_acts)
    dqc, dkv = cross_backward(order, n_live, qc, do_c, keep_cross, kv, scale)
    d_first, sent, dgb2 = returned(swap(dqc, ITEM), first_sum, d_second, gains, cross_query, output_weight)
    do1, col_cross = lax.optimization_barrier((swap(sent, ITEM), cross_grads(dqc, acts, gains, output_weight, dkv, patches_all)))
    dkv_got = swap(after(dkv, do1), ITEM)
    dqkv = self_backward(qkv, do1, keep_self, scale)
    col_late, sent = late_grads(dqkv, acts, weights_t, gains, dgb2, dgb3)
    sent, dkv_got = lax.optimization_barrier((sent, dkv_got))
    columns, row = hidden_grads(
        head.reshape(1), acts, late_acts, after(do1, sent), oc_t, expand_weight, reduce_weight, col_late, col_cross
    )
    got, columns, row = lax.optimization_barrier((swap(sent, ITEM), columns, row))
    columns = swap(columns, ITEMS)
    tokens_grad, camera_sum = leave(got, x, d_first, gains, query_weight, key_weight, value_weight)
    patches_grad = patches_back(dkv_got, cross_key, cross_value)

    camera_sum = camera_sum.reshape(8, -1)[:, : 3 * HEAD]
    high = camera_sum.astype(bf16)
    low = (camera_sum - high.astype(f32)).astype(bf16)
    lines = jnp.concatenate([high.reshape(8, 3, HEAD), low.reshape(8, 3, HEAD)], 1)
    mine = jnp.arange(4) == lax.axis_index(("zl", "yl"))
    lines = jnp.where(mine[None, :, None, None], lines[:, None], 0).astype(bf16).reshape(32, 6, HEAD)
    row = row + jnp.pad(lines, ((0, 0), (0, 26), (UNITS + HEAD, 0)))

    columns, row = lax.optimization_barrier((columns, row))
    rows = swap(row, ROW)
    summed = lax.ppermute(add_items(columns), AXES, home_route())
    *turned, e_grad = finish_columns(summed)
    q_grad, k_grad, v_grad, cq_grad, ck_grad, cv_grad, o_grad = (grad.T for grad in turned)
    r_grad, co_grad, modulation_grad = finish_rows(camera_ids, view.reshape(1), rows)
    return (
        layer_out[None, None],
        tokens_grad[None, None],
        patches_grad[None, None],
        modulation_grad,
        q_grad,
        k_grad,
        v_grad,
        o_grad,
        cq_grad,
        ck_grad,
        cv_grad,
        co_grad.T,
        e_grad,
        r_grad.T,
    )


def solution(mesh):
    fine = Mesh(mesh.devices.reshape(SIZES), AXES)
    split = P(ROW, VIEW, None, None)
    grads = P(VIEW, ROW)
    return jax.shard_map(
        on_device,
        mesh=fine,
        in_specs=(split, split) + (P(),) * 13 + (split,),
        out_specs=(split,) * 3 + (grads,) * 11,
        check_vma=False,
    )
```

```python
from functools import partial
from itertools import product as every

import jax
import jax.numpy as jnp
from jax import lax
from jax.experimental import pallas as pl
from jax.experimental.pallas import tpu as pltpu
from jax.sharding import Mesh
from jax.sharding import PartitionSpec as P

HEADS = 16
HEAD = 64
TOK = 128
SLOTS = 256
BLOCKS = 16
LIVE_MAX = 13
EPS = 1e-05
LOG2E = 1.4426950408889634
FAR = -1e30

AXES = ("yh", "c", "x", "zh", "zl", "yl")
SIZES = (2, 2, 4, 2, 2, 2)
VIEW = ("yh", "c")
ROW = ("x", "zh", "zl", "yl")
ITEM = ("yh", "c", "zl", "yl")
ITEMS = ("x", "zh")
GATHER = ("zl", "yl", "yh", "c")
VMEM_BYTES = 60 * 1024 * 1024

bf16 = jnp.bfloat16
f32 = jnp.float32


def mm(left, right, lc=1, rc=0):
    return lax.dot_general(left, right, (((lc,), (rc,)), ((), ())), preferred_element_type=f32)


def swap(block, axes):
    return lax.all_to_all(block, axes, 0, 0, tiled=True)


def three_parts(row):
    high = row.astype(bf16)
    rest = row - high.astype(f32)
    middle = rest.astype(bf16)
    low = (rest - middle.astype(f32)).astype(bf16)
    return high, middle, low


CHAINS, ROWS = 8, 2
BACK_CHAINS, BACK_ROWS = 8, 1
DEPTH = 3 * HEAD


def scaled(turned, factor):
    value = turned.astype(f32) * factor
    high = value.astype(bf16)
    low = value - high.astype(f32)
    return jnp.concatenate([high.astype(f32), low], 0)


def softmax_block(q, kt, v, o_ref, keep_ref, at):
    s = mm(q, kt)
    m = jnp.max(s, 1, keepdims=True)
    p = jnp.exp2(s - m)
    o = mm(p.astype(bf16), v)
    total = o[:, HEAD : HEAD + 1]
    o = o[:, :HEAD] / total
    lse = m + jnp.log2(total)
    packed = jnp.concatenate([o, jnp.broadcast_to(lse, o.shape)], 1).T
    for part in range(packed.shape[1] // TOK):
        piece = packed[:, part * TOK : (part + 1) * TOK]
        o_ref[at + part] = piece[:HEAD].astype(bf16)
        keep_ref[at + part] = piece[: HEAD + 8]


def backward_block(qts, dots, keeps, kt, k, vt, dk_acc, dv_acc, scale):
    q_rows, do_rows = [], []
    for qt, dot, keep in zip(qts, dots, keeps):
        lse = keep[HEAD : HEAD + 1]
        delta = jnp.sum(dot.astype(f32) * keep[:HEAD], 0, keepdims=True) * scale
        one = jnp.ones_like(lse)
        zero = jnp.zeros((HEAD - 4, TOK), f32)
        parts = [part.astype(f32) for part in three_parts(-lse)]
        q_rows.append(jnp.concatenate([scaled(qt, scale * LOG2E), one] + parts + [zero], 0))
        parts = [part.astype(f32) for part in three_parts(-delta)]
        do_rows.append(jnp.concatenate([dot.astype(f32) * scale] + parts + [0.0 * one, zero], 0))
    q = jnp.concatenate([rows.T for rows in q_rows], 0).astype(bf16)
    do = jnp.concatenate([rows.T for rows in do_rows], 0).astype(bf16)
    p = jnp.exp2(mm(q, kt))
    ds = (p * mm(do, vt)).astype(bf16)
    dq = mm(ds, k)
    dk_acc[...] += mm(jnp.concatenate(qts, 1), ds)
    dv_acc[...] += mm(jnp.concatenate(dots, 1), p.astype(bf16))
    return dq[:, :HEAD]


def store_blocks(ref, at, rows, value):
    turned = value.T
    for part in range(turned.shape[1] // TOK):
        ref[at + part, rows, :] = turned[:, part * TOK : (part + 1) * TOK].astype(ref.dtype)


def with_ones(rows):
    ones = jnp.where(lax.broadcasted_iota(jnp.int32, rows.shape, 1) == 0, 1.0, 0.0).astype(bf16)
    return jnp.concatenate([rows, ones], 1)


def self_forward_kernel(qkv_ref, o_ref, keep_ref, kt, v, *, scale):
    for j in range(BLOCKS):
        cols = slice(j * TOK, (j + 1) * TOK)
        kt[:HEAD, cols] = qkv_ref[j, HEAD : 2 * HEAD, :]
        kt[HEAD:, cols] = qkv_ref[j, HEAD : 2 * HEAD, :]
        v[cols, :] = with_ones(qkv_ref[j, 2 * HEAD :, :].T)

    def one(i, carry):
        for c in range(CHAINS):
            at = (i * CHAINS + c) * ROWS
            q = jnp.concatenate([scaled(qkv_ref[at + n, :HEAD, :], scale * LOG2E).T for n in range(ROWS)], 0).astype(bf16)
            softmax_block(q, kt[...], v[...], o_ref, keep_ref, at)
        return carry

    lax.fori_loop(0, BLOCKS // (ROWS * CHAINS), one, 0)


def self_backward_kernel(qkv_ref, do_ref, keep_ref, out_ref, kt, k, vt, dk_acc, dv_acc, *, scale):
    row = lax.broadcasted_iota(jnp.int32, (HEAD, BLOCKS * TOK), 0)
    kt[2 * HEAD :, :] = jnp.where((row >= 1) & (row < 4), 1.0, 0.0).astype(bf16)
    vt[HEAD:, :] = jnp.where(row < 3, 1.0, 0.0).astype(bf16)
    for j in range(BLOCKS):
        cols = slice(j * TOK, (j + 1) * TOK)
        kt[:HEAD, cols] = qkv_ref[j, HEAD : 2 * HEAD, :]
        kt[HEAD : 2 * HEAD, cols] = qkv_ref[j, HEAD : 2 * HEAD, :]
        k[cols, :] = kt[: 2 * HEAD, cols].T
        vt[:HEAD, cols] = qkv_ref[j, 2 * HEAD :, :]
    dk_acc[...] = jnp.zeros_like(dk_acc)
    dv_acc[...] = jnp.zeros_like(dv_acc)

    def one(i, carry):
        for c in range(BACK_CHAINS):
            at = (i * BACK_CHAINS + c) * BACK_ROWS
            qts = [qkv_ref[at + n, :HEAD, :] for n in range(BACK_ROWS)]
            dots = [do_ref[at + n, :HEAD, :] for n in range(BACK_ROWS)]
            keeps = [keep_ref[at + n] for n in range(BACK_ROWS)]
            dq = backward_block(qts, dots, keeps, kt[...], k[...], vt[...], dk_acc, dv_acc, scale)
            store_blocks(out_ref, at, slice(0, HEAD), dq)
        return carry

    lax.fori_loop(0, BLOCKS // (BACK_CHAINS * BACK_ROWS), one, 0)
    for j in range(BLOCKS):
        cols = slice(j * TOK, (j + 1) * TOK)
        out_ref[j, HEAD : 2 * HEAD, :] = dk_acc[:, cols].astype(bf16)
        out_ref[j, 2 * HEAD :, :] = dv_acc[:, cols].astype(bf16)


def slot_block(kv_ref, index):
    return kv_ref[:, pl.ds(pl.multiple_of(index * SLOTS, SLOTS), SLOTS)]


def own_place(index):
    return (index % 4) * 4 + index // 4


def cross_forward_kernel(order_ref, live_ref, q_ref, kv_ref, o_ref, keep_ref, kt, v, *, scale):
    for t in range(LIVE_MAX):
        cols = slice(t * SLOTS, (t + 1) * SLOTS)
        block = slot_block(kv_ref, order_ref[t])
        kt[:HEAD, cols] = block[:HEAD]
        kt[HEAD : 2 * HEAD, cols] = block[:HEAD]
        bias = jnp.where(t < live_ref[0], 0.0, FAR)
        row = lax.broadcasted_iota(jnp.int32, (HEAD, SLOTS), 0)
        kt[2 * HEAD :, cols] = jnp.where(row == 0, bias, 0.0).astype(bf16)
        v[cols, :] = with_ones(block[HEAD:].T)
    one_row = jnp.where(lax.broadcasted_iota(jnp.int32, (HEAD, TOK), 0) == 0, 1.0, 0.0)

    def one(i, carry):
        for c in range(CHAINS):
            at = (i * CHAINS + c) * ROWS
            q = jnp.concatenate(
                [jnp.concatenate([scaled(q_ref[at + n], scale * LOG2E), one_row], 0).T for n in range(ROWS)], 0
            ).astype(bf16)
            softmax_block(q, kt[...], v[...], o_ref, keep_ref, at)
        return carry

    lax.fori_loop(0, BLOCKS // (ROWS * CHAINS), one, 0)


def cross_backward_kernel(
    order_ref, live_ref, q_ref, do_ref, keep_ref, kv_ref, dq_ref, dkv_ref, kt, k, vt, dk_acc, dv_acc, *, scale
):
    shape = (HEAD, LIVE_MAX * SLOTS)
    row = lax.broadcasted_iota(jnp.int32, shape, 0)
    vt[HEAD:, :] = jnp.where(row < 3, 1.0, 0.0).astype(bf16)
    for t in range(LIVE_MAX):
        cols = slice(t * SLOTS, (t + 1) * SLOTS)
        block = slot_block(kv_ref, order_ref[t])
        kt[:HEAD, cols] = block[:HEAD]
        kt[HEAD : 2 * HEAD, cols] = block[:HEAD]
        bias = jnp.where(t < live_ref[0], 0.0, FAR)
        row = lax.broadcasted_iota(jnp.int32, (HEAD, SLOTS), 0)
        ones = jnp.where((row >= 1) & (row < 4), 1.0, 0.0)
        kt[2 * HEAD :, cols] = jnp.where(row == 0, bias, ones).astype(bf16)
        k[cols, :] = kt[: 2 * HEAD, cols].T
        vt[:HEAD, cols] = block[HEAD:]
    dk_acc[...] = jnp.zeros_like(dk_acc)
    dv_acc[...] = jnp.zeros_like(dv_acc)

    def one(i, carry):
        for c in range(BACK_CHAINS):
            at = (i * BACK_CHAINS + c) * BACK_ROWS
            qts = [q_ref[at + n] for n in range(BACK_ROWS)]
            dots = [do_ref[at + n] for n in range(BACK_ROWS)]
            keeps = [keep_ref[at + n] for n in range(BACK_ROWS)]
            dq = backward_block(qts, dots, keeps, kt[...], k[...], vt[...], dk_acc, dv_acc, scale)
            store_blocks(dq_ref, at, slice(0, HEAD), dq)
        return carry

    lax.fori_loop(0, BLOCKS // (BACK_CHAINS * BACK_ROWS), one, 0)
    for t in range(LIVE_MAX):
        cols = slice(t * SLOTS, (t + 1) * SLOTS)
        dkv_ref[own_place(order_ref[t]), :HEAD, :] = dk_acc[:, cols].astype(bf16)
        dkv_ref[own_place(order_ref[t]), HEAD:, :] = dv_acc[:, cols].astype(bf16)
    for t in range(LIVE_MAX, BLOCKS):
        dkv_ref[own_place(order_ref[t])] = jnp.zeros((2 * HEAD, SLOTS), bf16)


def params():
    return pltpu.CompilerParams(vmem_limit_bytes=40 << 20)


def vmem(count):
    return [pl.BlockSpec(memory_space=pltpu.VMEM)] * count


def smem(count):
    return [pl.BlockSpec(memory_space=pltpu.SMEM)] * count


def cost(keys, products):
    flops = 2 * BLOCKS * TOK * keys * HEAD * products
    return pl.CostEstimate(flops=4 * flops, bytes_accessed=4 << 20, transcendentals=BLOCKS * TOK * keys)


OUT_T = jax.ShapeDtypeStruct((BLOCKS, HEAD, TOK), bf16)
KEEP_T = jax.ShapeDtypeStruct((BLOCKS, HEAD + 8, TOK), f32)


def self_forward(qkv, scale):
    keys = BLOCKS * TOK
    return pl.pallas_call(
        partial(self_forward_kernel, scale=scale),
        out_shape=(OUT_T, KEEP_T),
        in_specs=vmem(1),
        out_specs=tuple(vmem(2)),
        scratch_shapes=[pltpu.VMEM((2 * HEAD, keys), bf16), pltpu.VMEM((keys, 2 * HEAD), bf16)],
        compiler_params=params(),
        cost_estimate=cost(keys, 2),
        name="self_forward",
    )(qkv)


def self_backward(qkv, do, keep, scale):
    keys = BLOCKS * TOK
    return pl.pallas_call(
        partial(self_backward_kernel, scale=scale),
        out_shape=jax.ShapeDtypeStruct((BLOCKS, 3 * HEAD, TOK), bf16),
        in_specs=vmem(3),
        out_specs=vmem(1)[0],
        scratch_shapes=[
            pltpu.VMEM((DEPTH, keys), bf16),
            pltpu.VMEM((keys, 2 * HEAD), bf16),
            pltpu.VMEM((2 * HEAD, keys), bf16),
            pltpu.VMEM((HEAD, keys), f32),
            pltpu.VMEM((HEAD, keys), f32),
        ],
        compiler_params=params(),
        cost_estimate=cost(keys, 5),
        name="self_backward",
    )(qkv, do, keep)


def cross_forward(order, live, q, kv, scale):
    keys = LIVE_MAX * SLOTS
    return pl.pallas_call(
        partial(cross_forward_kernel, scale=scale),
        out_shape=(OUT_T, KEEP_T),
        in_specs=smem(2) + vmem(2),
        out_specs=tuple(vmem(2)),
        scratch_shapes=[pltpu.VMEM((DEPTH, keys), bf16), pltpu.VMEM((keys, 2 * HEAD), bf16)],
        compiler_params=params(),
        cost_estimate=cost(keys, 2),
        name="cross_forward",
    )(order, live, q, kv)


def cross_backward(order, live, q, do, keep, kv, scale):
    keys = LIVE_MAX * SLOTS
    return pl.pallas_call(
        partial(cross_backward_kernel, scale=scale),
        out_shape=(OUT_T, jax.ShapeDtypeStruct((BLOCKS, 2 * HEAD, SLOTS), bf16)),
        in_specs=smem(2) + vmem(4),
        out_specs=tuple(vmem(2)),
        scratch_shapes=[
            pltpu.VMEM((DEPTH, keys), bf16),
            pltpu.VMEM((keys, 2 * HEAD), bf16),
            pltpu.VMEM((2 * HEAD, keys), bf16),
            pltpu.VMEM((HEAD, keys), f32),
            pltpu.VMEM((HEAD, keys), f32),
        ],
        compiler_params=params(),
        cost_estimate=cost(keys, 5),
        name="cross_backward",
    )(order, live, q, do, keep, kv)


def normed(v):
    centred = v - jnp.mean(v, -1, keepdims=True)
    spread = jnp.mean(centred * centred, -1, keepdims=True)
    r = lax.rsqrt(spread + EPS)
    return centred * r, r


def norm_backward(da, xh, r, gain):
    d = da * (1.0 + gain)
    along = jnp.mean(d * xh, -1, keepdims=True)
    return r * (d - jnp.mean(d, -1, keepdims=True) - xh * along)


def token_rows(ref, lo, hi):
    block = ref[:, lo:hi, :]
    return block.reshape(HEADS * (hi - lo), block.shape[2]).T


def store_heads(ref, lo, value):
    turned = value.T.astype(bf16)
    ref[:, lo : lo + HEAD, :] = turned.reshape(HEADS, HEAD, turned.shape[1])


def load_all(pairs, sems):
    copies = [pltpu.make_async_copy(src, dst, sems.at[n]) for n, (src, dst) in enumerate(pairs)]
    for copy in copies:
        copy.start()
    return copies


def enter_kernel(item_ref, camera_ref, x_ref, cot_ref, mod_ref, wq_any, wk_any, wv_any, sent_ref, acts_ref, gains_ref, wq, wk, wv, sems):
    copies = load_all(((wq_any, wq), (wk_any, wk), (wv_any, wv)), sems)
    row = mod_ref[pl.ds(camera_ref[item_ref[0]], 1), :]
    for n in range(6):
        gains_ref[n : n + 1, :] = row[:, n * WIDTH : (n + 1) * WIDTH]
    gains_ref[6:8, :] = jnp.zeros((2, WIDTH), f32)
    xh, _ = normed(x_ref[...].astype(f32))
    acts_ref[0] = cot_ref[...]
    acts_ref[1] = x_ref[...]
    a1 = (xh * (1.0 + gains_ref[0:1, :]) + gains_ref[1:2, :]).astype(bf16)
    for n, (copy, w) in enumerate(zip(copies, (wq, wk, wv))):
        copy.wait()
        store_heads(sent_ref, n * HEAD, mm(a1, w[...]))


def middle_kernel(o_ref, x_ref, gains_ref, early_ref, wo_any, wcq_any, first_ref, acts_ref, q_ref, wo, wcq, sems):
    copies = load_all(((wo_any, wo), (wcq_any, wcq)), sems)
    o1 = token_rows(o_ref, 0, HEAD)
    acts_ref[0:2] = early_ref[...]
    acts_ref[2] = o1
    copies[0].wait()
    first = x_ref[...].astype(f32) + mm(o1, wo[...])
    first_ref[...] = first
    xh, _ = normed(first)
    a2 = (xh * (1.0 + gains_ref[2:3, :]) + gains_ref[3:4, :]).astype(bf16)
    copies[1].wait()
    store_heads(q_ref, 0, mm(a2, wcq[...]))


def gelu_both(a3, cot, we, wr):
    u = mm(a3, we)
    square = u * u
    t = jnp.tanh(u * (GELU_A + GELU_A * GELU_B * square))
    h = (0.5 * u * (1.0 + t)).astype(bf16)
    dh = mm(cot, wr, 1, 1).astype(bf16).astype(f32)
    slope = 0.5 * (1.0 + t) + 0.5 * u * (1.0 - t * t) * (GELU_A + 3.0 * GELU_A * GELU_B * square)
    return h, (dh * slope).astype(bf16)


def mlp_kernel(
    oc_ref, first_ref, cot_ref, gains_ref, wco_ref, we_ref, wr_ref,
    out_ref, back_ref, acts_ref, do_ref, dgb_ref, a3, second, y, da3,
):
    step = pl.program_id(0)

    @pl.when(step == 0)
    def _():
        total = first_ref[...] + mm(token_rows(oc_ref, 0, HEAD), wco_ref[...])
        second[...] = total
        xh, _ = normed(total)
        a3[...] = (xh * (1.0 + gains_ref[4:5, :]) + gains_ref[5:6, :]).astype(bf16)
        y[...] = jnp.zeros_like(y)
        da3[...] = jnp.zeros_like(da3)

    h, du = gelu_both(a3[...], cot_ref[...], we_ref[...], wr_ref[...])
    y[...] += mm(h, wr_ref[...])
    da3[...] += mm(du, we_ref[...], 1, 1)

    @pl.when(step == pl.num_programs(0) - 1)
    def _():
        total = second[...]
        out_ref[...] = total + y[...]
        xh, r = normed(total)
        d = da3[...]
        dgb_ref[...] = jnp.zeros_like(dgb_ref)
        dgb_ref[0:1, :] = jnp.sum(d * xh, 0, keepdims=True)
        dgb_ref[1:2, :] = jnp.sum(d, 0, keepdims=True)
        back = cot_ref[...].astype(f32) + norm_backward(d, xh, r, gains_ref[4:5, :])
        back_ref[...] = back
        dy2 = back.astype(bf16)
        acts_ref[0] = a3[...]
        acts_ref[1] = dy2
        store_heads(do_ref, 0, mm(dy2, wco_ref[...], 1, 1))


def return_kernel(dq_ref, first_ref, second_back_ref, gains_ref, wcq_any, wo_any, back_ref, sent_ref, dgb_ref, wcq, wo, sems):
    copies = load_all(((wcq_any, wcq), (wo_any, wo)), sems)
    xh, r = normed(first_ref[...])
    dq = token_rows(dq_ref, 0, HEAD)
    copies[0].wait()
    da2 = mm(dq, wcq[...], 1, 1)
    dgb_ref[...] = jnp.zeros_like(dgb_ref)
    dgb_ref[0:1, :] = jnp.sum(da2 * xh, 0, keepdims=True)
    dgb_ref[1:2, :] = jnp.sum(da2, 0, keepdims=True)
    back = second_back_ref[...] + norm_backward(da2, xh, r, gains_ref[2:3, :])
    back_ref[...] = back
    dy1 = back.astype(bf16)
    store_heads(sent_ref, HEAD, back)
    copies[1].wait()
    store_heads(sent_ref, 0, mm(dy1, wo[...], 1, 1))


def leave_kernel(got_ref, x_ref, back_ref, gains_ref, wq_any, wk_any, wv_any, out_ref, camera_ref, wq, wk, wv, sems):
    copies = load_all(((wq_any, wq), (wk_any, wk), (wv_any, wv)), sems)
    lines = got_ref[0, 3 * HEAD :, :].astype(f32)
    for n in range(1, BLOCKS):
        lines += got_ref[n, 3 * HEAD :, :].astype(f32)
    camera_ref[...] = lines[:16] + lines[16:]
    xh, r = normed(x_ref[...].astype(f32))
    da1 = jnp.zeros(out_ref.shape, f32)
    for n, (copy, w) in enumerate(zip(copies, (wq, wk, wv))):
        copy.wait()
        da1 += mm(token_rows(got_ref, n * HEAD, (n + 1) * HEAD), w[...], 1, 1)
    out_ref[...] = back_ref[...] + norm_backward(da1, xh, r, gains_ref[0:1, :])


def patches_kernel(got_ref, wk_ref, wv_ref, out_ref):
    dk = token_rows(got_ref, 0, HEAD)
    dv = token_rows(got_ref, HEAD, 2 * HEAD)
    out_ref[...] = mm(dk, wk_ref[...], 1, 1) + mm(dv, wv_ref[...], 1, 1)


def side_by_side(ref, lo, hi):
    return jnp.concatenate([ref[n, lo:hi, :] for n in range(ref.shape[0])], 1)


def one_above_other(ref):
    block = ref[...]
    return block.reshape(-1, block.shape[-1])


def store_columns(ref, at, grad_t):
    columns, rows = grad_t.shape[0] // 2, grad_t.shape[1] // 4
    for e in range(2):
        for v in range(4):
            piece = grad_t[e * columns : (e + 1) * columns, v * rows : (v + 1) * rows]
            if rows < 256:
                piece = jnp.concatenate([piece, jnp.zeros((columns, 256 - rows), f32)], 1)
            ref[e * 4 + v, at : at + columns, :] = piece.astype(bf16)


def add_up(step, accs, terms):
    @pl.when(step == 0)
    def _():
        for acc, term in zip(accs, terms):
            acc[...] = term

    @pl.when(step > 0)
    def _():
        for acc, term in zip(accs, terms):
            acc[...] += term


def cross_grads_kernel(dqc_ref, x_ref, o1_ref, gains_ref, wo_ref, dkv_ref, patches_ref, col_ref, q_acc, kv_acc):
    step = pl.program_id(0)
    first = one_above_other(x_ref).astype(f32) + mm(one_above_other(o1_ref), wo_ref[...])
    a2 = (normed(first)[0] * (1.0 + gains_ref[2:3, :]) + gains_ref[3:4, :]).astype(bf16)
    q = mm(side_by_side(dqc_ref, 0, HEAD), a2)
    kv = mm(side_by_side(dkv_ref, 0, 2 * HEAD), one_above_other(patches_ref))
    add_up(step, (q_acc, kv_acc), (q, kv))

    @pl.when(step == pl.num_programs(0) - 1)
    def _():
        store_columns(col_ref, 0, q_acc[...])
        store_columns(col_ref, 32, kv_acc[:HEAD, :])
        store_columns(col_ref, 64, kv_acc[HEAD:, :])


def hidden_grads_kernel(
    head_ref, cot_ref, o1_ref, a3_ref, dy2_ref, do_ref, oc_ref, we_ref, wr_ref, late_ref, cross_ref,
    col_ref, row_ref, e_acc, r_acc, o_acc, oc_acc,
):
    step = pl.program_id(0)
    a3, cot = one_above_other(a3_ref), one_above_other(cot_ref)
    h, du = gelu_both(a3, cot, we_ref[...], wr_ref[...])
    e = mm(du.T, a3)
    r = mm(h.T, cot)
    o = mm(side_by_side(do_ref, HEAD, 2 * HEAD), one_above_other(o1_ref))
    oc = mm(side_by_side(oc_ref, 0, HEAD), one_above_other(dy2_ref))
    add_up(step, (e_acc, r_acc, o_acc, oc_acc), (e, r, o, oc))

    @pl.when(step == pl.num_programs(0) - 1)
    def _():
        col_ref[:, :96, :] = late_ref[...]
        col_ref[:, 96:192, :] = cross_ref[...]
        store_columns(col_ref, 192, o_acc[...])
        store_columns(col_ref, 224, e_acc[...])
        rows = jnp.concatenate([r_acc[...], oc_acc[...], jnp.zeros((HEAD, WIDTH), f32)], 0)
        row_ref[...] = rows.T.astype(bf16).reshape(row_ref.shape)


def late_kernel(dqkv_ref, x_ref, wt_ref, gains_ref, dgb2_ref, dgb3_ref, col_ref, sent_ref, qkv_acc, sums):
    step = pl.program_id(0)
    turned = side_by_side(dqkv_ref, 0, 3 * HEAD)
    xh = normed(one_above_other(x_ref).astype(f32))[0].astype(bf16)
    qkv = mm(turned, xh)
    total = jnp.broadcast_to(jnp.sum(turned.astype(f32), 1, keepdims=True), sums.shape)
    add_up(step, (qkv_acc, sums), (qkv, total))
    blocks = dqkv_ref.shape[0]
    for n in range(blocks):
        sent_ref[step * blocks + n, : 3 * HEAD, :] = dqkv_ref[n]

    @pl.when(step == pl.num_programs(0) - 1)
    def _():
        moment = qkv_acc[...]
        count = sums[:, 0:1]
        weights = wt_ref[...].astype(f32)
        grad = moment * (1.0 + gains_ref[0:1, :]) + count * gains_ref[1:2, :]
        for n in range(3):
            store_columns(col_ref, n * 32, grad[n * HEAD : (n + 1) * HEAD])
        dg1 = jnp.sum(weights * moment, 0, keepdims=True)
        db1 = jnp.sum(weights * count, 0, keepdims=True)
        flat = jnp.concatenate([dg1, db1] + [ref[n : n + 1, :] for ref in (dgb2_ref, dgb3_ref) for n in range(2)], 1)
        chunk = flat.shape[1] // 32
        fill = jnp.zeros((1, 2 * TOK - chunk), f32)
        for b in range(4):
            lines = []
            for i in range(8):
                at = (i * 4 + b) * chunk
                line = jnp.concatenate([flat[:, at : at + chunk], fill], 1)
                lines += [line[:, :TOK], line[:, TOK:]]
            lines = jnp.concatenate(lines, 0)
            high = lines.astype(bf16)
            both = jnp.concatenate([high, (lines - high.astype(f32)).astype(bf16)], 0)
            for v in range(4):
                sent_ref[v * 4 + b, 3 * HEAD :, :] = both


def add_items_kernel(got_ref, out_ref):
    total = got_ref[0].astype(f32)
    for n in range(1, 8):
        total += got_ref[n].astype(f32)
    out_ref[...] = total.astype(bf16)


def finish_columns_kernel(in_ref, *out_refs):
    at = 0
    for ref in out_refs[:-1]:
        columns, rows = ref.shape
        ref[...] = in_ref[at : at + columns, :rows].astype(f32)
        at += columns
    out_refs[-1][...] = in_ref[at:, :].astype(f32).T


def finish_rows_kernel(camera_ref, view_ref, got_ref, r_ref, oc_ref, modulation_ref):
    units = r_ref.shape[1] // 4
    for s in range(4):
        total = got_ref[s].astype(f32)
        for n in range(1, 8):
            total += got_ref[n * 4 + s].astype(f32)
        r_ref[:, s * units : (s + 1) * units] = total[:, :units]
        oc_ref[:, s * HEAD : (s + 1) * HEAD] = total[:, units : units + HEAD]
    rows = [jnp.zeros((16, HEAD), f32) for _ in range(4)]
    for n in range(8):
        part = sum(got_ref[n * 4 + s, 0:16, units + HEAD : units + 2 * HEAD].astype(f32) for s in range(4))
        for k in range(4):
            rows[k] += jnp.where(camera_ref[n] == view_ref[0] * 4 + k, part, 0.0)
    for k in range(4):
        for n in range(3):
            modulation_ref[k : k + 1, n * HEAD : (n + 1) * HEAD] = rows[k][n : n + 1] + rows[k][n + 3 : n + 4]


WIDTH = 1024
HIDDEN = 4096
PATCH = 768
UNITS = HIDDEN // BLOCKS
GELU_A = 0.7978845608028654
GELU_B = 0.044715


def shaped(*shape, dtype=bf16):
    return jax.ShapeDtypeStruct(shape, dtype)


ANY = pl.BlockSpec(memory_space=pl.ANY)
V = pl.BlockSpec(memory_space=pltpu.VMEM)
S = pl.BlockSpec(memory_space=pltpu.SMEM)
MB = 1 << 20


def weight(rows=WIDTH, columns=WIDTH):
    return pltpu.VMEM((rows, columns), bf16)


def call(kernel, name, ins, outs, scratch, flops, traffic, limit=60):
    return pl.pallas_call(
        kernel,
        out_shape=outs,
        in_specs=ins,
        out_specs=jax.tree.map(lambda _: V, outs),
        scratch_shapes=scratch,
        compiler_params=pltpu.CompilerParams(vmem_limit_bytes=limit * MB),
        cost_estimate=pl.CostEstimate(flops=flops, bytes_accessed=traffic, transcendentals=0),
        name=name,
    )


TOKENS_F32 = shaped(TOK, WIDTH, dtype=f32)
TOKENS_BF16 = shaped(TOK, WIDTH)
ROWS_F32 = shaped(8, WIDTH, dtype=f32)
SQUARE = 2 * TOK * WIDTH * WIDTH


def enter(*args):
    return call(
        enter_kernel, "enter", [S, S, V, V, V, ANY, ANY, ANY],
        (shaped(BLOCKS, 3 * HEAD, TOK), shaped(2, TOK, WIDTH), ROWS_F32),
        [weight(), weight(), weight(), pltpu.SemaphoreType.DMA((3,))], 3 * SQUARE, 8 * MB,
    )(*args)


def middle(*args):
    return call(
        middle_kernel, "middle", [V, V, V, V, ANY, ANY], (TOKENS_F32, shaped(3, TOK, WIDTH), OUT_T),
        [weight(), weight(), pltpu.SemaphoreType.DMA((2,))], 2 * SQUARE, 6 * MB, 24,
    )(*args)


def mlp(*args):
    steps = 4
    width = HIDDEN // steps
    whole = lambda *shape: pl.BlockSpec(shape, lambda i: (0,) * len(shape))
    outs = (TOKENS_F32, TOKENS_F32, shaped(2, TOK, WIDTH), OUT_T, ROWS_F32)
    out_specs = tuple(whole(*o.shape) for o in outs)
    tokens = whole(TOK, WIDTH)
    return pl.pallas_call(
        mlp_kernel,
        grid=(steps,),
        out_shape=outs,
        in_specs=[
            whole(BLOCKS, HEAD, TOK), tokens, tokens, whole(8, WIDTH), whole(WIDTH, WIDTH),
            pl.BlockSpec((WIDTH, width), lambda i: (0, i)), pl.BlockSpec((width, WIDTH), lambda i: (i, 0)),
        ],
        out_specs=out_specs,
        scratch_shapes=[
            pltpu.VMEM((TOK, WIDTH), bf16), pltpu.VMEM((TOK, WIDTH), f32),
            pltpu.VMEM((TOK, WIDTH), f32), pltpu.VMEM((TOK, WIDTH), f32),
        ],
        compiler_params=pltpu.CompilerParams(vmem_limit_bytes=46 << 20),
        cost_estimate=pl.CostEstimate(flops=18 * SQUARE, bytes_accessed=22 * MB, transcendentals=TOK * HIDDEN),
        name="mlp",
    )(*args)


def returned(*args):
    return call(
        return_kernel, "returned", [V, V, V, V, ANY, ANY], (TOKENS_F32, shaped(BLOCKS, 2 * HEAD, TOK), ROWS_F32),
        [weight(), weight(), pltpu.SemaphoreType.DMA((2,))], 2 * SQUARE, 6 * MB, 24,
    )(*args)


def leave(*args):
    return call(
        leave_kernel, "leave", [V, V, V, V, ANY, ANY, ANY], (TOKENS_F32, shaped(16, TOK, dtype=f32)),
        [weight(), weight(), weight(), pltpu.SemaphoreType.DMA((3,))], 3 * SQUARE, 8 * MB, 24)(*args)


def patches_back(*args):
    return call(
        patches_kernel, "patches_back", [V, V, V], shaped(SLOTS, PATCH, dtype=f32), [], 3 * SQUARE, 5 * MB, 24)(*args)


STEPS = 4


def blocks_of(*shape):
    return pl.BlockSpec((BLOCKS // STEPS,) + shape, lambda i: (i,) + (0,) * len(shape))


def gathered(*shape, at=None):
    plane = () if at is None else (at,)
    return pl.BlockSpec((4, 1) + (1,) * len(plane) + shape, lambda i: (0, i) + plane + (0,) * len(shape))


def whole_block(*shape):
    return pl.BlockSpec(shape, lambda i: (0,) * len(shape))


def cross_grads(dqc, acts, gains, output_weight, dkv, patches_all):
    out = shaped(8, 96, 256)
    return pl.pallas_call(
        cross_grads_kernel,
        grid=(STEPS,),
        out_shape=out,
        in_specs=[
            blocks_of(HEAD, TOK), gathered(TOK, WIDTH, at=1), gathered(TOK, WIDTH, at=2), whole_block(8, WIDTH),
            whole_block(WIDTH, WIDTH), blocks_of(2 * HEAD, SLOTS), gathered(SLOTS, PATCH),
        ],
        out_specs=whole_block(*out.shape),
        scratch_shapes=[pltpu.VMEM((HEAD, WIDTH), f32), pltpu.VMEM((2 * HEAD, PATCH), f32)],
        compiler_params=pltpu.CompilerParams(vmem_limit_bytes=VMEM_BYTES),
        cost_estimate=pl.CostEstimate(flops=22 * SQUARE, bytes_accessed=18 * MB, transcendentals=0),
        name="cross_grads",
    )(dqc, acts, acts, gains, output_weight, dkv, patches_all)


def hidden_grads(head, acts, late_acts, do1, oc_t, expand_weight, reduce_weight, col_late, col_cross):
    outs = (shaped(8, 352, 256), shaped(32, 32, UNITS + 2 * HEAD))
    by_head = lambda spec: pl.BlockSpec(spec.block_shape, lambda i, head: spec.index_map(i))
    ins = [
        gathered(TOK, WIDTH, at=0), gathered(TOK, WIDTH, at=2), gathered(TOK, WIDTH, at=0),
        gathered(TOK, WIDTH, at=1), blocks_of(2 * HEAD, TOK), blocks_of(HEAD, TOK),
    ]
    own = [
        pl.BlockSpec((WIDTH, UNITS), lambda i, head: (0, head[0])),
        pl.BlockSpec((UNITS, WIDTH), lambda i, head: (head[0], 0)),
        by_head(whole_block(8, 96, 256)), by_head(whole_block(8, 96, 256)),
    ]
    return pl.pallas_call(
        hidden_grads_kernel,
        grid_spec=pltpu.PrefetchScalarGridSpec(
            num_scalar_prefetch=1,
            grid=(STEPS,),
            in_specs=[by_head(spec) for spec in ins] + own,
            out_specs=tuple(by_head(whole_block(*o.shape)) for o in outs),
            scratch_shapes=[
                pltpu.VMEM((UNITS, WIDTH), f32), pltpu.VMEM((UNITS, WIDTH), f32),
                pltpu.VMEM((HEAD, WIDTH), f32), pltpu.VMEM((HEAD, WIDTH), f32),
            ],
        ),
        out_shape=outs,
        compiler_params=pltpu.CompilerParams(vmem_limit_bytes=VMEM_BYTES),
        cost_estimate=pl.CostEstimate(flops=20 * SQUARE, bytes_accessed=20 * MB, transcendentals=0),
        name="hidden_grads",
    )(head, acts, acts, late_acts, late_acts, do1, oc_t, expand_weight, reduce_weight, col_late, col_cross)


def late_grads(dqkv, acts, weights_t, gains, dgb2, dgb3):
    outs = (shaped(8, 96, 256), shaped(BLOCKS, 3 * HEAD + 32, TOK))
    return pl.pallas_call(
        late_kernel,
        grid=(STEPS,),
        out_shape=outs,
        in_specs=[blocks_of(3 * HEAD, TOK), gathered(TOK, WIDTH, at=1), whole_block(3 * HEAD, WIDTH)]
        + [whole_block(8, WIDTH)] * 3,
        out_specs=tuple(whole_block(*o.shape) for o in outs),
        scratch_shapes=[pltpu.VMEM((3 * HEAD, WIDTH), f32), pltpu.VMEM((3 * HEAD, TOK), f32)],
        compiler_params=pltpu.CompilerParams(vmem_limit_bytes=VMEM_BYTES),
        cost_estimate=pl.CostEstimate(flops=4 * SQUARE, bytes_accessed=6 * MB, transcendentals=0),
        name="late_grads",
    )(dqkv, acts, weights_t, gains, dgb2, dgb3)


def add_items(got):
    return call(add_items_kernel, "add_items", [V], shaped(*got.shape[1:]), [], MB, 2 * MB, 16)(got)


def finish_columns(summed):
    small = [(32, 256)] * 4 + [(32, 192)] * 2 + [(32, 256), (256, 128)]
    outs = tuple(shaped(*shape, dtype=f32) for shape in small)
    return call(finish_columns_kernel, "finish_columns", [V], outs, [], MB, MB, 16)(summed)


def finish_rows(camera_ids, view, got):
    outs = (shaped(32, HIDDEN // 4, dtype=f32), shaped(32, 256, dtype=f32), shaped(4, 192, dtype=f32))
    return call(finish_rows_kernel, "finish_rows", [S, S, V], outs, [], MB, 2 * MB, 16)(camera_ids, view, got)


def home_route():
    size = dict(zip(AXES, SIZES))
    place = lambda at: sum(at[a] * s for a, s in zip(AXES, (64, 32, 8, 4, 2, 1)))
    route = []
    for spot in every(*[range(size[a]) for a in AXES]):
        at = dict(zip(AXES, spot))
        p = at["x"] * 2 + at["zh"]
        to = dict(x=at["yh"] * 2 + at["c"], zh=at["zl"], zl=at["yl"], yl=p >> 2, yh=p >> 1 & 1, c=p & 1)
        route.append((place(at), place(to)))
    return route


def on_device(
    tokens, patches, patch_counts, camera_ids, modulation, query_weight, key_weight, value_weight, output_weight,
    cross_query, cross_key, cross_value, cross_output, expand_weight, reduce_weight, cotangent,
):
    scale = HEAD**-0.5
    item = lax.axis_index(ITEMS)
    head = lax.axis_index(ITEM)
    view = lax.axis_index(VIEW)
    counts = lax.dynamic_index_in_dim(patch_counts, item, 0, keepdims=False)
    gather = lambda block: lax.all_gather(block, GATHER, axis=0, tiled=False).reshape((4, 4) + block.shape)

    x = tokens[0, 0]
    grad_out = cotangent[0, 0]
    patches_all = gather(patches[0, 0])

    live = (jnp.arange(4)[:, None] * SLOTS < counts[None, :]).reshape(BLOCKS)
    n_live = jnp.sum(live.astype(jnp.int32))
    rank = jnp.where(live, jnp.cumsum(live) - 1, n_live + jnp.cumsum(~live) - 1)
    slot = jnp.arange(BLOCKS)
    order = jnp.sum(jnp.where(rank[None, :] == slot[:, None], slot[None, :], 0), 1).astype(jnp.int32)
    n_live = n_live.reshape(1)
    own_columns = lambda w: lax.dynamic_slice_in_dim(w, head * HEAD, HEAD, 1)
    kv_weight = jnp.concatenate([own_columns(cross_key), own_columns(cross_value)], 1)
    weights_t = jnp.concatenate([own_columns(w).T for w in (query_weight, key_weight, value_weight)], 0)

    after = lambda value, *others: lax.optimization_barrier((value,) + others)[0]
    sent, first_acts, gains = enter(item.reshape(1), camera_ids, x, grad_out, modulation, query_weight, key_weight, value_weight)
    qkv, kv_weight, weights_t, order, n_live = lax.optimization_barrier(
        (swap(sent, ITEM), kv_weight, weights_t, order, n_live)
    )
    o_t, keep_self = self_forward(qkv, scale)
    first_sum, acts, sent = middle(swap(o_t, ITEM), x, gains, first_acts, output_weight, cross_query)
    qc = swap(sent, ITEM)
    acts = gather(acts)
    kv = mm(kv_weight, patches_all.reshape(BLOCKS * SLOTS, -1), 0, 1).astype(bf16)
    oc_t, keep_cross = cross_forward(order, n_live, qc, kv, scale)
    layer_out, d_second, late_acts, sent, dgb3 = mlp(
        swap(oc_t, ITEM), first_sum, grad_out, gains, cross_output, expand_weight, reduce_weight
    )
    do_c = swap(sent, ITEM)
    late_acts = gather(late_acts)
    dqc, dkv = cross_backward(order, n_live, qc, do_c, keep_cross, kv, scale)
    d_first, sent, dgb2 = returned(swap(dqc, ITEM), first_sum, d_second, gains, cross_query, output_weight)
    do1, col_cross = lax.optimization_barrier((swap(sent, ITEM), cross_grads(dqc, acts, gains, output_weight, dkv, patches_all)))
    dkv_got = swap(after(dkv, do1), ITEM)
    dqkv = self_backward(qkv, do1, keep_self, scale)
    col_late, sent = late_grads(dqkv, acts, weights_t, gains, dgb2, dgb3)
    sent, dkv_got = lax.optimization_barrier((sent, dkv_got))
    columns, row = hidden_grads(
        head.reshape(1), acts, late_acts, after(do1, sent), oc_t, expand_weight, reduce_weight, col_late, col_cross
    )
    got, columns, row = lax.optimization_barrier((swap(sent, ITEM), columns, row))
    columns = swap(columns, ITEMS)
    tokens_grad, camera_sum = leave(got, x, d_first, gains, query_weight, key_weight, value_weight)
    patches_grad = patches_back(dkv_got, cross_key, cross_value)

    camera_sum = camera_sum.reshape(8, -1)[:, : 3 * HEAD]
    high = camera_sum.astype(bf16)
    low = (camera_sum - high.astype(f32)).astype(bf16)
    lines = jnp.concatenate([high.reshape(8, 3, HEAD), low.reshape(8, 3, HEAD)], 1)
    mine = jnp.arange(4) == lax.axis_index(("zl", "yl"))
    lines = jnp.where(mine[None, :, None, None], lines[:, None], 0).astype(bf16).reshape(32, 6, HEAD)
    row = row + jnp.pad(lines, ((0, 0), (0, 26), (UNITS + HEAD, 0)))

    columns, row = lax.optimization_barrier((columns, row))
    rows = swap(row, ROW)
    summed = lax.ppermute(add_items(columns), AXES, home_route())
    *turned, e_grad = finish_columns(summed)
    q_grad, k_grad, v_grad, cq_grad, ck_grad, cv_grad, o_grad = (grad.T for grad in turned)
    r_grad, co_grad, modulation_grad = finish_rows(camera_ids, view.reshape(1), rows)
    return (
        layer_out[None, None],
        tokens_grad[None, None],
        patches_grad[None, None],
        modulation_grad,
        q_grad,
        k_grad,
        v_grad,
        o_grad,
        cq_grad,
        ck_grad,
        cv_grad,
        co_grad.T,
        e_grad,
        r_grad.T,
    )


def solution(mesh):
    fine = Mesh(mesh.devices.reshape(SIZES), AXES)
    split = P(ROW, VIEW, None, None)
    grads = P(VIEW, ROW)
    return jax.shard_map(
        on_device,
        mesh=fine,
        in_specs=(split, split) + (P(),) * 13 + (split,),
        out_specs=(split,) * 3 + (grads,) * 11,
        check_vma=False,
    )
```
